32 devices in a mesh: group: 4 (over x, core), mp: 8 (over z, y).
Axes of the slice: x: 2, y: 2, z: 4, core: 2. Of those that a mesh axis runs over, the one named last changes fastest.
Arguments:
- arrivals: bfloat16 [4096, 2048], P(('group', 'mp')), may hold values from -6 to 6
- slots: int32 [4096], P(('group', 'mp')), may hold values from 0 to 1023, as said below
- lengths: int32 [4, 3], P('group'), may hold values from 1 to 768, 1024 in all within a row
- w_joined: float32 [2048, 1536], P('mp', 'group')
- w_expand: float32 [512, 2048], P('mp', 'group'), may hold values from -0.25 to 0.25
Outputs:
- attended: bfloat16 [4096, 1024], P(('group', 'mp'))
The draws below stay inside these ranges and needn't reach their ends.
Inputs may be any that keep to these rules, and one draw needn't show every extreme that they name: `slots`: within each group the entries form a permutation of 0 to 1023; the 128 entries of one device hold exactly 8 values of every aligned run of 64 values.
All inputs are finite; a program needn't handle non-finite values.
Results may differ from the reference program's by a relative error of at most 0.03.
The reference program's roundings to bfloat16 on the way (of `served`, `normed`, `query`, `latent`, `keyval`, `probs` and `outcome`) count: a program that leaves them out, or rounds other values in their place, can miss the bound.
Values may be sent and summed in bfloat16 or wider, within the bound.
No kernel may reach another device: no remote copies, remote signals or barrier semaphores. Data moves between devices by JAX's collectives and lax.ppermute only.
A program may use at most 64 MiB of HBM per device.

```python
import math
import jax
import jax.numpy as jnp
import numpy as np
from jax import lax

D = 2048
HEADS = 8
HDIM = 128
RANK = 512
TOK_DEV = 128
QCOLS = 1024
JOINED = 1536
TOKG = 1024
TOKENS = 4096
COUNT = 3
N_GROUP = 4
N_MP = 8


def draw_slots(key, part):
    group_tokens = TOK_DEV * N_MP
    half_rows = TOK_DEV // 2
    per_block = half_rows // N_MP
    block_count = 2 * N_MP

    def one_group(group_key):
        block_key = jax.random.fold_in(group_key, 1)
        shuffle_key = jax.random.fold_in(group_key, 2)
        block_perms = jax.vmap(lambda one_key: jax.random.permutation(one_key, half_rows))(jax.random.split(block_key, block_count))
        block_perms = block_perms.astype(jnp.int32) + (jnp.arange(block_count, dtype=jnp.int32) * half_rows)[:, None]
        grouped = jnp.transpose(block_perms.reshape(block_count, N_MP, per_block), (1, 0, 2)).reshape(N_MP, TOK_DEV)
        shuffles = jax.vmap(lambda one_key: jax.random.permutation(one_key, TOK_DEV))(jax.random.split(shuffle_key, N_MP))
        return jnp.take_along_axis(grouped, shuffles.astype(jnp.int32), axis=1).reshape(group_tokens)
    group_keys = jax.random.split(jax.random.fold_in(key, 11), N_GROUP)
    return jax.vmap(one_group)(group_keys).reshape(N_GROUP * group_tokens).astype(jnp.int32)


def draw_w_joined(key, part):
    values = jax.random.normal(jax.random.fold_in(key, 3), (D, JOINED), jnp.float32) * D ** (-0.5)
    return values


def steps_of(key, shape, cuts, least, largest):
    factor_of, own = 1.0, jax.random.fold_in(key, 6)
    for dim, parts in cuts:
        steps = jnp.exp(jax.random.uniform(jax.random.fold_in(own, dim), (parts,), jnp.float32, least / len(cuts), largest / len(cuts)))
        factor_of = factor_of * jnp.repeat(steps, shape[dim] // parts).reshape([-1 if axis == dim else 1 for axis in range(len(shape))])
    return factor_of


def split_up(count, total, limit, skew):
    portions = [(1 << 20) // math.isqrt(grade ** skew) + 1 for grade in range(2, count + 1)]
    surplus, counts = total - limit - (count - 1), [1] * (count - 1)
    while surplus > 0:
        free = [i for i in range(count - 1) if counts[i] < limit]
        whole, remaining = sum([portions[i] for i in free]), surplus
        for i in free:
            more = min(limit - counts[i], max(1, remaining * portions[i] // whole), surplus)
            counts[i] = counts[i] + more
            surplus = surplus - more
    return np.array([limit] + counts)


def ragged(own_key, count, total, reach, slope):
    if count == 2:
        one = jax.random.randint(own_key, (), max(1, total - reach), min(reach, total - 1) + 1)
        return jnp.stack([one, total - one])
    sizes = jnp.asarray(split_up(count, total, reach, slope), jnp.int32)
    twos = (count - 1) // 2
    giver, sink = sizes[1:1 + 2 * twos:2], sizes[2:2 + 2 * twos:2]
    margin = jnp.minimum(giver - 1, reach - sink)
    moved = jax.random.randint(jax.random.fold_in(own_key, 1), (twos,), 0, 1 << 20) % (margin + 1)
    sizes = sizes.at[1:1 + 2 * twos:2].set(giver - moved).at[2:2 + 2 * twos:2].set(sink + moved)
    return sizes[jax.random.permutation(jax.random.fold_in(own_key, 2), count)]


def normal_values(rng, extent, deviation, reach, cuts=(), kind=jnp.bfloat16):
    loudness = steps_of(rng, extent, cuts, -0.22, 0.18) if cuts else 1.0
    values = jax.random.normal(rng, extent, jnp.float32) * deviation * loudness
    return jnp.minimum(jnp.maximum(values, -reach), reach).astype(kind)


def setup_inputs(seed: int = 0) -> dict:
    streams_of = jax.random.split(jax.random.key(seed), 6)
    return {
        "arrivals": normal_values(streams_of[0], (TOKENS, D), 1.0, 6.0, ((0, 32),)),
        "slots": draw_slots(jax.random.fold_in(streams_of[5], 71), 0),
        "lengths": jax.vmap(lambda own: ragged(own, COUNT, TOKG, 3 * TOKG // 4, 2))(jax.random.split(streams_of[2], N_GROUP)).reshape((N_GROUP, COUNT)).astype(jnp.int32),
        "w_joined": draw_w_joined(jax.random.fold_in(streams_of[5], 71), 0),
        "w_expand": normal_values(streams_of[4], (RANK, 2 * QCOLS), RANK ** -0.5, 0.25, ((0, 8), (1, 4)), jnp.float32),
    }


EPS = 1e-06
NEGATIVE = -1e+30

def row_norm(values):
    mean_sq = lax.optimization_barrier(jnp.mean(values * values, axis=-1, keepdims=True))
    return values * lax.rsqrt(mean_sq + EPS)

def reference(arrivals, slots, lengths, w_joined, w_expand):
    qcols = HEADS * HDIM
    joined_half = w_joined.astype(jnp.bfloat16)
    expand_half = w_expand.astype(jnp.bfloat16)
    group_rows = arrivals.reshape(N_GROUP, TOKG, D)
    group_slots = slots.reshape(N_GROUP, TOKG)
    block_rows = min(512, TOKG)
    window = min(TOKG, block_rows + 3 * TOKG // 4)

    def one_group(inputs):
        rows_in, slots_in, lengths_in = inputs
        served = jnp.zeros_like(rows_in).at[slots_in].set(rows_in)
        normed = row_norm(served.astype(jnp.float32)).astype(jnp.bfloat16)
        proj = jnp.dot(normed, joined_half, preferred_element_type=jnp.float32)
        query = (proj[:, :qcols] * HDIM ** (-0.5)).astype(jnp.bfloat16)
        latent = row_norm(proj[:, qcols:]).astype(jnp.bfloat16)
        keyval = jnp.dot(latent, expand_half, preferred_element_type=jnp.float32).astype(jnp.bfloat16)
        keyval = lax.optimization_barrier(keyval).reshape(TOKG, HEADS, 2 * HDIM)
        ends = jnp.cumsum(lengths_in).astype(jnp.int32)
        positions = jnp.arange(TOKG, dtype=jnp.int32)
        segment = lax.optimization_barrier(jnp.sum((positions[:, None] >= ends[None, :]).astype(jnp.int32), axis=1)).astype(jnp.int32)

        def one_block(block_index):
            first_row = (block_index * block_rows).astype(jnp.int32)
            key_first = jnp.clip(first_row + block_rows - window, 0, TOKG - window).astype(jnp.int32)
            queries = lax.dynamic_slice_in_dim(query, first_row, block_rows, 0)
            queries = queries.reshape(block_rows, HEADS, HDIM).astype(jnp.float32)
            key_rows = lax.dynamic_slice_in_dim(keyval, key_first, window, 0).astype(jnp.float32)
            scores = jnp.einsum('qhd,khd->hqk', queries, key_rows[:, :, :HDIM])
            query_pos = first_row + jnp.arange(block_rows, dtype=jnp.int32)
            key_pos = key_first + jnp.arange(window, dtype=jnp.int32)
            query_seg = lax.dynamic_slice_in_dim(segment, first_row, block_rows, 0)
            key_seg = lax.dynamic_slice_in_dim(segment, key_first, window, 0)
            allowed = (key_pos[None, :] <= query_pos[:, None]) & (key_seg[None, :] == query_seg[:, None])
            masked = jnp.where(allowed[None], scores, NEGATIVE)
            peak = lax.optimization_barrier(jnp.max(masked, axis=-1, keepdims=True))
            weights = jnp.where(allowed[None], jnp.exp(masked - peak), 0.0)
            total = lax.optimization_barrier(jnp.sum(weights, axis=-1))
            probs = lax.optimization_barrier(weights.astype(jnp.bfloat16)).astype(jnp.float32)
            summed = jnp.einsum('hqk,khd->qhd', probs, key_rows[:, :, HDIM:])
            return (summed / jnp.transpose(total)[:, :, None]).reshape(block_rows, qcols)
        outcome = lax.map(one_block, jnp.arange(TOKG // block_rows, dtype=jnp.int32))
        outcome = outcome.reshape(TOKG, qcols).astype(jnp.bfloat16)
        return outcome[slots_in]
    result = lax.map(one_group, (group_rows, group_slots, lengths))
    return result.reshape(TOKENS, qcols)
```

```python
import functools

import jax
import jax.numpy as jnp
from jax import lax
from jax.experimental import pallas as pl
from jax.experimental.pallas import tpu as pltpu
from jax.sharding import PartitionSpec as P

HEADS = 8
HDIM = 128
QCOLS = HEADS * HDIM

EPS = 1e-06
NEGATIVE = -1e30
VMEM = pl.BlockSpec(memory_space=pltpu.VMEM)
SMEM = pl.BlockSpec(memory_space=pltpu.SMEM)
PARAMS = pltpu.CompilerParams(vmem_limit_bytes=56 * 1024 * 1024)


def row_norm(values):
    mean_sq = jnp.mean(values * values, axis=-1, keepdims=True)
    return values * lax.rsqrt(mean_sq + EPS)


def ring_to_mp(place, count):
    return jnp.where(place < count // 2, 2 * place, 2 * (count - 1 - place) + 1)


def ring_perm(count, step):
    order = [2 * r if r < count // 2 else 2 * (count - 1 - r) + 1 for r in range(count)]
    return [(order[r], order[(r + step) % count]) for r in range(count)]


def ring_gather(block, count):
    up, down = ring_perm(count, 1), ring_perm(count, -1)
    from_below, from_above = block, block
    blocks = [block]
    for _ in range((count - 1) // 2):
        from_below = lax.ppermute(from_below, "mp", up)
        from_above = lax.ppermute(from_above, "mp", down)
        blocks += [from_below, from_above]
    half = block.shape[0] // 2
    first = lax.ppermute(from_below[:half], "mp", up)
    second = lax.ppermute(from_above[half:], "mp", down)
    return blocks, (first, second)


def ring_owners(count):
    me = lax.axis_index("mp")
    place = jnp.where(me % 2 == 0, me // 2, count - 1 - me // 2)
    shifts = [0]
    for step in range(1, (count - 1) // 2 + 1):
        shifts += [-step, step]
    shifts.append(count // 2)
    return ring_to_mp((place + jnp.array(shifts, jnp.int32) + count) % count, count).astype(jnp.int32)


def group_gather(block, size):
    blocks = {0: block}
    bit = size // 2
    while bit:
        pairs = [(i, i ^ bit) for i in range(size)]
        for k in list(blocks):
            blocks[k ^ bit] = lax.ppermute(blocks[k], "group", pairs)
        bit //= 2
    return [blocks[k] for k in range(size)]


def place_rows(owners, blocks, halves, target):
    rows = blocks[0].shape[0]
    for i, block in enumerate(blocks):
        target[pl.ds(pl.multiple_of(owners[i] * rows, rows), rows), :] = block[...]
    last, half = owners[len(blocks)] * rows, rows // 2
    for i, block in enumerate(halves):
        target[pl.ds(pl.multiple_of(last + i * half, half), half), :] = block[...]


def proj_kernel(count, size, owners, column, *refs):
    tokens, refs = refs[:size], refs[size:]
    blocks, refs = refs[: count - 1], refs[count - 1 :]
    halves, refs = refs[:2], refs[2:]
    outs, weight = refs[:size], refs[size]
    place_rows(owners, blocks, halves, weight)
    columns = weight.shape[1]
    at = column[0] + lax.broadcasted_iota(jnp.int32, (1, columns), 1)
    scale = jnp.where(at < QCOLS, HDIM**-0.5, 1.0).astype(jnp.float32)
    for token, out in zip(tokens, outs):
        proj = jnp.dot(token[...], weight[...], preferred_element_type=jnp.float32)
        out[...] = (proj * scale).astype(jnp.bfloat16)


def attend_kernel(count, size, owners, parts, lengths, slots, own_slots, query, *refs):
    blocks, refs = refs[: count - 1], refs[count - 1 :]
    halves, refs = refs[:2], refs[2:]
    expands, refs = refs[:size], refs[size:]
    out, latent, expand = refs
    place_rows(owners, blocks, halves, latent)
    width = expands[0].shape[1]
    for i, block in enumerate(expands):
        expand[:, pl.ds(pl.multiple_of(parts[i] * width, width), width)] = block[...]
    position = own_slots[...]
    start = jnp.zeros_like(position)
    end = 0
    for i in range(lengths.shape[1]):
        end = end + lengths[0, i]
        start = jnp.where(position >= end, end, start)
    others = slots[...]
    allowed = (others <= position) & (others >= start)
    for head in range(HEADS):
        keyval = jnp.dot(
            latent[...], expand[:, head * 2 * HDIM : (head + 1) * 2 * HDIM], preferred_element_type=jnp.float32
        ).astype(jnp.bfloat16)
        columns = slice(head * HDIM, (head + 1) * HDIM)
        scores = lax.dot_general(
            query[:, columns], keyval[:, :HDIM], (((1,), (1,)), ((), ())), preferred_element_type=jnp.float32
        )
        scores = jnp.where(allowed, scores, NEGATIVE)
        peak = jnp.max(scores, axis=-1, keepdims=True)
        weights = jnp.exp(scores - peak)
        total = jnp.sum(weights, axis=-1, keepdims=True)
        summed = jnp.dot(weights.astype(jnp.bfloat16), keyval[:, HDIM:], preferred_element_type=jnp.float32)
        out[:, columns] = (summed / total).astype(jnp.bfloat16)


def body(arrivals, slots, lengths, w_joined, w_expand):
    count, size = lax.axis_size("mp"), lax.axis_size("group")
    group = lax.axis_index("group")
    rows = arrivals.shape[0]
    depth, columns = arrivals.shape[1], w_joined.shape[1]
    rank, joined = w_expand.shape[0] * count, columns * size
    owners = ring_owners(count)
    parts = group ^ jnp.arange(size, dtype=jnp.int32)

    all_slots = lax.all_gather(slots, "mp", axis=0, tiled=True).reshape(1, count * rows)
    blocks, halves = ring_gather(w_joined.astype(jnp.bfloat16), count)
    normed = row_norm(arrivals.astype(jnp.float32)).astype(jnp.bfloat16)
    tokens = group_gather(normed, size)
    projs = pl.pallas_call(
        functools.partial(proj_kernel, count, size),
        out_shape=[jax.ShapeDtypeStruct((rows, columns), jnp.bfloat16)] * size,
        in_specs=[SMEM, SMEM] + [VMEM] * (size + count + 1),
        out_specs=[VMEM] * size,
        scratch_shapes=[pltpu.VMEM((depth, columns), jnp.bfloat16)],
        compiler_params=PARAMS,
        cost_estimate=pl.CostEstimate(
            flops=2 * size * rows * depth * columns, bytes_accessed=4 * depth * columns, transcendentals=0
        ),
        name="project",
    )(owners, (group * columns).reshape(1), *tokens, *blocks, *halves)

    expand_half = w_expand.astype(jnp.bfloat16)
    expand_half, _ = lax.optimization_barrier((expand_half, halves[0]))
    ex_blocks, ex_halves = ring_gather(expand_half, count)
    expand_rows = jnp.stack(ex_blocks + [jnp.concatenate(ex_halves, axis=0)])
    own_expand = jnp.zeros_like(expand_rows).at[owners].set(expand_rows, unique_indices=True)
    own_expand = own_expand.reshape(rank, w_expand.shape[1])

    back = [projs[0]]
    for k in range(1, size):
        back.append(lax.ppermute(projs[k], "group", [(i, i ^ k) for i in range(size)]))
    own_expand, _ = lax.optimization_barrier((own_expand, back[-1]))
    expands = group_gather(own_expand, size)
    proj = jnp.stack(back)[parts]
    proj = jnp.transpose(proj, (1, 0, 2)).reshape(rows, joined)
    query = proj[:, :QCOLS]
    latent = row_norm(proj[:, QCOLS:].astype(jnp.float32)).astype(jnp.bfloat16)
    lat_blocks, lat_halves = ring_gather(latent, count)

    total = count * rows
    return pl.pallas_call(
        functools.partial(attend_kernel, count, size),
        out_shape=jax.ShapeDtypeStruct((rows, QCOLS), jnp.bfloat16),
        in_specs=[SMEM, SMEM, SMEM] + [VMEM] * (3 + count + 1 + size),
        out_specs=VMEM,
        scratch_shapes=[pltpu.VMEM((total, rank), jnp.bfloat16), pltpu.VMEM((rank, 2 * QCOLS), jnp.bfloat16)],
        compiler_params=PARAMS,
        cost_estimate=pl.CostEstimate(
            flops=4 * total * rank * QCOLS + 4 * rows * total * QCOLS,
            bytes_accessed=2 * (total + 2 * QCOLS) * rank,
            transcendentals=HEADS * rows * total,
        ),
        name="attend",
    )(owners, parts, lengths, all_slots, slots.reshape(rows, 1), query, *lat_blocks, *lat_halves, *expands)


def solution(mesh):
    in_specs = (
        P(("group", "mp"), None),
        P(("group", "mp")),
        P("group", None),
        P("mp", "group"),
        P("mp", "group"),
    )
    out_specs = P(("group", "mp"), None)
    return jax.shard_map(body, mesh=mesh, in_specs=in_specs, out_specs=out_specs, check_vma=False)
```

```python
import functools

import jax
import jax.numpy as jnp
from jax import lax
from jax.experimental import pallas as pl
from jax.experimental.pallas import tpu as pltpu
from jax.sharding import PartitionSpec as P

HEADS = 8
HDIM = 128
QCOLS = HEADS * HDIM

EPS = 1e-06
NEGATIVE = -1e30
VMEM = pl.BlockSpec(memory_space=pltpu.VMEM)
SMEM = pl.BlockSpec(memory_space=pltpu.SMEM)
PARAMS = pltpu.CompilerParams(vmem_limit_bytes=56 * 1024 * 1024)


def row_norm(values):
    mean_sq = jnp.mean(values * values, axis=-1, keepdims=True)
    return values * lax.rsqrt(mean_sq + EPS)


def ring_to_mp(place, count):
    return jnp.where(place < count // 2, 2 * place, 2 * (count - 1 - place) + 1)


def ring_perm(count, step):
    order = [2 * r if r < count // 2 else 2 * (count - 1 - r) + 1 for r in range(count)]
    return [(order[r], order[(r + step) % count]) for r in range(count)]


def doubling_step(values, count, bit):
    other = lax.ppermute(values, "mp", [(i, i ^ bit) for i in range(count)])
    mine_last = (lax.axis_index("mp") & bit) != 0
    return jnp.concatenate([jnp.where(mine_last, other, values), jnp.where(mine_last, values, other)])


def ring_gather(first, second, count, slots=None):
    up, down = ring_perm(count, 1), ring_perm(count, -1)
    steps = (count - 1) // 2
    states = [(first, first), (second, second)]
    outs = [[first], [second]]
    for step in range(steps):
        behind = states[1]
        if slots is not None and 1 << step < count:
            states[0], slots = lax.optimization_barrier((states[0], slots))
            slots = doubling_step(slots, count, 1 << step)
        for i in range(2):
            (from_below, from_above), _ = lax.optimization_barrier((states[i], behind))
            states[i] = (lax.ppermute(from_below, "mp", up), lax.ppermute(from_above, "mp", down))
            outs[i] += states[i]
            behind = (from_below, from_above)
    if slots is not None:
        states[0], slots = lax.optimization_barrier((states[0], slots))
    outs[0].append(lax.ppermute(states[0][0], "mp", up))
    outs[1].append(lax.ppermute(states[1][1], "mp", down))
    return outs if slots is None else (*outs, slots)


def ring_owners(count):
    me = lax.axis_index("mp")
    place = jnp.where(me % 2 == 0, me // 2, count - 1 - me // 2)
    shifts = [0]
    for step in range(1, (count - 1) // 2 + 1):
        shifts += [-step, step]
    shifts.append(count // 2)
    return ring_to_mp((place + jnp.array(shifts, jnp.int32) + count) % count, count).astype(jnp.int32)


def group_gather(block, size, after=None):
    blocks = {0: block}
    bit = size // 2
    while bit:
        pairs = [(i, i ^ bit) for i in range(size)]
        for k in list(blocks):
            sent = blocks[k]
            if k and after is not None:
                sent, _ = lax.optimization_barrier((sent, after))
            blocks[k ^ bit] = lax.ppermute(sent, "group", pairs)
        bit //= 2
    return [blocks[k] for k in range(size)]


def place_rows(owners, chunks, target):
    rows = 2 * chunks[0].shape[0]
    for i, chunk in enumerate(chunks):
        at = owners[i % (len(chunks) // 2)] * rows + (i >= len(chunks) // 2) * (rows // 2)
        target[pl.ds(pl.multiple_of(at, rows // 2), rows // 2), :] = chunk[:, : target.shape[1]]


def proj_kernel(count, size, owners, column, *refs):
    tokens, refs = refs[:size], refs[size:]
    chunks, refs = refs[: 2 * count], refs[2 * count :]
    outs, expand, token, weight = refs[:size], refs[size], refs[size + 1], refs[size + 2]
    place_rows(owners, chunks, weight)
    rows, columns = outs[0].shape
    for i, block in enumerate(tokens):
        token[i * rows : (i + 1) * rows, :] = block[...]
    at = column[0] + lax.broadcasted_iota(jnp.int32, (1, columns), 1)
    scale = jnp.where(at < QCOLS, HDIM**-0.5, 1.0).astype(jnp.float32)
    proj = jnp.dot(token[...], weight[...], preferred_element_type=jnp.float32) * scale
    for i, out in enumerate(outs):
        out[...] = proj[i * rows : (i + 1) * rows].astype(jnp.bfloat16)
    high = expand.shape[0] // count
    for i in range(count):
        parts = []
        for chunk in (chunks[i], chunks[count + i]):
            parts += [chunk[j * high : (j + 1) * high, columns:] for j in range(chunk.shape[0] // high)]
        expand[pl.ds(pl.multiple_of(owners[i] * high, high), high), :] = jnp.concatenate(parts, axis=1)


def attend_kernel(count, size, owners, parts, lengths, slots, own_slots, query, *refs):
    chunks, refs = refs[: 2 * count], refs[2 * count :]
    expands, refs = refs[:size], refs[size:]
    out, latent, expand = refs
    place_rows(owners, chunks, latent)
    width = expands[0].shape[1]
    for i, block in enumerate(expands):
        expand[:, pl.ds(pl.multiple_of(parts[i] * width, width), width)] = block[...]
    position = own_slots[...]
    start = jnp.zeros_like(position)
    end = 0
    for i in range(lengths.shape[1]):
        end = end + lengths[0, i]
        start = jnp.where(position >= end, end, start)
    others = slots[...]
    allowed = (others <= position) & (others >= start)
    for head in range(HEADS):
        keyval = jnp.dot(
            latent[...], expand[:, head * 2 * HDIM : (head + 1) * 2 * HDIM], preferred_element_type=jnp.float32
        ).astype(jnp.bfloat16)
        columns = slice(head * HDIM, (head + 1) * HDIM)
        scores = lax.dot_general(
            query[:, columns], keyval[:, :HDIM], (((1,), (1,)), ((), ())), preferred_element_type=jnp.float32
        )
        scores = jnp.where(allowed, scores, NEGATIVE)
        peak = jnp.max(scores, axis=-1, keepdims=True)
        weights = jnp.exp(scores - peak)
        total = jnp.sum(weights, axis=-1, keepdims=True)
        summed = jnp.dot(weights.astype(jnp.bfloat16), keyval[:, HDIM:], preferred_element_type=jnp.float32)
        out[:, columns] = (summed / total).astype(jnp.bfloat16)


def body(arrivals, slots, lengths, w_joined, w_expand):
    count, size = lax.axis_size("mp"), lax.axis_size("group")
    group = lax.axis_index("group")
    rows = arrivals.shape[0]
    depth, columns = arrivals.shape[1], w_joined.shape[1]
    rank, joined = w_expand.shape[0] * count, columns * size
    owners = ring_owners(count)
    parts = group ^ jnp.arange(size, dtype=jnp.int32)

    high, folds = w_expand.shape[0], w_joined.shape[0] // w_expand.shape[0]
    fold = w_expand.shape[1] // folds
    folded = jnp.concatenate([w_expand[:, i * fold : (i + 1) * fold] for i in range(folds)], axis=0)
    weights = jnp.concatenate([w_joined, folded], axis=1).astype(jnp.bfloat16)
    half = weights.shape[0] // 2
    first, second, all_slots = ring_gather(weights[:half], weights[half:], count, slots)
    all_slots = all_slots.reshape(1, count * rows)
    arrivals, _ = lax.optimization_barrier((arrivals, weights))
    normed = row_norm(arrivals.astype(jnp.float32)).astype(jnp.bfloat16)
    tokens = group_gather(normed, size)
    *projs, own_expand = pl.pallas_call(
        functools.partial(proj_kernel, count, size),
        out_shape=[jax.ShapeDtypeStruct((rows, columns), jnp.bfloat16)] * size
        + [jax.ShapeDtypeStruct((rank, w_expand.shape[1]), jnp.bfloat16)],
        in_specs=[SMEM, SMEM] + [VMEM] * (size + 2 * count),
        out_specs=[VMEM] * (size + 1),
        scratch_shapes=[
            pltpu.VMEM((size * rows, depth), jnp.bfloat16),
            pltpu.VMEM((depth, columns), jnp.bfloat16),
        ],
        compiler_params=PARAMS,
        cost_estimate=pl.CostEstimate(
            flops=2 * size * rows * depth * columns, bytes_accessed=4 * depth * columns, transcendentals=0
        ),
        name="project",
    )(owners, (group * columns).reshape(1), *tokens, *first, *second)

    back = [projs[0]]
    for k in range(1, size):
        back.append(lax.ppermute(projs[k], "group", [(i, i ^ k) for i in range(size)]))
    proj = jnp.stack(back)[parts]
    proj = jnp.transpose(proj, (1, 0, 2)).reshape(rows, joined)
    query = proj[:, :QCOLS]
    latent = row_norm(proj[:, QCOLS:].astype(jnp.float32)).astype(jnp.bfloat16)
    half = rows // 2
    lat_first, lat_second = ring_gather(latent[:half], latent[half:], count)
    own_expand, _ = lax.optimization_barrier((own_expand, latent))
    expands = group_gather(own_expand, size, (lat_first[-3:-1], lat_second[-3:-1]))

    total = count * rows
    return pl.pallas_call(
        functools.partial(attend_kernel, count, size),
        out_shape=jax.ShapeDtypeStruct((rows, QCOLS), jnp.bfloat16),
        in_specs=[SMEM, SMEM, SMEM] + [VMEM] * (3 + 2 * count + size),
        out_specs=VMEM,
        scratch_shapes=[pltpu.VMEM((total, rank), jnp.bfloat16), pltpu.VMEM((rank, 2 * QCOLS), jnp.bfloat16)],
        compiler_params=PARAMS,
        cost_estimate=pl.CostEstimate(
            flops=4 * total * rank * QCOLS + 4 * rows * total * QCOLS,
            bytes_accessed=2 * (total + 2 * QCOLS) * rank,
            transcendentals=HEADS * rows * total,
        ),
        name="attend",
    )(owners, parts, lengths, all_slots, slots.reshape(rows, 1), query, *lat_first, *lat_second, *expands)


def solution(mesh):
    in_specs = (
        P(("group", "mp"), None),
        P(("group", "mp")),
        P("group", None),
        P("mp", "group"),
        P("mp", "group"),
    )
    out_specs = P(("group", "mp"), None)
    return jax.shard_map(body, mesh=mesh, in_specs=in_specs, out_specs=out_specs, check_vma=False)
```

```python
import functools

import jax
import jax.numpy as jnp
from jax import lax
from jax.experimental import pallas as pl
from jax.experimental.pallas import tpu as pltpu
from jax.sharding import PartitionSpec as P

HEADS = 8
HDIM = 128
QCOLS = HEADS * HDIM

EPS = 1e-06
NEGATIVE = -1e30
LOG2_E = 1.4426950408889634
VMEM = pl.BlockSpec(memory_space=pltpu.VMEM)
SMEM = pl.BlockSpec(memory_space=pltpu.SMEM)
PARAMS = pltpu.CompilerParams(vmem_limit_bytes=56 * 1024 * 1024)


def row_norm(values):
    mean_sq = jnp.mean(values * values, axis=-1, keepdims=True)
    return values * lax.rsqrt(mean_sq + EPS)


def ring_to_mp(place, count):
    return jnp.where(place < count // 2, 2 * place, 2 * (count - 1 - place) + 1)


def ring_perm(count, step):
    order = [2 * r if r < count // 2 else 2 * (count - 1 - r) + 1 for r in range(count)]
    return [(order[r], order[(r + step) % count]) for r in range(count)]


def ring_gather(block, count):
    up, down = ring_perm(count, 1), ring_perm(count, -1)
    below = above = block
    blocks = [block]
    for _ in range((count - 1) // 2):
        below, above = lax.ppermute(below, "mp", up), lax.ppermute(above, "mp", down)
        blocks += [below, above]
    cut = -(-block.shape[0] // 32) * 16
    return blocks + [lax.ppermute(below[:cut], "mp", up), lax.ppermute(above[cut:], "mp", down)]


def ring_owners(count):
    me = lax.axis_index("mp")
    place = jnp.where(me % 2 == 0, me // 2, count - 1 - me // 2)
    shifts = [0]
    for step in range(1, (count - 1) // 2 + 1):
        shifts += [-step, step]
    shifts.append(count // 2)
    return ring_to_mp((place + jnp.array(shifts, jnp.int32) + count) % count, count).astype(jnp.int32)


def group_gather(block, size, after=None):
    blocks = {0: block}
    bit = size // 2
    while bit:
        pairs = [(i, i ^ bit) for i in range(size)]
        for k in list(blocks):
            sent = blocks[k]
            if k and after is not None:
                sent, _ = lax.optimization_barrier((sent, after))
            blocks[k ^ bit] = lax.ppermute(sent, "group", pairs)
        bit //= 2
    return [blocks[k] for k in range(size)]


def row_ranges(blocks):
    ranges = [(i, 0) for i in range(len(blocks) - 1)]
    return ranges + [(len(blocks) - 2, blocks[-2].shape[0])]


def proj_kernel(count, size, owners, column, *refs):
    tokens, refs = refs[:size], refs[size:]
    blocks, refs = refs[: count + 1], refs[count + 1 :]
    outs, expand = refs[:size], refs[size]
    depth, (rows, columns) = blocks[0].shape[0], outs[0].shape
    starts = [owners[i] * depth + offset for i, offset in row_ranges(blocks)]
    if blocks[-1].shape[0] % 128:
        weight = refs[size + 1]
        for start, block in zip(starts, blocks):
            length = block.shape[0]
            weight[pl.ds(pl.multiple_of(start, length), length), :] = block[:, :columns]
        products = [jnp.dot(token[...], weight[...], preferred_element_type=jnp.float32) for token in tokens]
        proj = jnp.concatenate(products, axis=0)
    else:
        proj = jnp.zeros((size * rows, columns), jnp.float32)
        for start, block in zip(starts, blocks):
            span = pl.ds(pl.multiple_of(start, 128), block.shape[0])
            left = jnp.concatenate([token[:, span] for token in tokens], axis=0)
            proj += jnp.dot(left, block[:, :columns], preferred_element_type=jnp.float32)
    at = column[0] + lax.broadcasted_iota(jnp.int32, (1, columns), 1)
    proj = proj * jnp.where(at < QCOLS, HDIM**-0.5, 1.0).astype(jnp.float32)
    for i, out in enumerate(outs):
        out[...] = proj[i * rows : (i + 1) * rows].astype(jnp.bfloat16)
    high = expand.shape[0] // count
    for i in range(count):
        parts = []
        for block in blocks[i:] if i == count - 1 else blocks[i : i + 1]:
            parts += [block[j * high : (j + 1) * high, columns:] for j in range(block.shape[0] // high)]
        expand[pl.ds(pl.multiple_of(owners[i] * high, high), high), :] = jnp.concatenate(parts, axis=1)


def attend_kernel(count, size, parts, lengths, own_slots, query, *refs):
    blocks, refs = refs[: count + 1], refs[count + 1 :]
    expands, refs = refs[:size], refs[size:]
    out, latent, expand, bias = refs
    rows, rank = query.shape[0], latent.shape[1]
    low, high = [], []
    for (i, offset), block in zip(row_ranges(blocks), blocks):
        length = min(rows - offset, block.shape[0])
        latent[i * rows + offset : i * rows + offset + length, :] = block[:length]
        if length < block.shape[0]:
            digits = block[length:].astype(jnp.float32)
            low.append(digits[:1, :rows])
            high.append(digits[1:2, :rows])
    others = jnp.concatenate(high, axis=1) * 256.0 + jnp.concatenate(low, axis=1)
    others = others.astype(jnp.int32)
    width = expands[0].shape[1]
    for i, block in enumerate(expands):
        expand[:, pl.ds(pl.multiple_of(parts[i] * width, width), width)] = block[...]
    position = own_slots[...]
    start = jnp.zeros_like(position)
    end = 0
    for i in range(lengths.shape[1]):
        end = end + lengths[0, i]
        start = jnp.where(position >= end, end, start)
    allowed = (others <= position) & (others >= start)
    bias[...] = jnp.where(allowed, 0.0, NEGATIVE)
    some = 4
    for first in range(0, HEADS, some):
        heads = range(first, first + some)
        turned = [
            lax.dot_general(
                query[:, head * HDIM : (head + 1) * HDIM],
                expand[:, head * 2 * HDIM : (2 * head + 1) * HDIM],
                (((1,), (1,)), ((), ())),
                preferred_element_type=jnp.float32,
            )
            for head in heads
        ]
        turned = (jnp.concatenate(turned, axis=0) * LOG2_E).astype(jnp.bfloat16)
        scores = lax.dot_general(
            turned, latent[...], (((1,), (1,)), ((), ())), preferred_element_type=jnp.float32
        )
        scores = scores.reshape(some, rows, count * rows) + bias[...][None]
        peak = jnp.max(scores, axis=-1, keepdims=True)
        weights = jnp.exp2(scores - peak)
        total = jnp.sum(weights, axis=-1, keepdims=True)
        probs = weights.astype(jnp.bfloat16).reshape(some * rows, count * rows)
        summed = jnp.dot(probs, latent[...], preferred_element_type=jnp.float32).astype(jnp.bfloat16)
        for i, head in enumerate(heads):
            value = expand[:, (2 * head + 1) * HDIM : (2 * head + 2) * HDIM]
            outcome = jnp.dot(summed[i * rows : (i + 1) * rows], value, preferred_element_type=jnp.float32)
            out[:, head * HDIM : (head + 1) * HDIM] = (outcome / total[i]).astype(jnp.bfloat16)


def body(arrivals, slots, lengths, w_joined, w_expand):
    count, size = lax.axis_size("mp"), lax.axis_size("group")
    group = lax.axis_index("group")
    rows = arrivals.shape[0]
    depth, columns = arrivals.shape[1], w_joined.shape[1]
    rank, joined = w_expand.shape[0] * count, columns * size
    owners = ring_owners(count)
    parts = group ^ jnp.arange(size, dtype=jnp.int32)

    high, folds = w_expand.shape[0], w_joined.shape[0] // w_expand.shape[0]
    fold = w_expand.shape[1] // folds
    folded = jnp.concatenate([w_expand[:, i * fold : (i + 1) * fold] for i in range(folds)], axis=0)
    weights = jnp.concatenate([w_joined, folded], axis=1).astype(jnp.bfloat16)
    blocks = ring_gather(weights, count)
    normed = row_norm(arrivals.astype(jnp.float32)).astype(jnp.bfloat16)
    normed, _ = lax.optimization_barrier((normed, blocks[1:3]))
    tokens = group_gather(normed, size)
    *projs, own_expand = pl.pallas_call(
        functools.partial(proj_kernel, count, size),
        out_shape=[jax.ShapeDtypeStruct((rows, columns), jnp.bfloat16)] * size
        + [jax.ShapeDtypeStruct((rank, w_expand.shape[1]), jnp.bfloat16)],
        in_specs=[SMEM, SMEM] + [VMEM] * (size + count + 1),
        out_specs=[VMEM] * (size + 1),
        scratch_shapes=[pltpu.VMEM((depth, columns), jnp.bfloat16)],
        compiler_params=PARAMS,
        cost_estimate=pl.CostEstimate(
            flops=2 * size * rows * depth * columns, bytes_accessed=4 * depth * columns, transcendentals=0
        ),
        name="project",
    )(owners, (group * columns).reshape(1), *tokens, *blocks)

    back = [projs[0]]
    for k in range(1, size):
        back.append(lax.ppermute(projs[k], "group", [(i, i ^ k) for i in range(size)]))
    proj = jnp.stack(back)[parts]
    proj = jnp.transpose(proj, (1, 0, 2)).reshape(rows, joined)
    query = proj[:, :QCOLS]
    latent = row_norm(proj[:, QCOLS:].astype(jnp.float32)).astype(jnp.bfloat16)
    digits = jnp.stack([slots & 255, slots >> 8]).astype(jnp.bfloat16)
    digits = jnp.pad(digits, ((0, 14), (0, rank - rows)))
    lat_blocks = ring_gather(jnp.concatenate([latent, digits], axis=0), count)
    own_expand, _ = lax.optimization_barrier((own_expand, latent))
    expands = group_gather(own_expand, size, lat_blocks[-4:-2])

    total = count * rows
    return pl.pallas_call(
        functools.partial(attend_kernel, count, size),
        out_shape=jax.ShapeDtypeStruct((rows, QCOLS), jnp.bfloat16),
        in_specs=[SMEM, SMEM] + [VMEM] * (2 + count + 1 + size),
        out_specs=VMEM,
        scratch_shapes=[
            pltpu.VMEM((total, rank), jnp.bfloat16),
            pltpu.VMEM((rank, 2 * QCOLS), jnp.bfloat16),
            pltpu.VMEM((rows, total), jnp.float32),
        ],
        compiler_params=PARAMS,
        cost_estimate=pl.CostEstimate(
            flops=4 * total * rank * QCOLS + 4 * rows * total * QCOLS,
            bytes_accessed=2 * (total + 2 * QCOLS) * rank,
            transcendentals=HEADS * rows * total,
        ),
        name="attend",
    )(parts, lengths, slots.reshape(rows, 1), query, *lat_blocks, *expands)


def solution(mesh):
    in_specs = (
        P(("group", "mp"), None),
        P(("group", "mp")),
        P("group", None),
        P("mp", "group"),
        P("mp", "group"),
    )
    out_specs = P(("group", "mp"), None)
    return jax.shard_map(body, mesh=mesh, in_specs=in_specs, out_specs=out_specs, check_vma=False)
```

```python
import functools

import jax
import jax.numpy as jnp
from jax import lax
from jax.experimental import pallas as pl
from jax.experimental.pallas import tpu as pltpu
from jax.sharding import PartitionSpec as P

HEADS = 8
HDIM = 128
QCOLS = HEADS * HDIM

EPS = 1e-06
NEGATIVE = -1e30
LOG2_E = 1.4426950408889634
VMEM = pl.BlockSpec(memory_space=pltpu.VMEM)
SMEM = pl.BlockSpec(memory_space=pltpu.SMEM)
PARAMS = pltpu.CompilerParams(vmem_limit_bytes=56 * 1024 * 1024)


def row_norm(values):
    mean_sq = jnp.mean(values * values, axis=-1, keepdims=True)
    return values * lax.rsqrt(mean_sq + EPS)


def ring_pairs(size, count, step):
    order = [2 * r if r < count // 2 else 2 * (count - 1 - r) + 1 for r in range(count)]
    pairs = []
    for group in range(size):
        for r in range(count):
            to = order[(r + (-step if group % 2 else step)) % count]
            pairs.append((group * count + order[r], group * count + to))
    return pairs


def ring_gather(block, size, count):
    up, down = ring_pairs(size, count, 1), ring_pairs(size, count, -1)
    below = above = block
    blocks = [block]
    for _ in range((count - 1) // 2):
        below, above = lax.ppermute(below, ("group", "mp"), up), lax.ppermute(above, ("group", "mp"), down)
        blocks += [below, above]
    return blocks + [lax.ppermute(below, ("group", "mp"), up)]


def ring_owners(count):
    me = lax.axis_index("mp")
    place = jnp.where(me % 2 == 0, me // 2, count - 1 - me // 2)
    turn = 1 - 2 * (lax.axis_index("group") % 2)
    owners = [me]
    for step in range(1, count // 2 + 1):
        for shift in (-step, step):
            at = lax.rem(place + turn * shift + count, count)
            owners.append(jnp.where(at < count // 2, 2 * at, 2 * (count - 1 - at) + 1))
    return owners[:count]


def group_gather(block, size, after=None):
    blocks = {0: block}
    bit = size // 2
    while bit:
        pairs = [(i, i ^ bit) for i in range(size)]
        for k in list(blocks):
            sent = blocks[k]
            if k and after is not None:
                sent, _ = lax.optimization_barrier((sent, after))
            blocks[k ^ bit] = lax.ppermute(sent, "group", pairs)
        bit //= 2
    return [blocks[k] for k in range(size)]


def pack_kernel(joined, expand, out):
    columns, high = joined.shape[1], expand.shape[0]
    folds = joined.shape[0] // high
    fold = expand.shape[1] // folds
    out[:, :columns] = joined[...].astype(jnp.bfloat16)
    for i in range(folds):
        out[i * high : (i + 1) * high, columns:] = expand[:, i * fold : (i + 1) * fold].astype(jnp.bfloat16)


def proj_kernel(count, size, *refs):
    tokens, refs = refs[:size], refs[size:]
    blocks, refs = refs[:count], refs[count:]
    outs, expand, weight = refs[:size], refs[size], refs[size + 1]
    depth, (rows, columns) = blocks[0].shape[0], outs[0].shape
    owners = ring_owners(count)
    if depth % 128:
        for owner, block in zip(owners, blocks):
            weight[pl.ds(pl.multiple_of(owner * depth, depth), depth), :] = block[:, :columns]
        products = [jnp.dot(token[...], weight[...], preferred_element_type=jnp.float32) for token in tokens]
        proj = jnp.concatenate(products, axis=0)
    else:
        proj = jnp.zeros((size * rows, columns), jnp.float32)
        for owner, block in zip(owners, blocks):
            span = pl.ds(pl.multiple_of(owner * depth, 128), depth)
            left = jnp.concatenate([token[:, span] for token in tokens], axis=0)
            proj += jnp.dot(left, block[:, :columns], preferred_element_type=jnp.float32)
    at = lax.axis_index("group") * columns + lax.broadcasted_iota(jnp.int32, (1, columns), 1)
    proj = proj * jnp.where(at < QCOLS, HDIM**-0.5, 1.0).astype(jnp.float32)
    for i, out in enumerate(outs):
        out[...] = proj[i * rows : (i + 1) * rows].astype(jnp.bfloat16)
    high = expand.shape[0] // count
    for owner, block in zip(owners, blocks):
        parts = [block[j * high : (j + 1) * high, columns:] for j in range(depth // high)]
        expand[pl.ds(pl.multiple_of(owner * high, high), high), :] = jnp.concatenate(parts, axis=1)


def assemble_kernel(size, slots, *refs):
    products, (query, block, proj) = refs[:size], refs[size:]
    rows, columns = products[0].shape
    group = lax.axis_index("group")
    for i, product in enumerate(products):
        proj[group ^ i] = product[...]
    whole = jnp.concatenate([proj[i] for i in range(size)], axis=1)
    query[...] = whole[:, :QCOLS]
    block[:rows] = row_norm(whole[:, QCOLS:].astype(jnp.float32)).astype(jnp.bfloat16)
    digits = jnp.concatenate([slots[...] & 255, slots[...] >> 8], axis=0).astype(jnp.float32)
    digits = jnp.concatenate([digits, jnp.zeros((14, rows), jnp.float32)], axis=0).astype(jnp.bfloat16)
    block[rows:] = jnp.zeros_like(block[rows:])
    block[rows:, :rows] = digits


def attend_kernel(count, size, lengths, query, *refs):
    blocks, refs = refs[:count], refs[count:]
    expands, refs = refs[:size], refs[size:]
    out, latent, expand, bias = refs
    rows, rank = query.shape[0], latent.shape[1]
    places = []
    for i, block in enumerate(blocks):
        latent[i * rows : (i + 1) * rows, :] = block[:rows]
        digits = block[rows:, :rows].astype(jnp.float32)
        places.append(digits[1:2] * 256.0 + digits[:1])
    others = jnp.concatenate(places, axis=1).astype(jnp.int32)
    width = expands[0].shape[1]
    for i, block in enumerate(expands):
        at = (lax.axis_index("group") ^ i) * width
        expand[:, pl.ds(pl.multiple_of(at, width), width)] = block[...]
    same = lax.broadcasted_iota(jnp.int32, (rows, rows), 0) == lax.broadcasted_iota(jnp.int32, (rows, rows), 1)
    position = jnp.sum(jnp.where(same, places[0], 0.0), axis=1, keepdims=True).astype(jnp.int32)
    start = jnp.zeros_like(position)
    end = 0
    for i in range(lengths.shape[1]):
        end = end + lengths[0, i]
        start = jnp.where(position >= end, end, start)
    allowed = (others <= position) & (others >= start)
    bias[...] = jnp.where(allowed, 0.0, NEGATIVE)
    some = 4
    for first in range(0, HEADS, some):
        heads = range(first, first + some)
        turned = [
            lax.dot_general(
                query[:, head * HDIM : (head + 1) * HDIM],
                expand[:, head * 2 * HDIM : (2 * head + 1) * HDIM],
                (((1,), (1,)), ((), ())),
                preferred_element_type=jnp.float32,
            )
            for head in heads
        ]
        turned = (jnp.concatenate(turned, axis=0) * LOG2_E).astype(jnp.bfloat16)
        scores = lax.dot_general(
            turned, latent[...], (((1,), (1,)), ((), ())), preferred_element_type=jnp.float32
        )
        scores = scores.reshape(some, rows, count * rows) + bias[...][None]
        peak = jnp.max(scores, axis=-1, keepdims=True)
        weights = jnp.exp2(scores - peak)
        total = jnp.sum(weights, axis=-1, keepdims=True)
        probs = weights.astype(jnp.bfloat16).reshape(some * rows, count * rows)
        summed = jnp.dot(probs, latent[...], preferred_element_type=jnp.float32).astype(jnp.bfloat16)
        for i, head in enumerate(heads):
            value = expand[:, (2 * head + 1) * HDIM : (2 * head + 2) * HDIM]
            outcome = jnp.dot(summed[i * rows : (i + 1) * rows], value, preferred_element_type=jnp.float32)
            out[:, head * HDIM : (head + 1) * HDIM] = (outcome / total[i]).astype(jnp.bfloat16)


def body(arrivals, slots, lengths, w_joined, w_expand):
    count, size = lax.axis_size("mp"), lax.axis_size("group")
    rows, depth = arrivals.shape
    columns, rank = w_joined.shape[1], w_expand.shape[0] * count
    own_columns = w_expand.shape[1]

    weights = pl.pallas_call(
        pack_kernel,
        out_shape=jax.ShapeDtypeStruct(
            (w_joined.shape[0], columns + own_columns * w_expand.shape[0] // w_joined.shape[0]), jnp.bfloat16
        ),
        in_specs=[VMEM, VMEM],
        out_specs=VMEM,
        compiler_params=PARAMS,
        name="pack",
    )(w_joined, w_expand)
    blocks = ring_gather(weights, size, count)
    arrivals, _ = lax.optimization_barrier((arrivals, weights))
    normed = row_norm(arrivals.astype(jnp.float32)).astype(jnp.bfloat16)
    tokens = group_gather(normed, size)
    *projs, own_expand = pl.pallas_call(
        functools.partial(proj_kernel, count, size),
        out_shape=[jax.ShapeDtypeStruct((rows, columns), jnp.bfloat16)] * size
        + [jax.ShapeDtypeStruct((rank, own_columns), jnp.bfloat16)],
        in_specs=[VMEM] * (size + count),
        out_specs=[VMEM] * (size + 1),
        scratch_shapes=[pltpu.VMEM((depth, columns), jnp.bfloat16)],
        compiler_params=PARAMS,
        cost_estimate=pl.CostEstimate(
            flops=2 * size * rows * depth * columns, bytes_accessed=4 * depth * columns, transcendentals=0
        ),
        name="project",
    )(*tokens, *blocks)

    back = [projs[0]]
    for k in range(1, size):
        back.append(lax.ppermute(projs[k], "group", [(i, i ^ k) for i in range(size)]))
    query, block = pl.pallas_call(
        functools.partial(assemble_kernel, size),
        out_shape=[
            jax.ShapeDtypeStruct((rows, QCOLS), jnp.bfloat16),
            jax.ShapeDtypeStruct((rows + 16, rank), jnp.bfloat16),
        ],
        in_specs=[VMEM] * (size + 1),
        out_specs=[VMEM, VMEM],
        scratch_shapes=[pltpu.VMEM((size, rows, columns), jnp.bfloat16)],
        compiler_params=PARAMS,
        name="assemble",
    )(slots.reshape(1, rows), *back)
    lat_blocks = ring_gather(block, size, count)
    own_expand, _ = lax.optimization_barrier((own_expand, lat_blocks[1:3]))
    expands = group_gather(own_expand, size, lat_blocks[-3:-1])

    total = count * rows
    return pl.pallas_call(
        functools.partial(attend_kernel, count, size),
        out_shape=jax.ShapeDtypeStruct((rows, QCOLS), jnp.bfloat16),
        in_specs=[SMEM] + [VMEM] * (1 + count + size),
        out_specs=VMEM,
        scratch_shapes=[
            pltpu.VMEM((total, rank), jnp.bfloat16),
            pltpu.VMEM((rank, 2 * QCOLS), jnp.bfloat16),
            pltpu.VMEM((rows, total), jnp.float32),
        ],
        compiler_params=PARAMS,
        cost_estimate=pl.CostEstimate(
            flops=4 * total * rank * QCOLS + 4 * rows * total * QCOLS,
            bytes_accessed=2 * (total + 2 * QCOLS) * rank,
            transcendentals=HEADS * rows * total,
        ),
        name="attend",
    )(lengths, query, *lat_blocks, *expands)


def solution(mesh):
    in_specs = (
        P(("group", "mp"), None),
        P(("group", "mp")),
        P("group", None),
        P("mp", "group"),
        P("mp", "group"),
    )
    out_specs = P(("group", "mp"), None)
    return jax.shard_map(body, mesh=mesh, in_specs=in_specs, out_specs=out_specs, check_vma=False)
```

```python
import functools

import jax
import jax.numpy as jnp
from jax import lax
from jax.experimental import pallas as pl
from jax.experimental.pallas import tpu as pltpu
from jax.sharding import PartitionSpec as P

HEADS = 8
HDIM = 128
QCOLS = HEADS * HDIM

EPS = 1e-06
NEGATIVE = -1e30
LOG2_E = 1.4426950408889634
VMEM = pl.BlockSpec(memory_space=pltpu.VMEM)
SMEM = pl.BlockSpec(memory_space=pltpu.SMEM)
PARAMS = pltpu.CompilerParams(vmem_limit_bytes=56 * 1024 * 1024)


def row_norm(values):
    mean_sq = jnp.mean(values * values, axis=-1, keepdims=True)
    return values * lax.rsqrt(mean_sq + EPS)


def ring_pairs(count, step):
    order = [2 * r if r < count // 2 else 2 * (count - 1 - r) + 1 for r in range(count)]
    return [(order[r], order[(r + step) % count]) for r in range(count)]


def ring_gather(block, count):
    up, down = ring_pairs(count, 1), ring_pairs(count, -1)
    below = above = block
    blocks = [block]
    for _ in range((count - 1) // 2):
        below, above = lax.ppermute(below, "mp", up), lax.ppermute(above, "mp", down)
        blocks += [below, above]
    cut = -(-block.shape[0] // 32) * 16
    return blocks + [lax.ppermute(below[:cut], "mp", up), lax.ppermute(above[cut:], "mp", down)]


def ring_owners(count):
    me = lax.axis_index("mp")
    place = jnp.where(me % 2 == 0, me // 2, count - 1 - me // 2)
    owners = [me]
    for step in range(1, count // 2 + 1):
        for shift in (-step, step):
            at = lax.rem(place + shift + count, count)
            owners.append(jnp.where(at < count // 2, 2 * at, 2 * (count - 1 - at) + 1))
    return owners[:count]


def row_ranges(blocks):
    last = len(blocks) - 2
    return [(i, 0) for i in range(last + 1)] + [(last, blocks[last].shape[0])]


def group_gather(block, size, after=None):
    blocks = {0: block}
    bit = size // 2
    while bit:
        pairs = [(i, i ^ bit) for i in range(size)]
        for k in list(blocks):
            sent = blocks[k]
            if k and after is not None:
                sent, _ = lax.optimization_barrier((sent, after))
            blocks[k ^ bit] = lax.ppermute(sent, "group", pairs)
        bit //= 2
    return [blocks[k] for k in range(size)]


def pack_kernel(joined, expand, out):
    columns, high = joined.shape[1], expand.shape[0]
    folds = joined.shape[0] // high
    fold = expand.shape[1] // folds
    out[:, :columns] = joined[...].astype(jnp.bfloat16)
    for i in range(folds):
        out[i * high : (i + 1) * high, columns:] = expand[:, i * fold : (i + 1) * fold].astype(jnp.bfloat16)


def multiply(tokens, starts, blocks, columns):
    total = None
    for start, block in zip(starts, blocks):
        span = pl.ds(pl.multiple_of(start, 128), block.shape[0])
        left = jnp.concatenate([token[:, span] for token in tokens], axis=0)
        product = jnp.dot(left, block[:, :columns], preferred_element_type=jnp.float32)
        total = product if total is None else total + product
    return total


def early_kernel(count, size, *refs):
    tokens, blocks, total = refs[:size], refs[size:-1], refs[-1]
    depth = blocks[0].shape[0]
    total[...] = multiply(tokens, [owner * depth for owner in ring_owners(count)], blocks, total.shape[1])


def proj_kernel(count, size, early, *refs):
    tokens, refs = refs[:size], refs[size:]
    blocks, refs = refs[: count + 1], refs[count + 1 :]
    depth = blocks[0].shape[0]
    owners = ring_owners(count)
    starts = [owners[i] * depth + offset for i, offset in row_ranges(blocks)]
    if early:
        total, refs = refs[0], refs[1:]
        outs, expand = refs[:size], refs[size]
        rows, columns = outs[0].shape
        proj = total[...] + multiply(tokens, starts[early:], blocks[early:], columns)
    else:
        outs, expand, weight = refs[:size], refs[size], refs[size + 1]
        rows, columns = outs[0].shape
        for start, block in zip(starts, blocks):
            length = block.shape[0]
            weight[pl.ds(pl.multiple_of(start, length), length), :] = block[:, :columns]
        products = [jnp.dot(token[...], weight[...], preferred_element_type=jnp.float32) for token in tokens]
        proj = jnp.concatenate(products, axis=0)
    at = lax.axis_index("group") * columns + lax.broadcasted_iota(jnp.int32, (1, columns), 1)
    proj = proj * jnp.where(at < QCOLS, HDIM**-0.5, 1.0).astype(jnp.float32)
    for i, out in enumerate(outs):
        out[...] = proj[i * rows : (i + 1) * rows].astype(jnp.bfloat16)
    high = expand.shape[0] // count
    for i, owner in enumerate(owners):
        parts = []
        for block in blocks[i:] if i == count - 1 else blocks[i : i + 1]:
            parts += [block[j * high : (j + 1) * high, columns:] for j in range(block.shape[0] // high)]
        expand[pl.ds(pl.multiple_of(owner * high, high), high), :] = jnp.concatenate(parts, axis=1)


def assemble_kernel(size, slots, *refs):
    products, (query, block, proj) = refs[:size], refs[size:]
    rows, columns = products[0].shape
    group = lax.axis_index("group")
    for i, product in enumerate(products):
        proj[group ^ i] = product[...]
    whole = jnp.concatenate([proj[i] for i in range(size)], axis=1)
    query[...] = whole[:, :QCOLS]
    block[:rows] = row_norm(whole[:, QCOLS:].astype(jnp.float32)).astype(jnp.bfloat16)
    digits = jnp.concatenate([slots[...] & 255, slots[...] >> 8], axis=0).astype(jnp.float32)
    digits = jnp.concatenate([digits, jnp.zeros((14, rows), jnp.float32)], axis=0).astype(jnp.bfloat16)
    block[rows:] = jnp.zeros_like(block[rows:])
    block[rows:, :rows] = digits


def attend_kernel(count, size, lengths, query, *refs):
    blocks, refs = refs[: count + 1], refs[count + 1 :]
    expands, refs = refs[:size], refs[size:]
    out, latent, expand, bias, scores, probs, totals = refs
    rows, rank = query.shape[0], latent.shape[1]
    places = []
    for (i, offset), block in zip(row_ranges(blocks), blocks):
        length = min(rows - offset, block.shape[0])
        latent[i * rows + offset : i * rows + offset + length, :] = block[:length]
        if length < block.shape[0]:
            digits = block[length:, :rows].astype(jnp.float32)
            places.append(digits[1:2] * 256.0 + digits[:1])
    others = jnp.concatenate(places, axis=1).astype(jnp.int32)
    width = expands[0].shape[1]
    for i, block in enumerate(expands):
        at = (lax.axis_index("group") ^ i) * width
        expand[:, pl.ds(pl.multiple_of(at, width), width)] = block[...]
    same = lax.broadcasted_iota(jnp.int32, (rows, rows), 0) == lax.broadcasted_iota(jnp.int32, (rows, rows), 1)
    position = jnp.sum(jnp.where(same, places[0], 0.0), axis=1, keepdims=True).astype(jnp.int32)
    start = jnp.zeros_like(position)
    end = 0
    for i in range(lengths.shape[1]):
        end = end + lengths[0, i]
        start = jnp.where(position >= end, end, start)
    allowed = (others <= position) & (others >= start)
    bias[...] = jnp.where(allowed, 0.0, NEGATIVE)
    some, tile = HEADS // 2, 16
    for first in range(0, HEADS, some):
        turned = [
            lax.dot_general(
                query[:, head * HDIM : (head + 1) * HDIM],
                expand[:, head * 2 * HDIM : (2 * head + 1) * HDIM],
                (((1,), (1,)), ((), ())),
                preferred_element_type=jnp.float32,
            )
            for head in range(first, first + some)
        ]
        turned = (jnp.concatenate(turned, axis=0) * LOG2_E).astype(jnp.bfloat16)
        scores[first * rows : (first + some) * rows] = lax.dot_general(
            turned, latent[...], (((1,), (1,)), ((), ())), preferred_element_type=jnp.float32
        )
    for first in range(0, HEADS, some):
        for at in range(first * rows, (first + some) * rows, tile):
            part = scores[at : at + tile] + bias[at % rows : at % rows + tile]
            weights = jnp.exp2(part - jnp.max(part, axis=-1, keepdims=True))
            totals[at : at + tile] = jnp.sum(weights, axis=-1, keepdims=True)
            probs[at : at + tile] = weights.astype(jnp.bfloat16)
        summed = jnp.dot(
            probs[first * rows : (first + some) * rows], latent[...], preferred_element_type=jnp.float32
        ).astype(jnp.bfloat16)
        for i in range(some):
            head = first + i
            value = expand[:, (2 * head + 1) * HDIM : (2 * head + 2) * HDIM]
            outcome = jnp.dot(summed[i * rows : (i + 1) * rows], value, preferred_element_type=jnp.float32)
            total = totals[head * rows : (head + 1) * rows]
            out[:, head * HDIM : (head + 1) * HDIM] = (outcome / total).astype(jnp.bfloat16)


def body(arrivals, slots, lengths, w_joined, w_expand):
    count, size = lax.axis_size("mp"), lax.axis_size("group")
    rows, depth = arrivals.shape
    columns, rank = w_joined.shape[1], w_expand.shape[0] * count
    own_columns = w_expand.shape[1]

    weights = pl.pallas_call(
        pack_kernel,
        out_shape=jax.ShapeDtypeStruct(
            (w_joined.shape[0], columns + own_columns * w_expand.shape[0] // w_joined.shape[0]), jnp.bfloat16
        ),
        in_specs=[VMEM, VMEM],
        out_specs=VMEM,
        compiler_params=PARAMS,
        name="pack",
    )(w_joined, w_expand)
    blocks = ring_gather(weights, count)
    arrivals, _ = lax.optimization_barrier((arrivals, weights))
    normed = row_norm(arrivals.astype(jnp.float32)).astype(jnp.bfloat16)
    tokens = group_gather(normed, size)
    early = 0 if w_joined.shape[0] // 2 % 128 else count - 3
    total = []
    if early:
        total = [
            pl.pallas_call(
                functools.partial(early_kernel, count, size),
                out_shape=jax.ShapeDtypeStruct((size * rows, columns), jnp.float32),
                in_specs=[VMEM] * (size + early),
                out_specs=VMEM,
                compiler_params=PARAMS,
                cost_estimate=pl.CostEstimate(
                    flops=2 * size * rows * depth * columns, bytes_accessed=4 * depth * columns, transcendentals=0
                ),
                name="project_early",
            )(*tokens, *blocks[:early])
        ]
    *projs, own_expand = pl.pallas_call(
        functools.partial(proj_kernel, count, size, early),
        out_shape=[jax.ShapeDtypeStruct((rows, columns), jnp.bfloat16)] * size
        + [jax.ShapeDtypeStruct((rank, own_columns), jnp.bfloat16)],
        in_specs=[VMEM] * (size + count + 1 + len(total)),
        out_specs=[VMEM] * (size + 1),
        scratch_shapes=[] if early else [pltpu.VMEM((depth, columns), jnp.bfloat16)],
        compiler_params=PARAMS,
        cost_estimate=pl.CostEstimate(
            flops=2 * size * rows * depth * columns, bytes_accessed=4 * depth * columns, transcendentals=0
        ),
        name="project",
    )(*tokens, *blocks, *total)

    back = [projs[0]]
    for k in range(1, size):
        back.append(lax.ppermute(projs[k], "group", [(i, i ^ k) for i in range(size)]))
    query, block = pl.pallas_call(
        functools.partial(assemble_kernel, size),
        out_shape=[
            jax.ShapeDtypeStruct((rows, QCOLS), jnp.bfloat16),
            jax.ShapeDtypeStruct((rows + 16, rank), jnp.bfloat16),
        ],
        in_specs=[VMEM] * (size + 1),
        out_specs=[VMEM, VMEM],
        scratch_shapes=[pltpu.VMEM((size, rows, columns), jnp.bfloat16)],
        compiler_params=PARAMS,
        name="assemble",
    )(slots.reshape(1, rows), *back)
    lat_blocks = ring_gather(block, count)
    own_expand, _ = lax.optimization_barrier((own_expand, lat_blocks[1:3]))
    expands = group_gather(own_expand, size, lat_blocks[-4:-2])

    total = count * rows
    return pl.pallas_call(
        functools.partial(attend_kernel, count, size),
        out_shape=jax.ShapeDtypeStruct((rows, QCOLS), jnp.bfloat16),
        in_specs=[SMEM] + [VMEM] * (2 + count + size),
        out_specs=VMEM,
        scratch_shapes=[
            pltpu.VMEM((total, rank), jnp.bfloat16),
            pltpu.VMEM((rank, 2 * QCOLS), jnp.bfloat16),
            pltpu.VMEM((rows, total), jnp.float32),
            pltpu.VMEM((HEADS * rows, total), jnp.float32),
            pltpu.VMEM((HEADS * rows, total), jnp.bfloat16),
            pltpu.VMEM((HEADS * rows, 1), jnp.float32),
        ],
        compiler_params=PARAMS,
        cost_estimate=pl.CostEstimate(
            flops=4 * total * rank * QCOLS + 4 * rows * total * QCOLS,
            bytes_accessed=2 * (total + 2 * QCOLS) * rank,
            transcendentals=HEADS * rows * total,
        ),
        name="attend",
    )(lengths, query, *lat_blocks, *expands)


def solution(mesh):
    in_specs = (
        P(("group", "mp"), None),
        P(("group", "mp")),
        P("group", None),
        P("mp", "group"),
        P("mp", "group"),
    )
    out_specs = P(("group", "mp"), None)
    return jax.shard_map(body, mesh=mesh, in_specs=in_specs, out_specs=out_specs, check_vma=False)
```

```python
import functools

import jax
import jax.numpy as jnp
from jax import lax
from jax.experimental import pallas as pl
from jax.experimental.pallas import tpu as pltpu
from jax.sharding import PartitionSpec as P

HEADS = 8
HDIM = 128
QCOLS = HEADS * HDIM

EPS = 1e-06
NEGATIVE = -1e30
LOG2_E = 1.4426950408889634
TILE = 16
VMEM = pl.BlockSpec(memory_space=pltpu.VMEM)
SMEM = pl.BlockSpec(memory_space=pltpu.SMEM)
PARAMS = pltpu.CompilerParams(vmem_limit_bytes=56 * 1024 * 1024)


def row_norm(values):
    mean_sq = jnp.mean(values * values, axis=-1, keepdims=True)
    return values * lax.rsqrt(mean_sq + EPS)


def ring_pairs(count, step):
    order = [2 * r if r < count // 2 else 2 * (count - 1 - r) + 1 for r in range(count)]
    return [(order[r], order[(r + step) % count]) for r in range(count)]


def ring_gather(block, count, beside):
    up, down = ring_pairs(count, 1), ring_pairs(count, -1)
    below = above = block
    blocks = [block]
    for _ in range((count - 1) // 2):
        below, above = lax.ppermute(below, "mp", up), lax.ppermute(above, "mp", down)
        blocks += [below, above]
    made = beside(blocks[:-2])
    below, above, made = lax.optimization_barrier((below, above, made))
    cut = -(-block.shape[0] // 32) * 16
    return blocks + [lax.ppermute(below[:cut], "mp", up), lax.ppermute(above[cut:], "mp", down)], made


def ring_owners(count):
    me = lax.axis_index("mp")
    place = jnp.where(me % 2 == 0, me // 2, count - 1 - me // 2)
    owners = [me]
    for step in range(1, count // 2 + 1):
        for shift in (-step, step):
            at = lax.rem(place + shift + count, count)
            owners.append(jnp.where(at < count // 2, 2 * at, 2 * (count - 1 - at) + 1))
    return owners[:count]


def row_ranges(blocks):
    last = len(blocks) - 2
    return [(i, 0) for i in range(last + 1)] + [(last, blocks[last].shape[0])]


def group_gather(block, size, after=None):
    blocks = {0: block}
    bit = size // 2
    while bit:
        pairs = [(i, i ^ bit) for i in range(size)]
        for k in list(blocks):
            sent = blocks[k]
            if k and after is not None:
                sent, _ = lax.optimization_barrier((sent, after))
            blocks[k ^ bit] = lax.ppermute(sent, "group", pairs)
        bit //= 2
    return [blocks[k] for k in range(size)]


def multiply(tokens, starts, blocks, columns):
    total = None
    for start, block in zip(starts, blocks):
        span = pl.ds(pl.multiple_of(start, 128), block.shape[0])
        left = jnp.concatenate([token[:, span] for token in tokens], axis=0)
        product = jnp.dot(left, block[:, :columns], preferred_element_type=jnp.float32)
        total = product if total is None else total + product
    return total


def early_kernel(count, size, first, *refs):
    tokens, refs = refs[:size], refs[size:]
    *blocks, total = refs
    depth = total.shape[1]
    before = None
    if first:
        *blocks, before = blocks
    starts = [owner * blocks[0].shape[0] for owner in ring_owners(count)[first:]]
    product = multiply(tokens, starts, blocks, depth)
    total[...] = before[...] + product if first else product


def proj_kernel(count, size, early, *refs):
    tokens, refs = refs[:size], refs[size:]
    blocks, refs = refs[: count + 1], refs[count + 1 :]
    depth = blocks[0].shape[0]
    owners = ring_owners(count)
    starts = [owners[i] * depth + offset for i, offset in row_ranges(blocks)]
    if early:
        total, refs = refs[0], refs[1:]
        outs, expand = refs[:size], refs[size]
        rows, columns = outs[0].shape
        proj = total[...] + multiply(tokens, starts[early:], blocks[early:], columns)
    else:
        outs, expand, weight = refs[:size], refs[size], refs[size + 1]
        rows, columns = outs[0].shape
        for start, block in zip(starts, blocks):
            length = block.shape[0]
            weight[pl.ds(pl.multiple_of(start, length), length), :] = block[:, :columns]
        products = [jnp.dot(token[...], weight[...], preferred_element_type=jnp.float32) for token in tokens]
        proj = jnp.concatenate(products, axis=0)
    at = lax.axis_index("group") * columns + lax.broadcasted_iota(jnp.int32, (1, columns), 1)
    proj = proj * jnp.where(at < QCOLS, HDIM**-0.5, 1.0).astype(jnp.float32)
    for i, out in enumerate(outs):
        out[...] = proj[i * rows : (i + 1) * rows].astype(jnp.bfloat16)
    high = expand.shape[0] // count
    for i, owner in enumerate(owners):
        parts = []
        for block in blocks[i:] if i == count - 1 else blocks[i : i + 1]:
            parts += [block[j * high : (j + 1) * high, columns:] for j in range(block.shape[0] // high)]
        expand[pl.ds(pl.multiple_of(owner * high, high), high), :] = jnp.concatenate(parts, axis=1)


def assemble_kernel(size, slots, *refs):
    products, (query, block, proj) = refs[:size], refs[size:]
    rows, columns = products[0].shape
    group = lax.axis_index("group")
    for i, product in enumerate(products):
        proj[group ^ i] = product[...]
    whole = jnp.concatenate([proj[i] for i in range(size)], axis=1)
    query[...] = whole[:, :QCOLS]
    block[:rows] = row_norm(whole[:, QCOLS:].astype(jnp.float32)).astype(jnp.bfloat16)
    digits = jnp.concatenate([slots[...] & 255, slots[...] >> 8], axis=0).astype(jnp.float32)
    digits = jnp.concatenate([digits, jnp.zeros((14, rows), jnp.float32)], axis=0).astype(jnp.bfloat16)
    block[rows:] = jnp.zeros_like(block[rows:])
    block[rows:, :rows] = digits


def position_of(block, rows):
    digits = block[block.shape[0] - 16 :, :rows].astype(jnp.float32)
    return digits[1:2] * 256.0 + digits[:1]


def place_latents(lengths, own, blocks, ranges, latent, bias):
    rows = own.shape[0] - 16
    places = []
    for (i, offset), block in zip(ranges, blocks):
        length = min(rows - offset, block.shape[0])
        latent[i * rows + offset : i * rows + offset + length, :] = block[:length]
        if length < block.shape[0]:
            places.append(position_of(block, rows))
    others = jnp.concatenate(places, axis=1).astype(jnp.int32)
    same = lax.broadcasted_iota(jnp.int32, (rows, rows), 0) == lax.broadcasted_iota(jnp.int32, (rows, rows), 1)
    position = jnp.sum(jnp.where(same, position_of(own, rows), 0.0), axis=1, keepdims=True).astype(jnp.int32)
    start = jnp.zeros_like(position)
    end = 0
    for i in range(lengths.shape[1]):
        end = end + lengths[0, i]
        start = jnp.where(position >= end, end, start)
    allowed = (others <= position) & (others >= start)
    bias[...] = jnp.where(allowed, 0.0, NEGATIVE)


def score(turned, latent, scores):
    half = turned.shape[0] // 2
    for at in (0, half):
        scores[at : at + half] = lax.dot_general(
            turned[at : at + half], latent[...], (((1,), (1,)), ((), ())), preferred_element_type=jnp.float32
        )


def attend_early_kernel(count, size, lengths, query, *refs):
    blocks, refs = refs[: count - 3], refs[count - 3 :]
    expands, refs = refs[:size], refs[size:]
    turned, value, state, summed, latent, expand, bias, scores, probs = refs
    rows = query.shape[0]
    place_latents(lengths, blocks[0], blocks, [(i, 0) for i in range(len(blocks))], latent, bias)
    width = expands[0].shape[1]
    for i, block in enumerate(expands):
        at = (lax.axis_index("group") ^ i) * width
        expand[:, pl.ds(pl.multiple_of(at, width), width)] = block[...]
    for head in range(HEADS):
        value[:, head * HDIM : (head + 1) * HDIM] = expand[:, (2 * head + 1) * HDIM : (2 * head + 2) * HDIM]
        product = lax.dot_general(
            query[:, head * HDIM : (head + 1) * HDIM],
            expand[:, head * 2 * HDIM : (2 * head + 1) * HDIM],
            (((1,), (1,)), ((), ())),
            preferred_element_type=jnp.float32,
        )
        turned[head * rows : (head + 1) * rows] = (product * LOG2_E).astype(jnp.bfloat16)
    score(turned, latent, scores)
    half = HEADS * rows // 2
    for first in (0, half):
        for at in range(first, first + half, TILE):
            part = scores[at : at + TILE] + bias[at % rows : at % rows + TILE]
            peak = jnp.max(part, axis=-1, keepdims=True)
            weights = jnp.exp2(part - peak)
            state[at : at + TILE] = jnp.concatenate([peak, jnp.sum(weights, axis=-1, keepdims=True)], axis=1)
            probs[at : at + TILE] = weights.astype(jnp.bfloat16)
        summed[first : first + half] = jnp.dot(
            probs[first : first + half], latent[...], preferred_element_type=jnp.float32
        )


def attend_kernel(lengths, own, turned, value, state, summed, *refs):
    blocks, (out, latent, bias, scores, probs, factors) = refs[:-6], refs[-6:]
    rows = out.shape[0]
    place_latents(lengths, own, blocks, row_ranges(blocks), latent, bias)
    score(turned, latent, scores)
    half = HEADS * rows // 2
    for first in (0, half):
        for at in range(first, first + half, TILE):
            part = scores[at : at + TILE] + bias[at % rows : at % rows + TILE]
            peak, total = state[at : at + TILE, :1], state[at : at + TILE, 1:2]
            new_peak = jnp.maximum(peak, jnp.max(part, axis=-1, keepdims=True))
            weights = jnp.exp2(part - new_peak)
            rescale = jnp.exp2(peak - new_peak)
            total = total * rescale + jnp.sum(weights, axis=-1, keepdims=True)
            factors[at : at + TILE] = jnp.concatenate([rescale, 1.0 / total], axis=1)
            probs[at : at + TILE] = weights.astype(jnp.bfloat16)
        update = jnp.dot(probs[first : first + half], latent[...], preferred_element_type=jnp.float32)
        update = summed[first : first + half] * factors[first : first + half, :1] + update
        update = update.astype(jnp.bfloat16)
        for i in range(HEADS // 2):
            columns = slice(first // rows * HDIM + i * HDIM, first // rows * HDIM + (i + 1) * HDIM)
            at = first + i * rows
            outcome = jnp.dot(update[i * rows : (i + 1) * rows], value[:, columns], preferred_element_type=jnp.float32)
            out[:, columns] = (outcome * factors[at : at + rows, 1:2]).astype(jnp.bfloat16)


def body(arrivals, slots, lengths, w_joined, w_expand):
    count, size = lax.axis_size("mp"), lax.axis_size("group")
    rows, depth = arrivals.shape
    columns, rank = w_joined.shape[1], w_expand.shape[0] * count
    own_columns = w_expand.shape[1]

    folds = w_joined.shape[0] // w_expand.shape[0]
    fold = own_columns // folds
    folded = jnp.concatenate([w_expand[:, i * fold : (i + 1) * fold] for i in range(folds)], axis=0)
    weights = jnp.concatenate([w_joined, folded], axis=1).astype(jnp.bfloat16)
    arrivals, _ = lax.optimization_barrier((arrivals, weights))
    normed = row_norm(arrivals.astype(jnp.float32)).astype(jnp.bfloat16)
    tokens = group_gather(normed, size)
    early = 0 if w_joined.shape[0] // 2 % 128 else count - 1

    def project_early(first, blocks, *before):
        if not early:
            return before
        return [
            pl.pallas_call(
                functools.partial(early_kernel, count, size, first),
                out_shape=jax.ShapeDtypeStruct((size * rows, columns), jnp.float32),
                in_specs=[VMEM] * (size + len(blocks) + len(before)),
                out_specs=VMEM,
                compiler_params=PARAMS,
                cost_estimate=pl.CostEstimate(
                    flops=2 * size * rows * depth * columns, bytes_accessed=4 * depth * columns, transcendentals=0
                ),
                name="project_early",
            )(*tokens, *blocks, *before)
        ]

    blocks, total = ring_gather(weights, count, lambda blocks: project_early(0, blocks))
    total = project_early(count - 3, blocks[count - 3 : count - 1], *total)
    *projs, own_expand = pl.pallas_call(
        functools.partial(proj_kernel, count, size, early),
        out_shape=[jax.ShapeDtypeStruct((rows, columns), jnp.bfloat16)] * size
        + [jax.ShapeDtypeStruct((rank, own_columns), jnp.bfloat16)],
        in_specs=[VMEM] * (size + count + 1 + len(total)),
        out_specs=[VMEM] * (size + 1),
        scratch_shapes=[] if early else [pltpu.VMEM((depth, columns), jnp.bfloat16)],
        compiler_params=PARAMS,
        cost_estimate=pl.CostEstimate(
            flops=2 * size * rows * depth * columns, bytes_accessed=4 * depth * columns, transcendentals=0
        ),
        name="project",
    )(*tokens, *blocks, *total)

    back = [projs[0]]
    for k in range(1, size):
        back.append(lax.ppermute(projs[k], "group", [(i, i ^ k) for i in range(size)]))
    query, block = pl.pallas_call(
        functools.partial(assemble_kernel, size),
        out_shape=[
            jax.ShapeDtypeStruct((rows, QCOLS), jnp.bfloat16),
            jax.ShapeDtypeStruct((rows + 16, rank), jnp.bfloat16),
        ],
        in_specs=[VMEM] * (size + 1),
        out_specs=[VMEM, VMEM],
        scratch_shapes=[pltpu.VMEM((size, rows, columns), jnp.bfloat16)],
        compiler_params=PARAMS,
        name="assemble",
    )(slots.reshape(1, rows), *back)
    total, seen = count * rows, (count - 3) * rows

    def attend_early(blocks):
        expands = group_gather(own_expand, size, blocks[1:3])
        return pl.pallas_call(
            functools.partial(attend_early_kernel, count, size),
            out_shape=[
                jax.ShapeDtypeStruct((HEADS * rows, rank), jnp.bfloat16),
                jax.ShapeDtypeStruct((rank, QCOLS), jnp.bfloat16),
                jax.ShapeDtypeStruct((HEADS * rows, 2), jnp.float32),
                jax.ShapeDtypeStruct((HEADS * rows, rank), jnp.float32),
            ],
            in_specs=[SMEM] + [VMEM] * (1 + len(blocks) + size),
            out_specs=[VMEM] * 4,
            scratch_shapes=[
                pltpu.VMEM((seen, rank), jnp.bfloat16),
                pltpu.VMEM((rank, 2 * QCOLS), jnp.bfloat16),
                pltpu.VMEM((rows, seen), jnp.float32),
                pltpu.VMEM((HEADS * rows, seen), jnp.float32),
                pltpu.VMEM((HEADS * rows, seen), jnp.bfloat16),
            ],
            compiler_params=PARAMS,
            cost_estimate=pl.CostEstimate(
                flops=4 * total * rank * QCOLS, bytes_accessed=8 * QCOLS * rank, transcendentals=HEADS * rows * seen
            ),
            name="attend_early",
        )(lengths, query, *blocks, *expands)

    own_expand, _ = lax.optimization_barrier((own_expand, back))
    lat_blocks, made = ring_gather(block, count, attend_early)
    late = lat_blocks[count - 3 :]
    return pl.pallas_call(
        attend_kernel,
        out_shape=jax.ShapeDtypeStruct((rows, QCOLS), jnp.bfloat16),
        in_specs=[SMEM] + [VMEM] * (5 + len(late)),
        out_specs=VMEM,
        scratch_shapes=[
            pltpu.VMEM((total - seen, rank), jnp.bfloat16),
            pltpu.VMEM((rows, total - seen), jnp.float32),
            pltpu.VMEM((HEADS * rows, total - seen), jnp.float32),
            pltpu.VMEM((HEADS * rows, total - seen), jnp.bfloat16),
            pltpu.VMEM((HEADS * rows, 2), jnp.float32),
        ],
        compiler_params=PARAMS,
        cost_estimate=pl.CostEstimate(
            flops=2 * total * rank * QCOLS, bytes_accessed=8 * QCOLS * rank, transcendentals=HEADS * rows * (total - seen)
        ),
        name="attend",
    )(lengths, block, *made, *late)


def solution(mesh):
    in_specs = (
        P(("group", "mp"), None),
        P(("group", "mp")),
        P("group", None),
        P("mp", "group"),
        P("mp", "group"),
    )
    out_specs = P(("group", "mp"), None)
    return jax.shard_map(body, mesh=mesh, in_specs=in_specs, out_specs=out_specs, check_vma=False)
```

```python
import functools

import jax
import jax.numpy as jnp
from jax import lax
from jax.experimental import pallas as pl
from jax.experimental.pallas import tpu as pltpu
from jax.sharding import PartitionSpec as P

HEADS = 8
HDIM = 128
QCOLS = HEADS * HDIM

EPS = 1e-06
NEGATIVE = -1e30
LOG2_E = 1.4426950408889634
VMEM = pl.BlockSpec(memory_space=pltpu.VMEM)
SMEM = pl.BlockSpec(memory_space=pltpu.SMEM)


def grant(mib):
    return pltpu.CompilerParams(vmem_limit_bytes=mib * 1024 * 1024)


def row_norm(values):
    mean_sq = jnp.mean(values * values, axis=-1, keepdims=True)
    return values * lax.rsqrt(mean_sq + EPS)


def ring_pairs(count, step):
    order = [2 * r if r < count // 2 else 2 * (count - 1 - r) + 1 for r in range(count)]
    return [(order[r], order[(r + step) % count]) for r in range(count)]


def ring_gather(block, count):
    up, down = ring_pairs(count, 1), ring_pairs(count, -1)
    below = above = block
    blocks = [block]
    for _ in range((count - 1) // 2):
        below, above = lax.ppermute(below, "mp", up), lax.ppermute(above, "mp", down)
        blocks += [below, above]
    cut = -(-block.shape[0] // 32) * 16
    return blocks + [lax.ppermute(below[:cut], "mp", up), lax.ppermute(above[cut:], "mp", down)]


def ring_owners(count):
    me = lax.axis_index("mp")
    place = jnp.where(me % 2 == 0, me // 2, count - 1 - me // 2)
    owners = [me]
    for step in range(1, count // 2 + 1):
        for shift in (-step, step):
            at = lax.rem(place + shift + count, count)
            owners.append(jnp.where(at < count // 2, 2 * at, 2 * (count - 1 - at) + 1))
    return owners[:count]


def row_ranges(blocks):
    last = len(blocks) - 2
    return [(i, 0) for i in range(last + 1)] + [(last, blocks[last].shape[0])]


def group_gather(block, size, after=None):
    blocks = {0: block}
    bit = size // 2
    while bit:
        pairs = [(i, i ^ bit) for i in range(size)]
        for k in list(blocks):
            sent = blocks[k]
            if k and after is not None:
                sent, _ = lax.optimization_barrier((sent, after))
            blocks[k ^ bit] = lax.ppermute(sent, "group", pairs)
        bit //= 2
    return [blocks[k] for k in range(size)]


def pack_kernel(joined, expand, out):
    columns, high = joined.shape[1], expand.shape[0]
    folds = joined.shape[0] // high
    fold = expand.shape[1] // folds
    out[:, :columns] = joined[...].astype(jnp.bfloat16)
    for i in range(folds):
        out[i * high : (i + 1) * high, columns:] = expand[:, i * fold : (i + 1) * fold].astype(jnp.bfloat16)


def multiply(tokens, starts, blocks, columns):
    total = None
    for start, block in zip(starts, blocks):
        span = pl.ds(pl.multiple_of(start, 128), block.shape[0])
        left = jnp.concatenate([token[:, span] for token in tokens], axis=0)
        product = jnp.dot(left, block[:, :columns], preferred_element_type=jnp.float32)
        total = product if total is None else total + product
    return total


def early_kernel(count, size, *refs):
    tokens, blocks, total = refs[:size], refs[size:-1], refs[-1]
    depth = blocks[0].shape[0]
    total[...] = multiply(tokens, [owner * depth for owner in ring_owners(count)], blocks, total.shape[1])


def proj_kernel(count, size, early, *refs):
    tokens, refs = refs[:size], refs[size:]
    blocks, refs = refs[: count + 1], refs[count + 1 :]
    depth = blocks[0].shape[0]
    owners = ring_owners(count)
    starts = [owners[i] * depth + offset for i, offset in row_ranges(blocks)]
    if early:
        total, refs = refs[0], refs[1:]
        outs, expand = refs[:size], refs[size]
        rows, columns = outs[0].shape
        proj = total[...] + multiply(tokens, starts[early:], blocks[early:], columns)
    else:
        outs, expand, weight = refs[:size], refs[size], refs[size + 1]
        rows, columns = outs[0].shape
        for start, block in zip(starts, blocks):
            length = block.shape[0]
            weight[pl.ds(pl.multiple_of(start, length), length), :] = block[:, :columns]
        products = [jnp.dot(token[...], weight[...], preferred_element_type=jnp.float32) for token in tokens]
        proj = jnp.concatenate(products, axis=0)
    at = lax.axis_index("group") * columns + lax.broadcasted_iota(jnp.int32, (1, columns), 1)
    proj = proj * jnp.where(at < QCOLS, HDIM**-0.5, 1.0).astype(jnp.float32)
    for i, out in enumerate(outs):
        out[...] = proj[i * rows : (i + 1) * rows].astype(jnp.bfloat16)
    high = expand.shape[0] // count
    for i, owner in enumerate(owners):
        parts = []
        for block in blocks[i:] if i == count - 1 else blocks[i : i + 1]:
            parts += [block[j * high : (j + 1) * high, columns:] for j in range(block.shape[0] // high)]
        expand[pl.ds(pl.multiple_of(owner * high, high), high), :] = jnp.concatenate(parts, axis=1)


def assemble_kernel(size, slots, *refs):
    products, (query, block, proj) = refs[:size], refs[size:]
    rows, columns = products[0].shape
    group = lax.axis_index("group")
    for i, product in enumerate(products):
        proj[group ^ i] = product[...]
    whole = jnp.concatenate([proj[i] for i in range(size)], axis=1)
    query[...] = whole[:, :QCOLS]
    block[:rows] = row_norm(whole[:, QCOLS:].astype(jnp.float32)).astype(jnp.bfloat16)
    digits = jnp.concatenate([slots[...] & 255, slots[...] >> 8], axis=0).astype(jnp.float32)
    digits = jnp.concatenate([digits, jnp.zeros((14, rows), jnp.float32)], axis=0).astype(jnp.bfloat16)
    block[rows:] = jnp.zeros_like(block[rows:])
    block[rows:, :rows] = digits


def attend_kernel(count, size, lengths, query, *refs):
    blocks, refs = refs[: count + 1], refs[count + 1 :]
    expands, refs = refs[:size], refs[size:]
    out, latent, expand, bias, scores, probs, totals = refs
    rows, rank = query.shape[0], latent.shape[1]
    places = []
    for (i, offset), block in zip(row_ranges(blocks), blocks):
        length = min(rows - offset, block.shape[0])
        latent[i * rows + offset : i * rows + offset + length, :] = block[:length]
        if length < block.shape[0]:
            digits = block[length:, :rows].astype(jnp.float32)
            places.append(digits[1:2] * 256.0 + digits[:1])
    others = jnp.concatenate(places, axis=1).astype(jnp.int32)
    width = expands[0].shape[1]
    for i, block in enumerate(expands):
        at = (lax.axis_index("group") ^ i) * width
        expand[:, pl.ds(pl.multiple_of(at, width), width)] = block[...]
    same = lax.broadcasted_iota(jnp.int32, (rows, rows), 0) == lax.broadcasted_iota(jnp.int32, (rows, rows), 1)
    position = jnp.sum(jnp.where(same, places[0], 0.0), axis=1, keepdims=True).astype(jnp.int32)
    start = jnp.zeros_like(position)
    end = 0
    for i in range(lengths.shape[1]):
        end = end + lengths[0, i]
        start = jnp.where(position >= end, end, start)
    allowed = (others <= position) & (others >= start)
    bias[...] = jnp.where(allowed, 0.0, NEGATIVE)
    some, tile = HEADS // 2, 16
    for first in range(0, HEADS, some):
        turned = [
            lax.dot_general(
                query[:, head * HDIM : (head + 1) * HDIM],
                expand[:, head * 2 * HDIM : (2 * head + 1) * HDIM],
                (((1,), (1,)), ((), ())),
                preferred_element_type=jnp.float32,
            )
            for head in range(first, first + some)
        ]
        turned = (jnp.concatenate(turned, axis=0) * LOG2_E).astype(jnp.bfloat16)
        scores[first * rows : (first + some) * rows] = lax.dot_general(
            turned, latent[...], (((1,), (1,)), ((), ())), preferred_element_type=jnp.float32
        )
    for first in range(0, HEADS, some):
        for at in range(first * rows, (first + some) * rows, tile):
            part = scores[at : at + tile] + bias[at % rows : at % rows + tile]
            weights = jnp.exp2(part - jnp.max(part, axis=-1, keepdims=True))
            totals[at : at + tile] = jnp.sum(weights, axis=-1, keepdims=True)
            probs[at : at + tile] = weights.astype(jnp.bfloat16)
        summed = jnp.dot(
            probs[first * rows : (first + some) * rows], latent[...], preferred_element_type=jnp.float32
        ).astype(jnp.bfloat16)
        for i in range(some):
            head = first + i
            value = expand[:, (2 * head + 1) * HDIM : (2 * head + 2) * HDIM]
            outcome = jnp.dot(summed[i * rows : (i + 1) * rows], value, preferred_element_type=jnp.float32)
            total = totals[head * rows : (head + 1) * rows]
            out[:, head * HDIM : (head + 1) * HDIM] = (outcome / total).astype(jnp.bfloat16)


def body(arrivals, slots, lengths, w_joined, w_expand):
    count, size = lax.axis_size("mp"), lax.axis_size("group")
    rows, depth = arrivals.shape
    columns, rank = w_joined.shape[1], w_expand.shape[0] * count
    own_columns = w_expand.shape[1]

    weights = pl.pallas_call(
        pack_kernel,
        out_shape=jax.ShapeDtypeStruct(
            (w_joined.shape[0], columns + own_columns * w_expand.shape[0] // w_joined.shape[0]), jnp.bfloat16
        ),
        in_specs=[VMEM, VMEM],
        out_specs=VMEM,
        compiler_params=grant(16),
        name="pack",
    )(w_joined, w_expand)
    blocks = ring_gather(weights, count)
    arrivals, _ = lax.optimization_barrier((arrivals, weights))
    normed = row_norm(arrivals.astype(jnp.float32)).astype(jnp.bfloat16)
    tokens = group_gather(normed, size)
    early = 0 if w_joined.shape[0] // 2 % 128 else count - 3
    total = []
    if early:
        total = [
            pl.pallas_call(
                functools.partial(early_kernel, count, size),
                out_shape=jax.ShapeDtypeStruct((size * rows, columns), jnp.float32),
                in_specs=[VMEM] * (size + early),
                out_specs=VMEM,
                compiler_params=grant(16),
                cost_estimate=pl.CostEstimate(
                    flops=2 * size * rows * depth * columns, bytes_accessed=4 * depth * columns, transcendentals=0
                ),
                name="project_early",
            )(*tokens, *blocks[:early])
        ]
    *projs, own_expand = pl.pallas_call(
        functools.partial(proj_kernel, count, size, early),
        out_shape=[jax.ShapeDtypeStruct((rows, columns), jnp.bfloat16)] * size
        + [jax.ShapeDtypeStruct((rank, own_columns), jnp.bfloat16)],
        in_specs=[VMEM] * (size + count + 1 + len(total)),
        out_specs=[VMEM] * (size + 1),
        scratch_shapes=[] if early else [pltpu.VMEM((depth, columns), jnp.bfloat16)],
        compiler_params=grant(16),
        cost_estimate=pl.CostEstimate(
            flops=2 * size * rows * depth * columns, bytes_accessed=4 * depth * columns, transcendentals=0
        ),
        name="project",
    )(*tokens, *blocks, *total)

    back = [projs[0]]
    for k in range(1, size):
        back.append(lax.ppermute(projs[k], "group", [(i, i ^ k) for i in range(size)]))
    query, block = pl.pallas_call(
        functools.partial(assemble_kernel, size),
        out_shape=[
            jax.ShapeDtypeStruct((rows, QCOLS), jnp.bfloat16),
            jax.ShapeDtypeStruct((rows + 16, rank), jnp.bfloat16),
        ],
        in_specs=[VMEM] * (size + 1),
        out_specs=[VMEM, VMEM],
        scratch_shapes=[pltpu.VMEM((size, rows, columns), jnp.bfloat16)],
        compiler_params=grant(16),
        name="assemble",
    )(slots.reshape(1, rows), *back)
    lat_blocks = ring_gather(block, count)
    own_expand, _ = lax.optimization_barrier((own_expand, lat_blocks[1:3]))
    expands = group_gather(own_expand, size, lat_blocks[-4:-2])

    total = count * rows
    return pl.pallas_call(
        functools.partial(attend_kernel, count, size),
        out_shape=jax.ShapeDtypeStruct((rows, QCOLS), jnp.bfloat16),
        in_specs=[SMEM] + [VMEM] * (2 + count + size),
        out_specs=VMEM,
        scratch_shapes=[
            pltpu.VMEM((total, rank), jnp.bfloat16),
            pltpu.VMEM((rank, 2 * QCOLS), jnp.bfloat16),
            pltpu.VMEM((rows, total), jnp.float32),
            pltpu.VMEM((HEADS * rows, total), jnp.float32),
            pltpu.VMEM((HEADS * rows, total), jnp.bfloat16),
            pltpu.VMEM((HEADS * rows, 1), jnp.float32),
        ],
        compiler_params=grant(8 + total * HEADS * rows * 8 // (1024 * 1024)),
        cost_estimate=pl.CostEstimate(
            flops=4 * total * rank * QCOLS + 4 * rows * total * QCOLS,
            bytes_accessed=2 * (total + 2 * QCOLS) * rank,
            transcendentals=HEADS * rows * total,
        ),
        name="attend",
    )(lengths, query, *lat_blocks, *expands)


def solution(mesh):
    in_specs = (
        P(("group", "mp"), None),
        P(("group", "mp")),
        P("group", None),
        P("mp", "group"),
        P("mp", "group"),
    )
    out_specs = P(("group", "mp"), None)
    return jax.shard_map(body, mesh=mesh, in_specs=in_specs, out_specs=out_specs, check_vma=False)
```

```python
import functools

import jax
import jax.numpy as jnp
from jax import lax
from jax.experimental import pallas as pl
from jax.experimental.pallas import tpu as pltpu
from jax.sharding import PartitionSpec as P

HEADS = 8
HDIM = 128
QCOLS = HEADS * HDIM

EPS = 1e-06
NEGATIVE = -1e30
LOG2_E = 1.4426950408889634
VMEM = pl.BlockSpec(memory_space=pltpu.VMEM)
SMEM = pl.BlockSpec(memory_space=pltpu.SMEM)
HBM = pl.BlockSpec(memory_space=pltpu.HBM)


def grant(mib):
    return pltpu.CompilerParams(vmem_limit_bytes=mib * 1024 * 1024)


def row_norm(values):
    mean_sq = jnp.mean(values * values, axis=-1, keepdims=True)
    return values * lax.rsqrt(mean_sq + EPS)


def ring_pairs(count, step):
    order = [2 * r if r < count // 2 else 2 * (count - 1 - r) + 1 for r in range(count)]
    return [(order[r], order[(r + step) % count]) for r in range(count)]


def ring_gather(first, second, count):
    up, down = ring_pairs(count, 1), ring_pairs(count, -1)
    chains, states = [[first], [second]], [(first, first), (second, second)]
    for _ in range((count - 1) // 2):
        for i, (below, above) in enumerate(states):
            states[i] = lax.ppermute(below, "mp", up), lax.ppermute(above, "mp", down)
            chains[i] += states[i]
    chains[0].append(lax.ppermute(states[0][0], "mp", up))
    chains[1].append(lax.ppermute(states[1][1], "mp", down))
    return chains


def ring_owners(count):
    me = lax.axis_index("mp")
    place = jnp.where(me % 2 == 0, me // 2, count - 1 - me // 2)
    owners = [me]
    for step in range(1, count // 2 + 1):
        for shift in (-step, step):
            at = lax.rem(place + shift + count, count)
            owners.append(jnp.where(at < count // 2, 2 * at, 2 * (count - 1 - at) + 1))
    return owners[:count]


def group_gather(block, size, after=None):
    blocks = {0: block}
    bit = size // 2
    while bit:
        pairs = [(i, i ^ bit) for i in range(size)]
        for k in list(blocks):
            sent = blocks[k]
            if k and after is not None:
                sent, _ = lax.optimization_barrier((sent, after))
            blocks[k ^ bit] = lax.ppermute(sent, "group", pairs)
        bit //= 2
    return [blocks[k] for k in range(size)]


def pack_kernel(*refs):
    sources, targets, refs = refs[:4], refs[4:8], refs[8:]
    (joined, expand, arrivals, slots), (first, second, normed, digits), sems = refs[:4], refs[4:8], refs[8]
    reads = [pltpu.make_async_copy(a, b, sems.at[i]) for i, (a, b) in enumerate(zip(sources, refs[:4]))]
    writes = [pltpu.make_async_copy(a, b, sems.at[4 + i]) for i, (a, b) in enumerate(zip(refs[4:8], targets))]
    for read in reads:
        read.start()
    half, (high, columns) = first.shape[0], (expand.shape[0], joined.shape[1])
    folds = joined.shape[0] // high
    fold = expand.shape[1] // folds
    reads[0].wait()
    first[:, :columns] = joined[:half].astype(jnp.bfloat16)
    second[:, :columns] = joined[half:].astype(jnp.bfloat16)
    reads[1].wait()
    for i in range(folds):
        part = expand[:, i * fold : (i + 1) * fold].astype(jnp.bfloat16)
        chunk, at = (first, i * high) if i * high < half else (second, i * high - half)
        chunk[at : at + high, columns:] = part
    writes[0].start()
    writes[1].start()
    reads[2].wait()
    normed[...] = row_norm(arrivals[...].astype(jnp.float32)).astype(jnp.bfloat16)
    writes[2].start()
    reads[3].wait()
    rows = slots.shape[1]
    bits = jnp.concatenate([slots[...] & 255, slots[...] >> 8], axis=0).astype(jnp.float32)
    bits = jnp.concatenate([bits, jnp.zeros((14, rows), jnp.float32)], axis=0)
    digits[...] = jnp.zeros_like(digits)
    digits[:, :rows] = bits.astype(jnp.bfloat16)
    writes[3].start()
    for write in writes:
        write.wait()


def multiply(tokens, starts, blocks, columns):
    total = None
    for start, block in zip(starts, blocks):
        span = pl.ds(pl.multiple_of(start, 128), block.shape[0])
        left = jnp.concatenate([token[:, span] for token in tokens], axis=0)
        product = jnp.dot(left, block[:, :columns], preferred_element_type=jnp.float32)
        total = product if total is None else total + product
    return total


def early_kernel(count, size, *refs):
    tokens, refs = refs[:size], refs[size:]
    chunks, total = refs[:-1], refs[-1]
    early, depth = len(chunks) // 2, chunks[0].shape[0]
    starts = [owner * 2 * depth + half * depth for half in (0, 1) for owner in ring_owners(count)[:early]]
    total[...] = multiply(tokens, starts, chunks, total.shape[1])


def proj_kernel(count, size, early, *refs):
    tokens, refs = refs[:size], refs[size:]
    chunks, refs = refs[: 2 * count], refs[2 * count :]
    depth = chunks[0].shape[0]
    owners = ring_owners(count)
    starts = [owner * 2 * depth + half * depth for half in (0, 1) for owner in owners]
    if early:
        total, refs = refs[0], refs[1:]
        outs, expand = refs[:size], refs[size]
        rows, columns = outs[0].shape
        late = [*range(early, count), *range(count + early, 2 * count)]
        proj = total[...] + multiply(tokens, [starts[i] for i in late], [chunks[i] for i in late], columns)
    else:
        outs, expand, weight = refs[:size], refs[size], refs[size + 1]
        rows, columns = outs[0].shape
        for start, chunk in zip(starts, chunks):
            weight[pl.ds(pl.multiple_of(start, depth), depth), :] = chunk[:, :columns]
        products = [jnp.dot(token[...], weight[...], preferred_element_type=jnp.float32) for token in tokens]
        proj = jnp.concatenate(products, axis=0)
    at = lax.axis_index("group") * columns + lax.broadcasted_iota(jnp.int32, (1, columns), 1)
    proj = proj * jnp.where(at < QCOLS, HDIM**-0.5, 1.0).astype(jnp.float32)
    for i, out in enumerate(outs):
        out[...] = proj[i * rows : (i + 1) * rows].astype(jnp.bfloat16)
    high = expand.shape[0] // count
    for i, owner in enumerate(owners):
        parts = []
        for chunk in (chunks[i], chunks[count + i]):
            parts += [chunk[j * high : (j + 1) * high, columns:] for j in range(depth // high)]
        expand[pl.ds(pl.multiple_of(owner * high, high), high), :] = jnp.concatenate(parts, axis=1)


def assemble_kernel(size, digits, *refs):
    products, (query, first, second, proj) = refs[:size], refs[size:]
    group = lax.axis_index("group")
    for i, product in enumerate(products):
        proj[group ^ i] = product[...]
    whole = jnp.concatenate([proj[i] for i in range(size)], axis=1)
    query[...] = whole[:, :QCOLS]
    latent = row_norm(whole[:, QCOLS:].astype(jnp.float32)).astype(jnp.bfloat16)
    cut, left = first.shape[0], latent.shape[0] - first.shape[0]
    first[...] = latent[:cut]
    second[:left] = latent[cut:]
    second[left:] = digits[...]


def attend_kernel(count, size, lengths, query, *refs):
    chunks, refs = refs[: 2 * count], refs[2 * count :]
    expands, refs = refs[:size], refs[size:]
    out, latent, expand, bias, scores, probs, totals = refs
    rows, rank = query.shape[0], latent.shape[1]
    places = []
    for i in range(count):
        first, second = chunks[i], chunks[count + i]
        cut = first.shape[0]
        latent[i * rows : i * rows + cut, :] = first[...]
        latent[i * rows + cut : (i + 1) * rows, :] = second[: rows - cut]
        digits = second[rows - cut :, :rows].astype(jnp.float32)
        places.append(digits[1:2] * 256.0 + digits[:1])
    others = jnp.concatenate(places, axis=1).astype(jnp.int32)
    width = expands[0].shape[1]
    for i, block in enumerate(expands):
        at = (lax.axis_index("group") ^ i) * width
        expand[:, pl.ds(pl.multiple_of(at, width), width)] = block[...]
    same = lax.broadcasted_iota(jnp.int32, (rows, rows), 0) == lax.broadcasted_iota(jnp.int32, (rows, rows), 1)
    position = jnp.sum(jnp.where(same, places[0], 0.0), axis=1, keepdims=True).astype(jnp.int32)
    start = jnp.zeros_like(position)
    end = 0
    for i in range(lengths.shape[1]):
        end = end + lengths[0, i]
        start = jnp.where(position >= end, end, start)
    allowed = (others <= position) & (others >= start)
    bias[...] = jnp.where(allowed, 0.0, NEGATIVE)
    some, tile = HEADS // 2, 16
    for first in range(0, HEADS, some):
        turned = [
            lax.dot_general(
                query[:, head * HDIM : (head + 1) * HDIM],
                expand[:, head * 2 * HDIM : (2 * head + 1) * HDIM],
                (((1,), (1,)), ((), ())),
                preferred_element_type=jnp.float32,
            )
            for head in range(first, first + some)
        ]
        turned = (jnp.concatenate(turned, axis=0) * LOG2_E).astype(jnp.bfloat16)
        scores[first * rows : (first + some) * rows] = lax.dot_general(
            turned, latent[...], (((1,), (1,)), ((), ())), preferred_element_type=jnp.float32
        )
    for first in range(0, HEADS, some):
        for at in range(first * rows, (first + some) * rows, tile):
            part = scores[at : at + tile] + bias[at % rows : at % rows + tile]
            weights = jnp.exp2(part - jnp.max(part, axis=-1, keepdims=True))
            totals[at : at + tile] = jnp.sum(weights, axis=-1, keepdims=True)
            probs[at : at + tile] = weights.astype(jnp.bfloat16)
        summed = jnp.dot(
            probs[first * rows : (first + some) * rows], latent[...], preferred_element_type=jnp.float32
        ).astype(jnp.bfloat16)
        for i in range(some):
            head = first + i
            value = expand[:, (2 * head + 1) * HDIM : (2 * head + 2) * HDIM]
            outcome = jnp.dot(summed[i * rows : (i + 1) * rows], value, preferred_element_type=jnp.float32)
            total = totals[head * rows : (head + 1) * rows]
            out[:, head * HDIM : (head + 1) * HDIM] = (outcome / total).astype(jnp.bfloat16)


def body(arrivals, slots, lengths, w_joined, w_expand):
    count, size = lax.axis_size("mp"), lax.axis_size("group")
    rows, depth = arrivals.shape
    columns, rank = w_joined.shape[1], w_expand.shape[0] * count
    own_columns = w_expand.shape[1]

    packed = columns + own_columns * w_expand.shape[0] // w_joined.shape[0]
    chunk = jax.ShapeDtypeStruct((w_joined.shape[0] // 2, packed), jnp.bfloat16)
    sources = (w_joined, w_expand, arrivals, slots.reshape(1, rows))
    made = [
        chunk,
        chunk,
        jax.ShapeDtypeStruct((rows, depth), jnp.bfloat16),
        jax.ShapeDtypeStruct((16, rank), jnp.bfloat16),
    ]
    first, second, normed, digits = pl.pallas_call(
        pack_kernel,
        out_shape=made,
        in_specs=[HBM] * 4,
        out_specs=[HBM] * 4,
        scratch_shapes=[pltpu.VMEM(array.shape, array.dtype) for array in (*sources, *made)]
        + [pltpu.SemaphoreType.DMA((8,))],
        compiler_params=grant(60),
        name="pack",
    )(*sources)
    firsts, seconds = ring_gather(first, second, count)
    tokens = group_gather(normed, size)
    early = 0 if chunk.shape[0] % 128 else count - 3
    total = []
    if early:
        total = [
            pl.pallas_call(
                functools.partial(early_kernel, count, size),
                out_shape=jax.ShapeDtypeStruct((size * rows, columns), jnp.float32),
                in_specs=[VMEM] * (size + 2 * early),
                out_specs=VMEM,
                compiler_params=grant(16),
                cost_estimate=pl.CostEstimate(
                    flops=2 * size * rows * depth * columns, bytes_accessed=4 * depth * columns, transcendentals=0
                ),
                name="project_early",
            )(*tokens, *firsts[:early], *seconds[:early])
        ]
    *projs, own_expand = pl.pallas_call(
        functools.partial(proj_kernel, count, size, early),
        out_shape=[jax.ShapeDtypeStruct((rows, columns), jnp.bfloat16)] * size
        + [jax.ShapeDtypeStruct((rank, own_columns), jnp.bfloat16)],
        in_specs=[VMEM] * (size + 2 * count + len(total)),
        out_specs=[VMEM] * (size + 1),
        scratch_shapes=[] if early else [pltpu.VMEM((depth, columns), jnp.bfloat16)],
        compiler_params=grant(16),
        cost_estimate=pl.CostEstimate(
            flops=2 * size * rows * depth * columns, bytes_accessed=4 * depth * columns, transcendentals=0
        ),
        name="project",
    )(*tokens, *firsts, *seconds, *total)

    back = [projs[0]]
    for k in range(1, size):
        back.append(lax.ppermute(projs[k], "group", [(i, i ^ k) for i in range(size)]))
    cut = -(-(rows + 16) // 32) * 16
    query, first, second = pl.pallas_call(
        functools.partial(assemble_kernel, size),
        out_shape=[
            jax.ShapeDtypeStruct((rows, QCOLS), jnp.bfloat16),
            jax.ShapeDtypeStruct((cut, rank), jnp.bfloat16),
            jax.ShapeDtypeStruct((rows + 16 - cut, rank), jnp.bfloat16),
        ],
        in_specs=[VMEM] * (size + 1),
        out_specs=[VMEM] * 3,
        scratch_shapes=[pltpu.VMEM((size, rows, columns), jnp.bfloat16)],
        compiler_params=grant(16),
        name="assemble",
    )(digits, *back)
    firsts, seconds = ring_gather(first, second, count)
    own_expand, _ = lax.optimization_barrier((own_expand, firsts[1]))
    expands = group_gather(own_expand, size, (firsts[-3:-1], seconds[-3:-1]))

    total = count * rows
    return pl.pallas_call(
        functools.partial(attend_kernel, count, size),
        out_shape=jax.ShapeDtypeStruct((rows, QCOLS), jnp.bfloat16),
        in_specs=[SMEM] + [VMEM] * (1 + 2 * count + size),
        out_specs=VMEM,
        scratch_shapes=[
            pltpu.VMEM((total, rank), jnp.bfloat16),
            pltpu.VMEM((rank, 2 * QCOLS), jnp.bfloat16),
            pltpu.VMEM((rows, total), jnp.float32),
            pltpu.VMEM((HEADS * rows, total), jnp.float32),
            pltpu.VMEM((HEADS * rows, total), jnp.bfloat16),
            pltpu.VMEM((HEADS * rows, 1), jnp.float32),
        ],
        compiler_params=grant(8 + total * HEADS * rows * 8 // (1024 * 1024)),
        cost_estimate=pl.CostEstimate(
            flops=4 * total * rank * QCOLS + 4 * rows * total * QCOLS,
            bytes_accessed=2 * (total + 2 * QCOLS) * rank,
            transcendentals=HEADS * rows * total,
        ),
        name="attend",
    )(lengths, query, *firsts, *seconds, *expands)


def solution(mesh):
    in_specs = (
        P(("group", "mp"), None),
        P(("group", "mp")),
        P("group", None),
        P("mp", "group"),
        P("mp", "group"),
    )
    out_specs = P(("group", "mp"), None)
    return jax.shard_map(body, mesh=mesh, in_specs=in_specs, out_specs=out_specs, check_vma=False)
```

```python
import functools

import jax
import jax.numpy as jnp
from jax import lax
from jax.experimental import pallas as pl
from jax.experimental.pallas import tpu as pltpu
from jax.sharding import PartitionSpec as P

HEADS = 8
HDIM = 128
QCOLS = HEADS * HDIM

EPS = 1e-06
NEGATIVE = -1e30
LOG2_E = 1.4426950408889634
VMEM = pl.BlockSpec(memory_space=pltpu.VMEM)
SMEM = pl.BlockSpec(memory_space=pltpu.SMEM)
HBM = pl.BlockSpec(memory_space=pltpu.HBM)


def grant(mib):
    return pltpu.CompilerParams(vmem_limit_bytes=mib * 1024 * 1024)


def row_norm(values):
    mean_sq = jnp.mean(values * values, axis=-1, keepdims=True)
    return values * lax.rsqrt(mean_sq + EPS)


def ring_pairs(count, step):
    order = [2 * r if r < count // 2 else 2 * (count - 1 - r) + 1 for r in range(count)]
    return [(order[r], order[(r + step) % count]) for r in range(count)]


def ring_gather(first, second, count):
    up, down = ring_pairs(count, 1), ring_pairs(count, -1)
    chains, states = [[first], [second]], [(first, first), (second, second)]
    for _ in range((count - 1) // 2):
        for i, (below, above) in enumerate(states):
            states[i] = lax.ppermute(below, "mp", up), lax.ppermute(above, "mp", down)
            chains[i] += states[i]
    chains[0].append(lax.ppermute(states[0][0], "mp", up))
    chains[1].append(lax.ppermute(states[1][1], "mp", down))
    return chains


def whole_ring_gather(block, cut, count):
    up, down = ring_pairs(count, 1), ring_pairs(count, -1)
    below = above = block
    blocks = [block]
    for _ in range((count - 1) // 2):
        below, above = lax.ppermute(below, "mp", up), lax.ppermute(above, "mp", down)
        blocks += [below, above]
    return blocks + [lax.ppermute(below[:cut], "mp", up), lax.ppermute(above[cut:], "mp", down)]


def ring_owners(count):
    me = lax.axis_index("mp")
    place = jnp.where(me % 2 == 0, me // 2, count - 1 - me // 2)
    owners = [me]
    for step in range(1, count // 2 + 1):
        for shift in (-step, step):
            at = lax.rem(place + shift + count, count)
            owners.append(jnp.where(at < count // 2, 2 * at, 2 * (count - 1 - at) + 1))
    return owners[:count]


def group_gather(block, size, after=None):
    blocks = {0: block}
    bit = size // 2
    while bit:
        pairs = [(i, i ^ bit) for i in range(size)]
        for k in list(blocks):
            sent = blocks[k]
            if k and after is not None:
                sent, _ = lax.optimization_barrier((sent, after))
            blocks[k ^ bit] = lax.ppermute(sent, "group", pairs)
        bit //= 2
    return [blocks[k] for k in range(size)]


def pack_kernel(*refs):
    sources, targets, refs = refs[:4], refs[4:8], refs[8:]
    (joined, expand, arrivals, slots), (first, second, normed, digits), sems = refs[:4], refs[4:8], refs[8]
    reads = [pltpu.make_async_copy(a, b, sems.at[i]) for i, (a, b) in enumerate(zip(sources, refs[:4]))]
    writes = [pltpu.make_async_copy(a, b, sems.at[4 + i]) for i, (a, b) in enumerate(zip(refs[4:8], targets))]
    for read in reads:
        read.start()
    half, (high, columns) = first.shape[0], (expand.shape[0], joined.shape[1])
    folds = joined.shape[0] // high
    fold = expand.shape[1] // folds
    reads[0].wait()
    first[:, :columns] = joined[:half].astype(jnp.bfloat16)
    second[:, :columns] = joined[half:].astype(jnp.bfloat16)
    reads[1].wait()
    for i in range(folds):
        part = expand[:, i * fold : (i + 1) * fold].astype(jnp.bfloat16)
        chunk, at = (first, i * high) if i * high < half else (second, i * high - half)
        chunk[at : at + high, columns:] = part
    writes[0].start()
    writes[1].start()
    reads[2].wait()
    normed[...] = row_norm(arrivals[...].astype(jnp.float32)).astype(jnp.bfloat16)
    writes[2].start()
    reads[3].wait()
    rows = slots.shape[1]
    bits = jnp.concatenate([slots[...] & 255, slots[...] >> 8], axis=0).astype(jnp.float32)
    bits = jnp.concatenate([bits, jnp.zeros((14, rows), jnp.float32)], axis=0)
    digits[...] = jnp.zeros_like(digits)
    digits[:, :rows] = bits.astype(jnp.bfloat16)
    writes[3].start()
    for write in writes:
        write.wait()


def multiply(tokens, starts, blocks, columns):
    total = None
    for start, block in zip(starts, blocks):
        span = pl.ds(pl.multiple_of(start, 128), block.shape[0])
        left = jnp.concatenate([token[:, span] for token in tokens], axis=0)
        product = jnp.dot(left, block[:, :columns], preferred_element_type=jnp.float32)
        total = product if total is None else total + product
    return total


def early_kernel(count, size, *refs):
    tokens, refs = refs[:size], refs[size:]
    chunks, total = refs[:-1], refs[-1]
    early, depth = len(chunks) // 2, chunks[0].shape[0]
    starts = [owner * 2 * depth + half * depth for half in (0, 1) for owner in ring_owners(count)[:early]]
    total[...] = multiply(tokens, starts, chunks, total.shape[1])


def proj_kernel(count, size, early, *refs):
    tokens, refs = refs[:size], refs[size:]
    chunks, refs = refs[: 2 * count], refs[2 * count :]
    depth = chunks[0].shape[0]
    owners = ring_owners(count)
    starts = [owner * 2 * depth + half * depth for half in (0, 1) for owner in owners]
    if early:
        total, refs = refs[0], refs[1:]
        outs, expand = refs[:size], refs[size]
        rows, columns = outs[0].shape
        late = [*range(early, count), *range(count + early, 2 * count)]
        proj = total[...] + multiply(tokens, [starts[i] for i in late], [chunks[i] for i in late], columns)
    else:
        outs, expand, weight = refs[:size], refs[size], refs[size + 1]
        rows, columns = outs[0].shape
        for start, chunk in zip(starts, chunks):
            weight[pl.ds(pl.multiple_of(start, depth), depth), :] = chunk[:, :columns]
        products = [jnp.dot(token[...], weight[...], preferred_element_type=jnp.float32) for token in tokens]
        proj = jnp.concatenate(products, axis=0)
    at = lax.axis_index("group") * columns + lax.broadcasted_iota(jnp.int32, (1, columns), 1)
    proj = proj * jnp.where(at < QCOLS, HDIM**-0.5, 1.0).astype(jnp.float32)
    for i, out in enumerate(outs):
        out[...] = proj[i * rows : (i + 1) * rows].astype(jnp.bfloat16)
    high = expand.shape[0] // count
    for i, owner in enumerate(owners):
        parts = []
        for chunk in (chunks[i], chunks[count + i]):
            parts += [chunk[j * high : (j + 1) * high, columns:] for j in range(depth // high)]
        expand[pl.ds(pl.multiple_of(owner * high, high), high), :] = jnp.concatenate(parts, axis=1)


def assemble_kernel(size, digits, *refs):
    products, (query, block, proj) = refs[:size], refs[size:]
    group = lax.axis_index("group")
    for i, product in enumerate(products):
        proj[group ^ i] = product[...]
    whole = jnp.concatenate([proj[i] for i in range(size)], axis=1)
    query[...] = whole[:, :QCOLS]
    rows = query.shape[0]
    block[:rows] = row_norm(whole[:, QCOLS:].astype(jnp.float32)).astype(jnp.bfloat16)
    block[rows:] = digits[...]


def attend_kernel(count, size, lengths, query, *refs):
    blocks, refs = refs[: count + 1], refs[count + 1 :]
    expands, refs = refs[:size], refs[size:]
    out, latent, expand, bias, scores, probs, totals = refs
    rows, rank = query.shape[0], latent.shape[1]
    places = []
    for i, block in enumerate(blocks):
        start = i * rows if i < count else (count - 1) * rows + blocks[-2].shape[0]
        length = min(rows, block.shape[0]) if i < count else rows - blocks[-2].shape[0]
        latent[start : start + length, :] = block[:length]
        if length < block.shape[0]:
            digits = block[length:, :rows].astype(jnp.float32)
            places.append(digits[1:2] * 256.0 + digits[:1])
    others = jnp.concatenate(places, axis=1).astype(jnp.int32)
    width = expands[0].shape[1]
    for i, block in enumerate(expands):
        at = (lax.axis_index("group") ^ i) * width
        expand[:, pl.ds(pl.multiple_of(at, width), width)] = block[...]
    same = lax.broadcasted_iota(jnp.int32, (rows, rows), 0) == lax.broadcasted_iota(jnp.int32, (rows, rows), 1)
    position = jnp.sum(jnp.where(same, places[0], 0.0), axis=1, keepdims=True).astype(jnp.int32)
    start = jnp.zeros_like(position)
    end = 0
    for i in range(lengths.shape[1]):
        end = end + lengths[0, i]
        start = jnp.where(position >= end, end, start)
    allowed = (others <= position) & (others >= start)
    bias[...] = jnp.where(allowed, 0.0, NEGATIVE)
    some, tile = HEADS // 2, 16
    for first in range(0, HEADS, some):
        turned = [
            lax.dot_general(
                query[:, head * HDIM : (head + 1) * HDIM],
                expand[:, head * 2 * HDIM : (2 * head + 1) * HDIM],
                (((1,), (1,)), ((), ())),
                preferred_element_type=jnp.float32,
            )
            for head in range(first, first + some)
        ]
        turned = (jnp.concatenate(turned, axis=0) * LOG2_E).astype(jnp.bfloat16)
        scores[first * rows : (first + some) * rows] = lax.dot_general(
            turned, latent[...], (((1,), (1,)), ((), ())), preferred_element_type=jnp.float32
        )
    for first in range(0, HEADS, some):
        for at in range(first * rows, (first + some) * rows, tile):
            part = scores[at : at + tile] + bias[at % rows : at % rows + tile]
            weights = jnp.exp2(part - jnp.max(part, axis=-1, keepdims=True))
            totals[at : at + tile] = jnp.sum(weights, axis=-1, keepdims=True)
            probs[at : at + tile] = weights.astype(jnp.bfloat16)
        summed = jnp.dot(
            probs[first * rows : (first + some) * rows], latent[...], preferred_element_type=jnp.float32
        ).astype(jnp.bfloat16)
        for i in range(some):
            head = first + i
            value = expand[:, (2 * head + 1) * HDIM : (2 * head + 2) * HDIM]
            outcome = jnp.dot(summed[i * rows : (i + 1) * rows], value, preferred_element_type=jnp.float32)
            total = totals[head * rows : (head + 1) * rows]
            out[:, head * HDIM : (head + 1) * HDIM] = (outcome / total).astype(jnp.bfloat16)


def body(arrivals, slots, lengths, w_joined, w_expand):
    count, size = lax.axis_size("mp"), lax.axis_size("group")
    rows, depth = arrivals.shape
    columns, rank = w_joined.shape[1], w_expand.shape[0] * count
    own_columns = w_expand.shape[1]

    packed = columns + own_columns * w_expand.shape[0] // w_joined.shape[0]
    chunk = jax.ShapeDtypeStruct((w_joined.shape[0] // 2, packed), jnp.bfloat16)
    sources = (w_joined, w_expand, arrivals, slots.reshape(1, rows))
    made = [
        chunk,
        chunk,
        jax.ShapeDtypeStruct((rows, depth), jnp.bfloat16),
        jax.ShapeDtypeStruct((16, rank), jnp.bfloat16),
    ]
    first, second, normed, digits = pl.pallas_call(
        pack_kernel,
        out_shape=made,
        in_specs=[HBM] * 4,
        out_specs=[HBM] * 4,
        scratch_shapes=[pltpu.VMEM(array.shape, array.dtype) for array in (*sources, *made)]
        + [pltpu.SemaphoreType.DMA((8,))],
        compiler_params=grant(60),
        name="pack",
    )(*sources)
    firsts, seconds = ring_gather(first, second, count)
    tokens = group_gather(normed, size, (firsts[3:5], seconds[3:5]))
    early = 0 if chunk.shape[0] % 128 else count - 3
    total = []
    if early:
        total = [
            pl.pallas_call(
                functools.partial(early_kernel, count, size),
                out_shape=jax.ShapeDtypeStruct((size * rows, columns), jnp.float32),
                in_specs=[VMEM] * (size + 2 * early),
                out_specs=VMEM,
                compiler_params=grant(16),
                cost_estimate=pl.CostEstimate(
                    flops=2 * size * rows * depth * columns, bytes_accessed=4 * depth * columns, transcendentals=0
                ),
                name="project_early",
            )(*tokens, *firsts[:early], *seconds[:early])
        ]
    *projs, own_expand = pl.pallas_call(
        functools.partial(proj_kernel, count, size, early),
        out_shape=[jax.ShapeDtypeStruct((rows, columns), jnp.bfloat16)] * size
        + [jax.ShapeDtypeStruct((rank, own_columns), jnp.bfloat16)],
        in_specs=[VMEM] * (size + 2 * count + len(total)),
        out_specs=[VMEM] * (size + 1),
        scratch_shapes=[] if early else [pltpu.VMEM((depth, columns), jnp.bfloat16)],
        compiler_params=grant(16),
        cost_estimate=pl.CostEstimate(
            flops=2 * size * rows * depth * columns, bytes_accessed=4 * depth * columns, transcendentals=0
        ),
        name="project",
    )(*tokens, *firsts, *seconds, *total)

    back = [projs[0]]
    for k in range(1, size):
        back.append(lax.ppermute(projs[k], "group", [(i, i ^ k) for i in range(size)]))
    query, block = pl.pallas_call(
        functools.partial(assemble_kernel, size),
        out_shape=[
            jax.ShapeDtypeStruct((rows, QCOLS), jnp.bfloat16),
            jax.ShapeDtypeStruct((rows + 16, rank), jnp.bfloat16),
        ],
        in_specs=[VMEM] * (size + 1),
        out_specs=[VMEM] * 2,
        scratch_shapes=[pltpu.VMEM((size, rows, columns), jnp.bfloat16)],
        compiler_params=grant(16),
        name="assemble",
    )(digits, *back)
    blocks = whole_ring_gather(block, -(-(rows + 16) // 32) * 16, count)
    own_expand, _ = lax.optimization_barrier((own_expand, blocks[1:3]))
    expands = group_gather(own_expand, size, blocks[-4:-2])

    total = count * rows
    return pl.pallas_call(
        functools.partial(attend_kernel, count, size),
        out_shape=jax.ShapeDtypeStruct((rows, QCOLS), jnp.bfloat16),
        in_specs=[SMEM] + [VMEM] * (2 + count + size),
        out_specs=VMEM,
        scratch_shapes=[
            pltpu.VMEM((total, rank), jnp.bfloat16),
            pltpu.VMEM((rank, 2 * QCOLS), jnp.bfloat16),
            pltpu.VMEM((rows, total), jnp.float32),
            pltpu.VMEM((HEADS * rows, total), jnp.float32),
            pltpu.VMEM((HEADS * rows, total), jnp.bfloat16),
            pltpu.VMEM((HEADS * rows, 1), jnp.float32),
        ],
        compiler_params=grant(8 + total * HEADS * rows * 8 // (1024 * 1024)),
        cost_estimate=pl.CostEstimate(
            flops=4 * total * rank * QCOLS + 4 * rows * total * QCOLS,
            bytes_accessed=2 * (total + 2 * QCOLS) * rank,
            transcendentals=HEADS * rows * total,
        ),
        name="attend",
    )(lengths, query, *blocks, *expands)


def solution(mesh):
    in_specs = (
        P(("group", "mp"), None),
        P(("group", "mp")),
        P("group", None),
        P("mp", "group"),
        P("mp", "group"),
    )
    out_specs = P(("group", "mp"), None)
    return jax.shard_map(body, mesh=mesh, in_specs=in_specs, out_specs=out_specs, check_vma=False)
```

```python
import functools

import jax
import jax.numpy as jnp
from jax import lax
from jax.experimental import pallas as pl
from jax.experimental.pallas import tpu as pltpu
from jax.sharding import PartitionSpec as P

HEADS = 8
HDIM = 128
QCOLS = HEADS * HDIM

EPS = 1e-06
NEGATIVE = -1e30
LOG2_E = 1.4426950408889634
TILE = 16
VMEM = pl.BlockSpec(memory_space=pltpu.VMEM)
SMEM = pl.BlockSpec(memory_space=pltpu.SMEM)


def grant(mib):
    return pltpu.CompilerParams(vmem_limit_bytes=mib * 1024 * 1024)


def row_norm(values):
    mean_sq = jnp.mean(values * values, axis=-1, keepdims=True)
    return values * lax.rsqrt(mean_sq + EPS)


def ring_pairs(count, step):
    order = [2 * r if r < count // 2 else 2 * (count - 1 - r) + 1 for r in range(count)]
    return [(order[r], order[(r + step) % count]) for r in range(count)]


def ring_gather(block, count):
    up, down = ring_pairs(count, 1), ring_pairs(count, -1)
    below = above = block
    blocks = [block]
    for _ in range((count - 1) // 2):
        below, above = lax.ppermute(below, "mp", up), lax.ppermute(above, "mp", down)
        blocks += [below, above]
    cut = -(-block.shape[0] // 32) * 16
    return blocks + [lax.ppermute(below[:cut], "mp", up), lax.ppermute(above[cut:], "mp", down)]


def ring_owners(count):
    me = lax.axis_index("mp")
    place = jnp.where(me % 2 == 0, me // 2, count - 1 - me // 2)
    owners = [me]
    for step in range(1, count // 2 + 1):
        for shift in (-step, step):
            at = lax.rem(place + shift + count, count)
            owners.append(jnp.where(at < count // 2, 2 * at, 2 * (count - 1 - at) + 1))
    return owners[:count]


def row_ranges(blocks):
    last = len(blocks) - 2
    return [(i, 0) for i in range(last + 1)] + [(last, blocks[last].shape[0])]


def group_gather(block, size, after=None):
    blocks = {0: block}
    bit = size // 2
    while bit:
        pairs = [(i, i ^ bit) for i in range(size)]
        for k in list(blocks):
            sent = blocks[k]
            if k and after is not None:
                sent, _ = lax.optimization_barrier((sent, after))
            blocks[k ^ bit] = lax.ppermute(sent, "group", pairs)
        bit //= 2
    return [blocks[k] for k in range(size)]


def pack_kernel(joined, expand, out):
    columns, high = joined.shape[1], expand.shape[0]
    folds = joined.shape[0] // high
    fold = expand.shape[1] // folds
    out[:, :columns] = joined[...].astype(jnp.bfloat16)
    for i in range(folds):
        out[i * high : (i + 1) * high, columns:] = expand[:, i * fold : (i + 1) * fold].astype(jnp.bfloat16)


def multiply(tokens, starts, blocks, columns):
    total = None
    for start, block in zip(starts, blocks):
        span = pl.ds(pl.multiple_of(start, 128), block.shape[0])
        left = jnp.concatenate([token[:, span] for token in tokens], axis=0)
        product = jnp.dot(left, block[:, :columns], preferred_element_type=jnp.float32)
        total = product if total is None else total + product
    return total


def early_kernel(count, size, *refs):
    tokens, blocks, total = refs[:size], refs[size:-1], refs[-1]
    depth = blocks[0].shape[0]
    total[...] = multiply(tokens, [owner * depth for owner in ring_owners(count)], blocks, total.shape[1])


def proj_kernel(count, size, early, *refs):
    tokens, refs = refs[:size], refs[size:]
    blocks, refs = refs[: count + 1], refs[count + 1 :]
    depth = blocks[0].shape[0]
    owners = ring_owners(count)
    starts = [owners[i] * depth + offset for i, offset in row_ranges(blocks)]
    if early:
        total, refs = refs[0], refs[1:]
        outs, expand = refs[:size], refs[size]
        rows, columns = outs[0].shape
        proj = total[...] + multiply(tokens, starts[early:], blocks[early:], columns)
    else:
        outs, expand, weight = refs[:size], refs[size], refs[size + 1]
        rows, columns = outs[0].shape
        for start, block in zip(starts, blocks):
            length = block.shape[0]
            weight[pl.ds(pl.multiple_of(start, length), length), :] = block[:, :columns]
        products = [jnp.dot(token[...], weight[...], preferred_element_type=jnp.float32) for token in tokens]
        proj = jnp.concatenate(products, axis=0)
    at = lax.axis_index("group") * columns + lax.broadcasted_iota(jnp.int32, (1, columns), 1)
    proj = proj * jnp.where(at < QCOLS, HDIM**-0.5, 1.0).astype(jnp.float32)
    for i, out in enumerate(outs):
        out[...] = proj[i * rows : (i + 1) * rows].astype(jnp.bfloat16)
    high = expand.shape[0] // count
    for i, owner in enumerate(owners):
        parts = []
        for block in blocks[i:] if i == count - 1 else blocks[i : i + 1]:
            parts += [block[j * high : (j + 1) * high, columns:] for j in range(block.shape[0] // high)]
        expand[pl.ds(pl.multiple_of(owner * high, high), high), :] = jnp.concatenate(parts, axis=1)


def assemble_kernel(size, digits, *refs):
    products, (query, block, proj) = refs[:size], refs[size:]
    group = lax.axis_index("group")
    for i, product in enumerate(products):
        proj[group ^ i] = product[...]
    whole = jnp.concatenate([proj[i] for i in range(size)], axis=1)
    query[...] = whole[:, :QCOLS]
    rows = query.shape[0]
    block[:rows] = row_norm(whole[:, QCOLS:].astype(jnp.float32)).astype(jnp.bfloat16)
    block[rows:] = digits[...]


def position_of(block, rows):
    digits = block[block.shape[0] - 16 :, :rows].astype(jnp.float32)
    return digits[1:2] * 256.0 + digits[:1]


def bias_of(lengths, own, others):
    rows = own.shape[0] - 16
    same = lax.broadcasted_iota(jnp.int32, (rows, rows), 0) == lax.broadcasted_iota(jnp.int32, (rows, rows), 1)
    position = jnp.sum(jnp.where(same, position_of(own, rows), 0.0), axis=1, keepdims=True).astype(jnp.int32)
    start = jnp.zeros_like(position)
    end = 0
    for i in range(lengths.shape[1]):
        end = end + lengths[0, i]
        start = jnp.where(position >= end, end, start)
    others = others.astype(jnp.int32)
    return jnp.where((others <= position) & (others >= start), 0.0, NEGATIVE)


def score(turned, latent, scores):
    half = turned.shape[0] // 2
    for at in (0, half):
        scores[at : at + half] = lax.dot_general(
            turned[at : at + half], latent[...], (((1,), (1,)), ((), ())), preferred_element_type=jnp.float32
        )


def score_kernel(count, size, lengths, query, *refs):
    blocks, refs = refs[: count - 1], refs[count - 1 :]
    expands, refs = refs[:size], refs[size:]
    turned, value, latent, bias, scores, expand = refs
    rows = query.shape[0]
    for i, block in enumerate(blocks):
        latent[i * rows : (i + 1) * rows, :] = block[:rows]
    bias[...] = bias_of(lengths, blocks[0], jnp.concatenate([position_of(block, rows) for block in blocks], axis=1))
    width = expands[0].shape[1]
    for i, block in enumerate(expands):
        at = (lax.axis_index("group") ^ i) * width
        expand[:, pl.ds(pl.multiple_of(at, width), width)] = block[...]
    for head in range(HEADS):
        value[:, head * HDIM : (head + 1) * HDIM] = expand[:, (2 * head + 1) * HDIM : (2 * head + 2) * HDIM]
        product = lax.dot_general(
            query[:, head * HDIM : (head + 1) * HDIM],
            expand[:, head * 2 * HDIM : (2 * head + 1) * HDIM],
            (((1,), (1,)), ((), ())),
            preferred_element_type=jnp.float32,
        )
        turned[head * rows : (head + 1) * rows] = (product * LOG2_E).astype(jnp.bfloat16)
    score(turned, latent, scores)


def attend_kernel(lengths, own, turned, value, latent, bias, scores, first, second, out, last, last_scores, probs, totals):
    rows, seen = out.shape[0], latent.shape[0]
    cut = first.shape[0]
    last[:cut] = first[...]
    last[cut:] = second[: rows - cut]
    last_bias = bias_of(lengths, own, position_of(second, rows))
    score(turned, last, last_scores)
    half = HEADS * rows // 2
    for begin in (0, half):
        for at in range(begin, begin + half, TILE):
            here = at % rows
            part = scores[at : at + TILE] + bias[here : here + TILE]
            last_part = last_scores[at : at + TILE] + last_bias[here : here + TILE]
            peak = jnp.maximum(
                jnp.max(part, axis=-1, keepdims=True), jnp.max(last_part, axis=-1, keepdims=True)
            )
            weights, last_weights = jnp.exp2(part - peak), jnp.exp2(last_part - peak)
            totals[at : at + TILE] = jnp.sum(weights, axis=-1, keepdims=True) + jnp.sum(
                last_weights, axis=-1, keepdims=True
            )
            probs[at : at + TILE, :seen] = weights.astype(jnp.bfloat16)
            probs[at : at + TILE, seen:] = last_weights.astype(jnp.bfloat16)
        summed = jnp.dot(
            probs[begin : begin + half, :seen], latent[...], preferred_element_type=jnp.float32
        ) + jnp.dot(probs[begin : begin + half, seen:], last[...], preferred_element_type=jnp.float32)
        summed = summed.astype(jnp.bfloat16)
        for i in range(HEADS // 2):
            head = begin // rows + i
            columns = slice(head * HDIM, (head + 1) * HDIM)
            outcome = jnp.dot(summed[i * rows : (i + 1) * rows], value[:, columns], preferred_element_type=jnp.float32)
            out[:, columns] = (outcome / totals[head * rows : (head + 1) * rows]).astype(jnp.bfloat16)


def body(arrivals, slots, lengths, w_joined, w_expand):
    count, size = lax.axis_size("mp"), lax.axis_size("group")
    rows, depth = arrivals.shape
    columns, rank = w_joined.shape[1], w_expand.shape[0] * count
    own_columns = w_expand.shape[1]

    weights = pl.pallas_call(
        pack_kernel,
        out_shape=jax.ShapeDtypeStruct(
            (w_joined.shape[0], columns + own_columns * w_expand.shape[0] // w_joined.shape[0]), jnp.bfloat16
        ),
        in_specs=[VMEM, VMEM],
        out_specs=VMEM,
        compiler_params=grant(16),
        name="pack",
    )(w_joined, w_expand)
    blocks = ring_gather(weights, count)
    normed = row_norm(arrivals.astype(jnp.float32)).astype(jnp.bfloat16)
    digits = jnp.pad(jnp.stack([slots & 255, slots >> 8]), ((0, 14), (0, rank - rows))).astype(jnp.bfloat16)
    normed, digits, _ = lax.optimization_barrier((normed, digits, blocks[1:3]))
    tokens = group_gather(normed, size, blocks[-4:-2])
    early = 0 if w_joined.shape[0] // 2 % 128 else count - 3
    total = []
    if early:
        total = [
            pl.pallas_call(
                functools.partial(early_kernel, count, size),
                out_shape=jax.ShapeDtypeStruct((size * rows, columns), jnp.float32),
                in_specs=[VMEM] * (size + early),
                out_specs=VMEM,
                compiler_params=grant(16),
                cost_estimate=pl.CostEstimate(
                    flops=2 * size * rows * depth * columns, bytes_accessed=4 * depth * columns, transcendentals=0
                ),
                name="project_early",
            )(*tokens, *blocks[:early])
        ]
    *projs, own_expand = pl.pallas_call(
        functools.partial(proj_kernel, count, size, early),
        out_shape=[jax.ShapeDtypeStruct((rows, columns), jnp.bfloat16)] * size
        + [jax.ShapeDtypeStruct((rank, own_columns), jnp.bfloat16)],
        in_specs=[VMEM] * (size + count + 1 + len(total)),
        out_specs=[VMEM] * (size + 1),
        scratch_shapes=[] if early else [pltpu.VMEM((depth, columns), jnp.bfloat16)],
        compiler_params=grant(16),
        cost_estimate=pl.CostEstimate(
            flops=2 * size * rows * depth * columns, bytes_accessed=4 * depth * columns, transcendentals=0
        ),
        name="project",
    )(*tokens, *blocks, *total)

    back = [projs[0]]
    for k in range(1, size):
        back.append(lax.ppermute(projs[k], "group", [(i, i ^ k) for i in range(size)]))
    query, block = pl.pallas_call(
        functools.partial(assemble_kernel, size),
        out_shape=[
            jax.ShapeDtypeStruct((rows, QCOLS), jnp.bfloat16),
            jax.ShapeDtypeStruct((rows + 16, rank), jnp.bfloat16),
        ],
        in_specs=[VMEM] * (size + 1),
        out_specs=[VMEM, VMEM],
        scratch_shapes=[pltpu.VMEM((size, rows, columns), jnp.bfloat16)],
        compiler_params=grant(16),
        name="assemble",
    )(digits, *back)
    lat_blocks = ring_gather(block, count)
    own_expand, _ = lax.optimization_barrier((own_expand, lat_blocks[1:3]))
    expands = group_gather(own_expand, size, lat_blocks[-4:-2])

    total, seen = count * rows, (count - 1) * rows
    needed = grant(8 + total * HEADS * rows * 8 // (1024 * 1024))
    made = pl.pallas_call(
        functools.partial(score_kernel, count, size),
        out_shape=[
            jax.ShapeDtypeStruct((HEADS * rows, rank), jnp.bfloat16),
            jax.ShapeDtypeStruct((rank, QCOLS), jnp.bfloat16),
            jax.ShapeDtypeStruct((seen, rank), jnp.bfloat16),
            jax.ShapeDtypeStruct((rows, seen), jnp.float32),
            jax.ShapeDtypeStruct((HEADS * rows, seen), jnp.float32),
        ],
        in_specs=[SMEM] + [VMEM] * (count + size),
        out_specs=[VMEM] * 5,
        scratch_shapes=[pltpu.VMEM((rank, 2 * QCOLS), jnp.bfloat16)],
        compiler_params=needed,
        cost_estimate=pl.CostEstimate(
            flops=2 * total * rank * QCOLS, bytes_accessed=8 * QCOLS * rank, transcendentals=0
        ),
        name="score",
    )(lengths, query, *lat_blocks[: count - 1], *expands)
    return pl.pallas_call(
        attend_kernel,
        out_shape=jax.ShapeDtypeStruct((rows, QCOLS), jnp.bfloat16),
        in_specs=[SMEM] + [VMEM] * 8,
        out_specs=VMEM,
        scratch_shapes=[
            pltpu.VMEM((rows, rank), jnp.bfloat16),
            pltpu.VMEM((HEADS * rows, rows), jnp.float32),
            pltpu.VMEM((HEADS * rows, total), jnp.bfloat16),
            pltpu.VMEM((HEADS * rows, 1), jnp.float32),
        ],
        compiler_params=needed,
        cost_estimate=pl.CostEstimate(
            flops=2 * total * rank * QCOLS, bytes_accessed=8 * QCOLS * rank, transcendentals=HEADS * rows * total
        ),
        name="attend",
    )(lengths, block, *made, *lat_blocks[count - 1 :])


def solution(mesh):
    in_specs = (
        P(("group", "mp"), None),
        P(("group", "mp")),
        P("group", None),
        P("mp", "group"),
        P("mp", "group"),
    )
    out_specs = P(("group", "mp"), None)
    return jax.shard_map(body, mesh=mesh, in_specs=in_specs, out_specs=out_specs, check_vma=False)
```

```python
import functools

import jax
import jax.numpy as jnp
from jax import lax
from jax.experimental import pallas as pl
from jax.experimental.pallas import tpu as pltpu
from jax.sharding import PartitionSpec as P

HEADS = 8
HDIM = 128
QCOLS = HEADS * HDIM

EPS = 1e-06
NEGATIVE = -1e30
LOG2_E = 1.4426950408889634
TILE = 16
NORM_COST = 64
VMEM = pl.BlockSpec(memory_space=pltpu.VMEM)
SMEM = pl.BlockSpec(memory_space=pltpu.SMEM)


def grant(mib):
    return pltpu.CompilerParams(vmem_limit_bytes=mib * 1024 * 1024)


def row_norm(values):
    mean_sq = jnp.mean(values * values, axis=-1, keepdims=True)
    return values * lax.rsqrt(mean_sq + EPS)


def ring_pairs(count, step):
    order = [2 * r if r < count // 2 else 2 * (count - 1 - r) + 1 for r in range(count)]
    return [(order[r], order[(r + step) % count]) for r in range(count)]


def ring_gather(block, count):
    up, down = ring_pairs(count, 1), ring_pairs(count, -1)
    below = above = block
    blocks = [block]
    for _ in range((count - 1) // 2):
        below, above = lax.ppermute(below, "mp", up), lax.ppermute(above, "mp", down)
        blocks += [below, above]
    cut = -(-block.shape[0] // 32) * 16
    return blocks + [lax.ppermute(below[:cut], "mp", up), lax.ppermute(above[cut:], "mp", down)]


def ring_owners(count):
    me = lax.axis_index("mp")
    place = jnp.where(me % 2 == 0, me // 2, count - 1 - me // 2)
    owners = [me]
    for step in range(1, count // 2 + 1):
        for shift in (-step, step):
            at = lax.rem(place + shift + count, count)
            owners.append(jnp.where(at < count // 2, 2 * at, 2 * (count - 1 - at) + 1))
    return owners[:count]


def row_ranges(blocks):
    last = len(blocks) - 2
    return [(i, 0) for i in range(last + 1)] + [(last, blocks[last].shape[0])]


def group_gather(block, size, after=None):
    blocks = {0: block}
    bit = size // 2
    while bit:
        pairs = [(i, i ^ bit) for i in range(size)]
        for k in list(blocks):
            sent = blocks[k]
            if k and after is not None:
                sent, _ = lax.optimization_barrier((sent, after))
            blocks[k ^ bit] = lax.ppermute(sent, "group", pairs)
        bit //= 2
    return [blocks[k] for k in range(size)]


def pack_kernel(joined, expand, out):
    columns, high = joined.shape[1], expand.shape[0]
    folds = joined.shape[0] // high
    fold = expand.shape[1] // folds
    out[:, :columns] = joined[...].astype(jnp.bfloat16)
    for i in range(folds):
        out[i * high : (i + 1) * high, columns:] = expand[:, i * fold : (i + 1) * fold].astype(jnp.bfloat16)


def norm_kernel(arrivals, slots, normed, digits):
    normed[...] = row_norm(arrivals[...].astype(jnp.float32)).astype(jnp.bfloat16)
    rows = slots.shape[1]
    bits = jnp.concatenate([slots[...] & 255, slots[...] >> 8], axis=0).astype(jnp.float32)
    bits = jnp.concatenate([bits, jnp.zeros((14, rows), jnp.float32)], axis=0)
    digits[...] = jnp.zeros_like(digits)
    digits[:, :rows] = bits.astype(jnp.bfloat16)


def multiply(tokens, starts, blocks, columns):
    total = None
    for start, block in zip(starts, blocks):
        span = pl.ds(pl.multiple_of(start, 128), block.shape[0])
        left = jnp.concatenate([token[:, span] for token in tokens], axis=0)
        product = jnp.dot(left, block[:, :columns], preferred_element_type=jnp.float32)
        total = product if total is None else total + product
    return total


def early_kernel(count, size, *refs):
    tokens, blocks, total = refs[:size], refs[size:-1], refs[-1]
    depth = blocks[0].shape[0]
    total[...] = multiply(tokens, [owner * depth for owner in ring_owners(count)], blocks, total.shape[1])


def proj_kernel(count, size, early, *refs):
    tokens, refs = refs[:size], refs[size:]
    blocks, refs = refs[: count + 1], refs[count + 1 :]
    depth = blocks[0].shape[0]
    owners = ring_owners(count)
    starts = [owners[i] * depth + offset for i, offset in row_ranges(blocks)]
    if early:
        total, refs = refs[0], refs[1:]
        outs, expand = refs[:size], refs[size]
        rows, columns = outs[0].shape
        proj = total[...] + multiply(tokens, starts[early:], blocks[early:], columns)
    else:
        outs, expand, weight = refs[:size], refs[size], refs[size + 1]
        rows, columns = outs[0].shape
        for start, block in zip(starts, blocks):
            length = block.shape[0]
            weight[pl.ds(pl.multiple_of(start, length), length), :] = block[:, :columns]
        products = [jnp.dot(token[...], weight[...], preferred_element_type=jnp.float32) for token in tokens]
        proj = jnp.concatenate(products, axis=0)
    at = lax.axis_index("group") * columns + lax.broadcasted_iota(jnp.int32, (1, columns), 1)
    proj = proj * jnp.where(at < QCOLS, HDIM**-0.5, 1.0).astype(jnp.float32)
    for i, out in enumerate(outs):
        out[...] = proj[i * rows : (i + 1) * rows].astype(jnp.bfloat16)
    high = expand.shape[0] // count
    for i, owner in enumerate(owners):
        parts = []
        for block in blocks[i:] if i == count - 1 else blocks[i : i + 1]:
            parts += [block[j * high : (j + 1) * high, columns:] for j in range(block.shape[0] // high)]
        expand[pl.ds(pl.multiple_of(owner * high, high), high), :] = jnp.concatenate(parts, axis=1)


def assemble_kernel(size, digits, *refs):
    products, (query, block, proj) = refs[:size], refs[size:]
    group = lax.axis_index("group")
    for i, product in enumerate(products):
        proj[group ^ i] = product[...]
    whole = jnp.concatenate([proj[i] for i in range(size)], axis=1)
    query[...] = whole[:, :QCOLS]
    rows = query.shape[0]
    block[:rows] = row_norm(whole[:, QCOLS:].astype(jnp.float32)).astype(jnp.bfloat16)
    block[rows:] = digits[...]


def position_of(block, rows):
    digits = block[block.shape[0] - 16 :, :rows].astype(jnp.float32)
    return digits[1:2] * 256.0 + digits[:1]


def bias_of(lengths, own, others):
    rows = own.shape[0] - 16
    same = lax.broadcasted_iota(jnp.int32, (rows, rows), 0) == lax.broadcasted_iota(jnp.int32, (rows, rows), 1)
    position = jnp.sum(jnp.where(same, position_of(own, rows), 0.0), axis=1, keepdims=True).astype(jnp.int32)
    start = jnp.zeros_like(position)
    end = 0
    for i in range(lengths.shape[1]):
        end = end + lengths[0, i]
        start = jnp.where(position >= end, end, start)
    others = others.astype(jnp.int32)
    return jnp.where((others <= position) & (others >= start), 0.0, NEGATIVE)


def score(turned, latent, scores):
    half = turned.shape[0] // 2
    for at in (0, half):
        scores[at : at + half] = lax.dot_general(
            turned[at : at + half], latent[...], (((1,), (1,)), ((), ())), preferred_element_type=jnp.float32
        )


def score_kernel(count, size, lengths, query, *refs):
    blocks, refs = refs[: count - 1], refs[count - 1 :]
    expands, refs = refs[:size], refs[size:]
    turned, value, latent, bias, scores, expand = refs
    rows = query.shape[0]
    for i, block in enumerate(blocks):
        latent[i * rows : (i + 1) * rows, :] = block[:rows]
    bias[...] = bias_of(lengths, blocks[0], jnp.concatenate([position_of(block, rows) for block in blocks], axis=1))
    width = expands[0].shape[1]
    for i, block in enumerate(expands):
        at = (lax.axis_index("group") ^ i) * width
        expand[:, pl.ds(pl.multiple_of(at, width), width)] = block[...]
    for head in range(HEADS):
        value[:, head * HDIM : (head + 1) * HDIM] = expand[:, (2 * head + 1) * HDIM : (2 * head + 2) * HDIM]
        product = lax.dot_general(
            query[:, head * HDIM : (head + 1) * HDIM],
            expand[:, head * 2 * HDIM : (2 * head + 1) * HDIM],
            (((1,), (1,)), ((), ())),
            preferred_element_type=jnp.float32,
        )
        turned[head * rows : (head + 1) * rows] = (product * LOG2_E).astype(jnp.bfloat16)
    score(turned, latent, scores)


def attend_kernel(lengths, own, turned, value, latent, bias, scores, first, second, out, last, last_scores, probs, totals):
    rows, seen = out.shape[0], latent.shape[0]
    cut = first.shape[0]
    last[:cut] = first[...]
    last[cut:] = second[: rows - cut]
    last_bias = bias_of(lengths, own, position_of(second, rows))
    score(turned, last, last_scores)
    half = HEADS * rows // 2
    for begin in (0, half):
        for at in range(begin, begin + half, TILE):
            here = at % rows
            part = scores[at : at + TILE] + bias[here : here + TILE]
            last_part = last_scores[at : at + TILE] + last_bias[here : here + TILE]
            peak = jnp.maximum(
                jnp.max(part, axis=-1, keepdims=True), jnp.max(last_part, axis=-1, keepdims=True)
            )
            weights, last_weights = jnp.exp2(part - peak), jnp.exp2(last_part - peak)
            totals[at : at + TILE] = jnp.sum(weights, axis=-1, keepdims=True) + jnp.sum(
                last_weights, axis=-1, keepdims=True
            )
            probs[at : at + TILE, :seen] = weights.astype(jnp.bfloat16)
            probs[at : at + TILE, seen:] = last_weights.astype(jnp.bfloat16)
        summed = jnp.dot(
            probs[begin : begin + half, :seen], latent[...], preferred_element_type=jnp.float32
        ) + jnp.dot(probs[begin : begin + half, seen:], last[...], preferred_element_type=jnp.float32)
        summed = summed.astype(jnp.bfloat16)
        for i in range(HEADS // 2):
            head = begin // rows + i
            columns = slice(head * HDIM, (head + 1) * HDIM)
            outcome = jnp.dot(summed[i * rows : (i + 1) * rows], value[:, columns], preferred_element_type=jnp.float32)
            out[:, columns] = (outcome / totals[head * rows : (head + 1) * rows]).astype(jnp.bfloat16)


def body(arrivals, slots, lengths, w_joined, w_expand):
    count, size = lax.axis_size("mp"), lax.axis_size("group")
    rows, depth = arrivals.shape
    columns, rank = w_joined.shape[1], w_expand.shape[0] * count
    own_columns = w_expand.shape[1]

    weights = pl.pallas_call(
        pack_kernel,
        out_shape=jax.ShapeDtypeStruct(
            (w_joined.shape[0], columns + own_columns * w_expand.shape[0] // w_joined.shape[0]), jnp.bfloat16
        ),
        in_specs=[VMEM, VMEM],
        out_specs=VMEM,
        compiler_params=grant(16),
        name="pack",
    )(w_joined, w_expand)
    blocks = ring_gather(weights, count)
    arrivals, _ = lax.optimization_barrier((arrivals, weights))
    normed, digits = pl.pallas_call(
        norm_kernel,
        out_shape=[
            jax.ShapeDtypeStruct((rows, depth), jnp.bfloat16),
            jax.ShapeDtypeStruct((16, rank), jnp.bfloat16),
        ],
        in_specs=[VMEM, VMEM],
        out_specs=[VMEM, VMEM],
        compiler_params=grant(16),
        cost_estimate=pl.CostEstimate(flops=NORM_COST * rows * depth, bytes_accessed=NORM_COST * rows * depth, transcendentals=rows),
        name="norm",
    )(arrivals, slots.reshape(1, rows))
    tokens = group_gather(normed, size, blocks[-4:-2])
    early = 0 if w_joined.shape[0] // 2 % 128 else count - 3
    total = []
    if early:
        total = [
            pl.pallas_call(
                functools.partial(early_kernel, count, size),
                out_shape=jax.ShapeDtypeStruct((size * rows, columns), jnp.float32),
                in_specs=[VMEM] * (size + early),
                out_specs=VMEM,
                compiler_params=grant(16),
                cost_estimate=pl.CostEstimate(
                    flops=2 * size * rows * depth * columns, bytes_accessed=4 * depth * columns, transcendentals=0
                ),
                name="project_early",
            )(*tokens, *blocks[:early])
        ]
    *projs, own_expand = pl.pallas_call(
        functools.partial(proj_kernel, count, size, early),
        out_shape=[jax.ShapeDtypeStruct((rows, columns), jnp.bfloat16)] * size
        + [jax.ShapeDtypeStruct((rank, own_columns), jnp.bfloat16)],
        in_specs=[VMEM] * (size + count + 1 + len(total)),
        out_specs=[VMEM] * (size + 1),
        scratch_shapes=[] if early else [pltpu.VMEM((depth, columns), jnp.bfloat16)],
        compiler_params=grant(16),
        cost_estimate=pl.CostEstimate(
            flops=2 * size * rows * depth * columns, bytes_accessed=4 * depth * columns, transcendentals=0
        ),
        name="project",
    )(*tokens, *blocks, *total)

    back = [projs[0]]
    for k in range(1, size):
        back.append(lax.ppermute(projs[k], "group", [(i, i ^ k) for i in range(size)]))
    query, block = pl.pallas_call(
        functools.partial(assemble_kernel, size),
        out_shape=[
            jax.ShapeDtypeStruct((rows, QCOLS), jnp.bfloat16),
            jax.ShapeDtypeStruct((rows + 16, rank), jnp.bfloat16),
        ],
        in_specs=[VMEM] * (size + 1),
        out_specs=[VMEM, VMEM],
        scratch_shapes=[pltpu.VMEM((size, rows, columns), jnp.bfloat16)],
        compiler_params=grant(16),
        name="assemble",
    )(digits, *back)
    lat_blocks = ring_gather(block, count)
    own_expand, _ = lax.optimization_barrier((own_expand, lat_blocks[1:3]))
    expands = group_gather(own_expand, size, lat_blocks[-4:-2])

    total, seen = count * rows, (count - 1) * rows
    needed = grant(8 + total * HEADS * rows * 8 // (1024 * 1024))
    made = pl.pallas_call(
        functools.partial(score_kernel, count, size),
        out_shape=[
            jax.ShapeDtypeStruct((HEADS * rows, rank), jnp.bfloat16),
            jax.ShapeDtypeStruct((rank, QCOLS), jnp.bfloat16),
            jax.ShapeDtypeStruct((seen, rank), jnp.bfloat16),
            jax.ShapeDtypeStruct((rows, seen), jnp.float32),
            jax.ShapeDtypeStruct((HEADS * rows, seen), jnp.float32),
        ],
        in_specs=[SMEM] + [VMEM] * (count + size),
        out_specs=[VMEM] * 5,
        scratch_shapes=[pltpu.VMEM((rank, 2 * QCOLS), jnp.bfloat16)],
        compiler_params=needed,
        cost_estimate=pl.CostEstimate(
            flops=2 * total * rank * QCOLS, bytes_accessed=8 * QCOLS * rank, transcendentals=0
        ),
        name="score",
    )(lengths, query, *lat_blocks[: count - 1], *expands)
    return pl.pallas_call(
        attend_kernel,
        out_shape=jax.ShapeDtypeStruct((rows, QCOLS), jnp.bfloat16),
        in_specs=[SMEM] + [VMEM] * 8,
        out_specs=VMEM,
        scratch_shapes=[
            pltpu.VMEM((rows, rank), jnp.bfloat16),
            pltpu.VMEM((HEADS * rows, rows), jnp.float32),
            pltpu.VMEM((HEADS * rows, total), jnp.bfloat16),
            pltpu.VMEM((HEADS * rows, 1), jnp.float32),
        ],
        compiler_params=needed,
        cost_estimate=pl.CostEstimate(
            flops=2 * total * rank * QCOLS, bytes_accessed=8 * QCOLS * rank, transcendentals=HEADS * rows * total
        ),
        name="attend",
    )(lengths, block, *made, *lat_blocks[count - 1 :])


def solution(mesh):
    in_specs = (
        P(("group", "mp"), None),
        P(("group", "mp")),
        P("group", None),
        P("mp", "group"),
        P("mp", "group"),
    )
    out_specs = P(("group", "mp"), None)
    return jax.shard_map(body, mesh=mesh, in_specs=in_specs, out_specs=out_specs, check_vma=False)
```

```python
import functools

import jax
import jax.numpy as jnp
from jax import lax
from jax.experimental import pallas as pl
from jax.experimental.pallas import tpu as pltpu
from jax.sharding import PartitionSpec as P

HEADS = 8
HDIM = 128
QCOLS = HEADS * HDIM

EPS = 1e-06
NEGATIVE = -1e30
LOG2_E = 1.4426950408889634
TILE = 16
NORM_COST = 64
VMEM = pl.BlockSpec(memory_space=pltpu.VMEM)
SMEM = pl.BlockSpec(memory_space=pltpu.SMEM)


def grant(mib):
    return pltpu.CompilerParams(vmem_limit_bytes=mib * 1024 * 1024)


def row_norm(values):
    mean_sq = jnp.mean(values * values, axis=-1, keepdims=True)
    return values * lax.rsqrt(mean_sq + EPS)


def ring_pairs(count, step):
    order = [2 * r if r < count // 2 else 2 * (count - 1 - r) + 1 for r in range(count)]
    return [(order[r], order[(r + step) % count]) for r in range(count)]


def ring_gather(block, count):
    up, down = ring_pairs(count, 1), ring_pairs(count, -1)
    below = above = block
    blocks = [block]
    for _ in range((count - 1) // 2):
        below, above = lax.ppermute(below, "mp", up), lax.ppermute(above, "mp", down)
        blocks += [below, above]
    cut = -(-block.shape[0] // 32) * 16
    return blocks + [lax.ppermute(below[:cut], "mp", up), lax.ppermute(above[cut:], "mp", down)]


def ring_owners(count):
    me = lax.axis_index("mp")
    place = jnp.where(me % 2 == 0, me // 2, count - 1 - me // 2)
    owners = [me]
    for step in range(1, count // 2 + 1):
        for shift in (-step, step):
            at = lax.rem(place + shift + count, count)
            owners.append(jnp.where(at < count // 2, 2 * at, 2 * (count - 1 - at) + 1))
    return owners[:count]


def row_ranges(blocks):
    last = len(blocks) - 2
    return [(i, 0) for i in range(last + 1)] + [(last, blocks[last].shape[0])]


def group_gather(block, size, after=None):
    blocks = {0: block}
    bit = size // 2
    while bit:
        pairs = [(i, i ^ bit) for i in range(size)]
        for k in list(blocks):
            sent = blocks[k]
            if k and after is not None:
                sent, _ = lax.optimization_barrier((sent, after))
            blocks[k ^ bit] = lax.ppermute(sent, "group", pairs)
        bit //= 2
    return [blocks[k] for k in range(size)]


def pack_kernel(joined, expand, out):
    columns, high = joined.shape[1], expand.shape[0]
    folds = joined.shape[0] // high
    fold = expand.shape[1] // folds
    out[:, :columns] = joined[...].astype(jnp.bfloat16)
    for i in range(folds):
        out[i * high : (i + 1) * high, columns:] = expand[:, i * fold : (i + 1) * fold].astype(jnp.bfloat16)


def norm_kernel(arrivals, slots, normed, digits):
    normed[...] = row_norm(arrivals[...].astype(jnp.float32)).astype(jnp.bfloat16)
    rows = slots.shape[1]
    bits = jnp.concatenate([slots[...] & 255, slots[...] >> 8], axis=0).astype(jnp.float32)
    bits = jnp.concatenate([bits, jnp.zeros((14, rows), jnp.float32)], axis=0)
    digits[...] = jnp.zeros_like(digits)
    digits[:, :rows] = bits.astype(jnp.bfloat16)


def multiply(tokens, starts, blocks, columns):
    total = None
    for start, block in zip(starts, blocks):
        span = pl.ds(pl.multiple_of(start, 128), block.shape[0])
        left = jnp.concatenate([token[:, span] for token in tokens], axis=0)
        product = jnp.dot(left, block[:, :columns], preferred_element_type=jnp.float32)
        total = product if total is None else total + product
    return total


def early_kernel(count, size, *refs):
    tokens, blocks, total = refs[:size], refs[size:-1], refs[-1]
    depth = blocks[0].shape[0]
    total[...] = multiply(tokens, [owner * depth for owner in ring_owners(count)], blocks, total.shape[1])


def proj_kernel(count, size, early, *refs):
    tokens, refs = refs[:size], refs[size:]
    blocks, refs = refs[: count + 1], refs[count + 1 :]
    depth = blocks[0].shape[0]
    owners = ring_owners(count)
    starts = [owners[i] * depth + offset for i, offset in row_ranges(blocks)]
    if early:
        total, refs = refs[0], refs[1:]
        outs, expand = refs[:size], refs[size]
        rows, columns = outs[0].shape
        proj = total[...] + multiply(tokens, starts[early:], blocks[early:], columns)
    else:
        outs, expand, weight = refs[:size], refs[size], refs[size + 1]
        rows, columns = outs[0].shape
        for start, block in zip(starts, blocks):
            length = block.shape[0]
            weight[pl.ds(pl.multiple_of(start, length), length), :] = block[:, :columns]
        products = [jnp.dot(token[...], weight[...], preferred_element_type=jnp.float32) for token in tokens]
        proj = jnp.concatenate(products, axis=0)
    at = lax.axis_index("group") * columns + lax.broadcasted_iota(jnp.int32, (1, columns), 1)
    proj = proj * jnp.where(at < QCOLS, HDIM**-0.5, 1.0).astype(jnp.float32)
    for i, out in enumerate(outs):
        out[...] = proj[i * rows : (i + 1) * rows].astype(jnp.bfloat16)
    high = expand.shape[0] // count
    for i, owner in enumerate(owners):
        parts = []
        for block in blocks[i:] if i == count - 1 else blocks[i : i + 1]:
            parts += [block[j * high : (j + 1) * high, columns:] for j in range(block.shape[0] // high)]
        expand[pl.ds(pl.multiple_of(owner * high, high), high), :] = jnp.concatenate(parts, axis=1)


def assemble_kernel(size, digits, *refs):
    products, (query, block, proj) = refs[:size], refs[size:]
    group = lax.axis_index("group")
    for i, product in enumerate(products):
        proj[group ^ i] = product[...]
    whole = jnp.concatenate([proj[i] for i in range(size)], axis=1)
    query[...] = whole[:, :QCOLS]
    rows = query.shape[0]
    block[:rows] = row_norm(whole[:, QCOLS:].astype(jnp.float32)).astype(jnp.bfloat16)
    block[rows:] = digits[...]


def position_of(block, rows):
    digits = block[block.shape[0] - 16 :, :rows].astype(jnp.float32)
    return digits[1:2] * 256.0 + digits[:1]


def bias_of(lengths, own, others):
    rows = own.shape[0] - 16
    same = lax.broadcasted_iota(jnp.int32, (rows, rows), 0) == lax.broadcasted_iota(jnp.int32, (rows, rows), 1)
    position = jnp.sum(jnp.where(same, position_of(own, rows), 0.0), axis=1, keepdims=True).astype(jnp.int32)
    start = jnp.zeros_like(position)
    end = 0
    for i in range(lengths.shape[1]):
        end = end + lengths[0, i]
        start = jnp.where(position >= end, end, start)
    others = others.astype(jnp.int32)
    return jnp.where((others <= position) & (others >= start), 0.0, NEGATIVE)


def score(turned, latent, scores):
    half = turned.shape[0] // 2
    for at in (0, half):
        scores[at : at + half] = lax.dot_general(
            turned[at : at + half], latent[...], (((1,), (1,)), ((), ())), preferred_element_type=jnp.float32
        )


def score_kernel(count, size, lengths, query, *refs):
    blocks, refs = refs[: count - 1], refs[count - 1 :]
    expands, refs = refs[:size], refs[size:]
    turned, value, latent, probs, peaks, sums, expand, scores = refs
    rows = query.shape[0]
    for i, block in enumerate(blocks):
        latent[i * rows : (i + 1) * rows, :] = block[:rows]
    bias = bias_of(lengths, blocks[0], jnp.concatenate([position_of(block, rows) for block in blocks], axis=1))
    width = expands[0].shape[1]
    for i, block in enumerate(expands):
        at = (lax.axis_index("group") ^ i) * width
        expand[:, pl.ds(pl.multiple_of(at, width), width)] = block[...]
    for head in range(HEADS):
        value[:, head * HDIM : (head + 1) * HDIM] = expand[:, (2 * head + 1) * HDIM : (2 * head + 2) * HDIM]
        product = lax.dot_general(
            query[:, head * HDIM : (head + 1) * HDIM],
            expand[:, head * 2 * HDIM : (2 * head + 1) * HDIM],
            (((1,), (1,)), ((), ())),
            preferred_element_type=jnp.float32,
        )
        turned[head * rows : (head + 1) * rows] = (product * LOG2_E).astype(jnp.bfloat16)
    score(turned, latent, scores)
    for at in range(0, HEADS * rows, TILE):
        here = at % rows
        part = scores[at : at + TILE] + bias[here : here + TILE]
        peak = jnp.max(part, axis=-1, keepdims=True)
        weights = jnp.exp2(part - peak)
        peaks[at : at + TILE] = peak
        sums[at : at + TILE] = jnp.sum(weights, axis=-1, keepdims=True)
        probs[at : at + TILE] = weights.astype(jnp.bfloat16)


def attend_kernel(lengths, own, turned, value, latent, probs, peaks, sums, *refs):
    pieces, (out, last, scores, last_probs, factors, totals) = refs[:-6], refs[-6:]
    rows, done = out.shape[0], 0
    for piece in pieces:
        length = min(rows - done, piece.shape[0])
        last[done : done + length] = piece[:length]
        done += length
    bias = bias_of(lengths, own, position_of(pieces[-1], rows))
    score(turned, last, scores)
    half = HEADS * rows // 2
    for begin in (0, half):
        for at in range(begin, begin + half, TILE):
            here = at % rows
            part = scores[at : at + TILE] + bias[here : here + TILE]
            peak = jnp.maximum(peaks[at : at + TILE], jnp.max(part, axis=-1, keepdims=True))
            weights = jnp.exp2(part - peak)
            factor = jnp.exp2(peaks[at : at + TILE] - peak)
            factors[at : at + TILE] = factor
            totals[at : at + TILE] = sums[at : at + TILE] * factor + jnp.sum(weights, axis=-1, keepdims=True)
            last_probs[at : at + TILE] = weights.astype(jnp.bfloat16)
        summed = jnp.dot(probs[begin : begin + half], latent[...], preferred_element_type=jnp.float32)
        summed = summed * factors[begin : begin + half] + jnp.dot(
            last_probs[begin : begin + half], last[...], preferred_element_type=jnp.float32
        )
        summed = summed.astype(jnp.bfloat16)
        for i in range(HEADS // 2):
            head = begin // rows + i
            columns = slice(head * HDIM, (head + 1) * HDIM)
            outcome = jnp.dot(summed[i * rows : (i + 1) * rows], value[:, columns], preferred_element_type=jnp.float32)
            out[:, columns] = (outcome / totals[head * rows : (head + 1) * rows]).astype(jnp.bfloat16)


def body(arrivals, slots, lengths, w_joined, w_expand):
    count, size = lax.axis_size("mp"), lax.axis_size("group")
    rows, depth = arrivals.shape
    columns, rank = w_joined.shape[1], w_expand.shape[0] * count
    own_columns = w_expand.shape[1]

    weights = pl.pallas_call(
        pack_kernel,
        out_shape=jax.ShapeDtypeStruct(
            (w_joined.shape[0], columns + own_columns * w_expand.shape[0] // w_joined.shape[0]), jnp.bfloat16
        ),
        in_specs=[VMEM, VMEM],
        out_specs=VMEM,
        compiler_params=grant(16),
        name="pack",
    )(w_joined, w_expand)
    blocks = ring_gather(weights, count)
    arrivals, _ = lax.optimization_barrier((arrivals, weights))
    normed, digits = pl.pallas_call(
        norm_kernel,
        out_shape=[
            jax.ShapeDtypeStruct((rows, depth), jnp.bfloat16),
            jax.ShapeDtypeStruct((16, rank), jnp.bfloat16),
        ],
        in_specs=[VMEM, VMEM],
        out_specs=[VMEM, VMEM],
        compiler_params=grant(16),
        cost_estimate=pl.CostEstimate(flops=NORM_COST * rows * depth, bytes_accessed=NORM_COST * rows * depth, transcendentals=rows),
        name="norm",
    )(arrivals, slots.reshape(1, rows))
    tokens = group_gather(normed, size, blocks[-4:-2])
    early = 0 if w_joined.shape[0] // 2 % 128 else count - 3
    total = []
    if early:
        total = [
            pl.pallas_call(
                functools.partial(early_kernel, count, size),
                out_shape=jax.ShapeDtypeStruct((size * rows, columns), jnp.float32),
                in_specs=[VMEM] * (size + early),
                out_specs=VMEM,
                compiler_params=grant(16),
                cost_estimate=pl.CostEstimate(
                    flops=2 * size * rows * depth * columns, bytes_accessed=4 * depth * columns, transcendentals=0
                ),
                name="project_early",
            )(*tokens, *blocks[:early])
        ]
    *projs, own_expand = pl.pallas_call(
        functools.partial(proj_kernel, count, size, early),
        out_shape=[jax.ShapeDtypeStruct((rows, columns), jnp.bfloat16)] * size
        + [jax.ShapeDtypeStruct((rank, own_columns), jnp.bfloat16)],
        in_specs=[VMEM] * (size + count + 1 + len(total)),
        out_specs=[VMEM] * (size + 1),
        scratch_shapes=[] if early else [pltpu.VMEM((depth, columns), jnp.bfloat16)],
        compiler_params=grant(16),
        cost_estimate=pl.CostEstimate(
            flops=2 * size * rows * depth * columns, bytes_accessed=4 * depth * columns, transcendentals=0
        ),
        name="project",
    )(*tokens, *blocks, *total)

    back = [projs[0]]
    for k in range(1, size):
        back.append(lax.ppermute(projs[k], "group", [(i, i ^ k) for i in range(size)]))
    query, block = pl.pallas_call(
        functools.partial(assemble_kernel, size),
        out_shape=[
            jax.ShapeDtypeStruct((rows, QCOLS), jnp.bfloat16),
            jax.ShapeDtypeStruct((rows + 16, rank), jnp.bfloat16),
        ],
        in_specs=[VMEM] * (size + 1),
        out_specs=[VMEM, VMEM],
        scratch_shapes=[pltpu.VMEM((size, rows, columns), jnp.bfloat16)],
        compiler_params=grant(16),
        name="assemble",
    )(digits, *back)
    lat_blocks = ring_gather(block, count)
    own_expand, _ = lax.optimization_barrier((own_expand, lat_blocks[1:3]))
    expands = group_gather(own_expand, size, lat_blocks[-4:-2])

    total, seen = count * rows, (count - 1) * rows
    needed = grant(8 + total * HEADS * rows * 8 // (1024 * 1024))
    made = pl.pallas_call(
        functools.partial(score_kernel, count, size),
        out_shape=[
            jax.ShapeDtypeStruct((HEADS * rows, rank), jnp.bfloat16),
            jax.ShapeDtypeStruct((rank, QCOLS), jnp.bfloat16),
            jax.ShapeDtypeStruct((seen, rank), jnp.bfloat16),
            jax.ShapeDtypeStruct((HEADS * rows, seen), jnp.bfloat16),
            jax.ShapeDtypeStruct((HEADS * rows, 1), jnp.float32),
            jax.ShapeDtypeStruct((HEADS * rows, 1), jnp.float32),
        ],
        in_specs=[SMEM] + [VMEM] * (count + size),
        out_specs=[VMEM] * 6,
        scratch_shapes=[
            pltpu.VMEM((rank, 2 * QCOLS), jnp.bfloat16),
            pltpu.VMEM((HEADS * rows, seen), jnp.float32),
        ],
        compiler_params=needed,
        cost_estimate=pl.CostEstimate(
            flops=2 * total * rank * QCOLS, bytes_accessed=8 * QCOLS * rank, transcendentals=0
        ),
        name="score",
    )(lengths, query, *lat_blocks[: count - 1], *expands)
    return pl.pallas_call(
        attend_kernel,
        out_shape=jax.ShapeDtypeStruct((rows, QCOLS), jnp.bfloat16),
        in_specs=[SMEM] + [VMEM] * (3 + len(made)),
        out_specs=VMEM,
        scratch_shapes=[
            pltpu.VMEM((rows, rank), jnp.bfloat16),
            pltpu.VMEM((HEADS * rows, rows), jnp.float32),
            pltpu.VMEM((HEADS * rows, rows), jnp.bfloat16),
            pltpu.VMEM((HEADS * rows, 1), jnp.float32),
            pltpu.VMEM((HEADS * rows, 1), jnp.float32),
        ],
        compiler_params=needed,
        cost_estimate=pl.CostEstimate(
            flops=2 * total * rank * QCOLS, bytes_accessed=8 * QCOLS * rank, transcendentals=HEADS * rows * total
        ),
        name="attend",
    )(lengths, block, *made, *lat_blocks[count - 1 :])


def solution(mesh):
    in_specs = (
        P(("group", "mp"), None),
        P(("group", "mp")),
        P("group", None),
        P("mp", "group"),
        P("mp", "group"),
    )
    out_specs = P(("group", "mp"), None)
    return jax.shard_map(body, mesh=mesh, in_specs=in_specs, out_specs=out_specs, check_vma=False)
```

```python
import functools

import jax
import jax.numpy as jnp
from jax import lax
from jax.experimental import pallas as pl
from jax.experimental.pallas import tpu as pltpu
from jax.sharding import PartitionSpec as P

HEADS = 8
HDIM = 128
QCOLS = HEADS * HDIM

EPS = 1e-06
NEGATIVE = -1e30
LOG2_E = 1.4426950408889634
TILE = 16
NORM_COST = 64
VMEM = pl.BlockSpec(memory_space=pltpu.VMEM)
SMEM = pl.BlockSpec(memory_space=pltpu.SMEM)


def grant(mib):
    return pltpu.CompilerParams(vmem_limit_bytes=mib * 1024 * 1024)


def row_norm(values):
    mean_sq = jnp.mean(values * values, axis=-1, keepdims=True)
    return values * lax.rsqrt(mean_sq + EPS)


def ring_pairs(count, step):
    order = [2 * r if r < count // 2 else 2 * (count - 1 - r) + 1 for r in range(count)]
    return [(order[r], order[(r + step) % count]) for r in range(count)]


def ring_gather(block, count):
    up, down = ring_pairs(count, 1), ring_pairs(count, -1)
    below = above = block
    blocks = [block]
    for _ in range((count - 1) // 2):
        below, above = lax.ppermute(below, "mp", up), lax.ppermute(above, "mp", down)
        blocks += [below, above]
    cut = -(-block.shape[0] // 32) * 16
    return blocks + [lax.ppermute(below[:cut], "mp", up), lax.ppermute(above[cut:], "mp", down)]


def ring_owners(count):
    me = lax.axis_index("mp")
    place = jnp.where(me % 2 == 0, me // 2, count - 1 - me // 2)
    owners = [me]
    for step in range(1, count // 2 + 1):
        for shift in (-step, step):
            at = lax.rem(place + shift + count, count)
            owners.append(jnp.where(at < count // 2, 2 * at, 2 * (count - 1 - at) + 1))
    return owners[:count]


def row_ranges(blocks):
    last = len(blocks) - 2
    return [(i, 0) for i in range(last + 1)] + [(last, blocks[last].shape[0])]


def group_gather(block, size, after=None):
    blocks = {0: block}
    bit = size // 2
    while bit:
        pairs = [(i, i ^ bit) for i in range(size)]
        for k in list(blocks):
            sent = blocks[k]
            if k and after is not None:
                sent, _ = lax.optimization_barrier((sent, after))
            blocks[k ^ bit] = lax.ppermute(sent, "group", pairs)
        bit //= 2
    return [blocks[k] for k in range(size)]


def pack_kernel(joined, expand, out):
    columns, high = joined.shape[1], expand.shape[0]
    folds = joined.shape[0] // high
    fold = expand.shape[1] // folds
    out[:, :columns] = joined[...].astype(jnp.bfloat16)
    for i in range(folds):
        out[i * high : (i + 1) * high, columns:] = expand[:, i * fold : (i + 1) * fold].astype(jnp.bfloat16)


def norm_kernel(arrivals, slots, normed, digits):
    normed[...] = row_norm(arrivals[...].astype(jnp.float32)).astype(jnp.bfloat16)
    rows = slots.shape[1]
    bits = jnp.concatenate([slots[...] & 255, slots[...] >> 8], axis=0).astype(jnp.float32)
    bits = jnp.concatenate([bits, jnp.zeros((14, rows), jnp.float32)], axis=0)
    digits[...] = jnp.zeros_like(digits)
    digits[:, :rows] = bits.astype(jnp.bfloat16)


def multiply(tokens, starts, blocks, columns):
    total = None
    for start, block in zip(starts, blocks):
        span = pl.ds(pl.multiple_of(start, 128), block.shape[0])
        left = jnp.concatenate([token[:, span] for token in tokens], axis=0)
        product = jnp.dot(left, block[:, :columns], preferred_element_type=jnp.float32)
        total = product if total is None else total + product
    return total


def early_kernel(count, size, *refs):
    tokens, blocks, total = refs[:size], refs[size:-1], refs[-1]
    depth = blocks[0].shape[0]
    total[...] = multiply(tokens, [owner * depth for owner in ring_owners(count)], blocks, total.shape[1])


def proj_kernel(count, size, early, *refs):
    tokens, refs = refs[:size], refs[size:]
    blocks, refs = refs[: count + 1], refs[count + 1 :]
    depth = blocks[0].shape[0]
    owners = ring_owners(count)
    starts = [owners[i] * depth + offset for i, offset in row_ranges(blocks)]
    if early:
        total, refs = refs[0], refs[1:]
        outs, expand = refs[:size], refs[size]
        rows, columns = outs[0].shape
        proj = total[...] + multiply(tokens, starts[early:], blocks[early:], columns)
    else:
        outs, expand, weight = refs[:size], refs[size], refs[size + 1]
        rows, columns = outs[0].shape
        for start, block in zip(starts, blocks):
            length = block.shape[0]
            weight[pl.ds(pl.multiple_of(start, length), length), :] = block[:, :columns]
        products = [jnp.dot(token[...], weight[...], preferred_element_type=jnp.float32) for token in tokens]
        proj = jnp.concatenate(products, axis=0)
    at = lax.axis_index("group") * columns + lax.broadcasted_iota(jnp.int32, (1, columns), 1)
    proj = proj * jnp.where(at < QCOLS, HDIM**-0.5, 1.0).astype(jnp.float32)
    for i, out in enumerate(outs):
        out[...] = proj[i * rows : (i + 1) * rows].astype(jnp.bfloat16)
    high = expand.shape[0] // count
    for i, owner in enumerate(owners):
        parts = []
        for block in blocks[i:] if i == count - 1 else blocks[i : i + 1]:
            parts += [block[j * high : (j + 1) * high, columns:] for j in range(block.shape[0] // high)]
        expand[pl.ds(pl.multiple_of(owner * high, high), high), :] = jnp.concatenate(parts, axis=1)


def assemble_kernel(size, digits, *refs):
    products, (query, block, proj) = refs[:size], refs[size:]
    group = lax.axis_index("group")
    for i, product in enumerate(products):
        proj[group ^ i] = product[...]
    whole = jnp.concatenate([proj[i] for i in range(size)], axis=1)
    query[...] = whole[:, :QCOLS]
    rows = query.shape[0]
    block[:rows] = row_norm(whole[:, QCOLS:].astype(jnp.float32)).astype(jnp.bfloat16)
    block[rows:] = digits[...]


def position_of(block, rows):
    digits = block[block.shape[0] - 16 :, :rows].astype(jnp.float32)
    return digits[1:2] * 256.0 + digits[:1]


def bias_of(lengths, own, others):
    rows = own.shape[0] - 16
    same = lax.broadcasted_iota(jnp.int32, (rows, rows), 0) == lax.broadcasted_iota(jnp.int32, (rows, rows), 1)
    position = jnp.sum(jnp.where(same, position_of(own, rows), 0.0), axis=1, keepdims=True).astype(jnp.int32)
    start = jnp.zeros_like(position)
    end = 0
    for i in range(lengths.shape[1]):
        end = end + lengths[0, i]
        start = jnp.where(position >= end, end, start)
    others = others.astype(jnp.int32)
    return jnp.where((others <= position) & (others >= start), 0.0, NEGATIVE)


def score(turned, latent, scores):
    half = turned.shape[0] // 2
    for at in (0, half):
        scores[at : at + half] = lax.dot_general(
            turned[at : at + half], latent[...], (((1,), (1,)), ((), ())), preferred_element_type=jnp.float32
        )


def score_kernel(count, size, lengths, query, *refs):
    blocks, refs = refs[: count - 1], refs[count - 1 :]
    expands, refs = refs[:size], refs[size:]
    turned, value, latent, probs, peaks, sums, expand, scores = refs
    rows = query.shape[0]
    for i, block in enumerate(blocks):
        latent[i * rows : (i + 1) * rows, :] = block[:rows]
    bias = bias_of(lengths, blocks[0], jnp.concatenate([position_of(block, rows) for block in blocks], axis=1))
    width = expands[0].shape[1]
    for i, block in enumerate(expands):
        at = (lax.axis_index("group") ^ i) * width
        expand[:, pl.ds(pl.multiple_of(at, width), width)] = block[...]
    for head in range(HEADS):
        value[:, head * HDIM : (head + 1) * HDIM] = expand[:, (2 * head + 1) * HDIM : (2 * head + 2) * HDIM]
        product = lax.dot_general(
            query[:, head * HDIM : (head + 1) * HDIM],
            expand[:, head * 2 * HDIM : (2 * head + 1) * HDIM],
            (((1,), (1,)), ((), ())),
            preferred_element_type=jnp.float32,
        )
        turned[head * rows : (head + 1) * rows] = (product * LOG2_E).astype(jnp.bfloat16)
    score(turned, latent, scores)
    for at in range(0, HEADS * rows, TILE):
        here = at % rows
        part = scores[at : at + TILE] + bias[here : here + TILE]
        peak = jnp.max(part, axis=-1, keepdims=True)
        weights = jnp.exp2(part - peak)
        peaks[at : at + TILE] = jnp.broadcast_to(peak, (TILE, HDIM))
        sums[at : at + TILE] = jnp.broadcast_to(jnp.sum(weights, axis=-1, keepdims=True), (TILE, HDIM))
        probs[at : at + TILE] = weights.astype(jnp.bfloat16)


def attend_kernel(lengths, own, turned, value, latent, probs, peaks, sums, *refs):
    pieces, (out, last, scores) = refs[:-3], refs[-3:]
    rows, rank, done = out.shape[0], latent.shape[1], 0
    for piece in pieces:
        length = min(rows - done, piece.shape[0])
        last[done : done + length] = piece[:length]
        done += length
    bias = bias_of(lengths, own, position_of(pieces[-1], rows))
    score(turned, last, scores)
    some = HEADS // 2
    biases = jnp.concatenate([bias] * some, axis=0)
    for first in range(0, HEADS, some):
        here = slice(first * rows, (first + some) * rows)
        part = scores[here] + biases
        peak = jnp.maximum(peaks[here], jnp.max(part, axis=-1, keepdims=True))
        weights = jnp.exp2(part - peak)
        factor = jnp.exp2(peaks[here] - peak)
        total = sums[here] * factor + jnp.sum(weights, axis=-1, keepdims=True)
        summed = jnp.dot(probs[here], latent[...], preferred_element_type=jnp.float32)
        summed = summed * jnp.concatenate([factor] * (rank // HDIM), axis=1) + jnp.dot(
            weights.astype(jnp.bfloat16), last[...], preferred_element_type=jnp.float32
        )
        summed = summed.astype(jnp.bfloat16)
        for i in range(some):
            columns = slice((first + i) * HDIM, (first + i + 1) * HDIM)
            outcome = jnp.dot(summed[i * rows : (i + 1) * rows], value[:, columns], preferred_element_type=jnp.float32)
            out[:, columns] = (outcome / total[i * rows : (i + 1) * rows]).astype(jnp.bfloat16)


def body(arrivals, slots, lengths, w_joined, w_expand):
    count, size = lax.axis_size("mp"), lax.axis_size("group")
    rows, depth = arrivals.shape
    columns, rank = w_joined.shape[1], w_expand.shape[0] * count
    own_columns = w_expand.shape[1]

    weights = pl.pallas_call(
        pack_kernel,
        out_shape=jax.ShapeDtypeStruct(
            (w_joined.shape[0], columns + own_columns * w_expand.shape[0] // w_joined.shape[0]), jnp.bfloat16
        ),
        in_specs=[VMEM, VMEM],
        out_specs=VMEM,
        compiler_params=grant(16),
        name="pack",
    )(w_joined, w_expand)
    blocks = ring_gather(weights, count)
    arrivals, _ = lax.optimization_barrier((arrivals, weights))
    normed, digits = pl.pallas_call(
        norm_kernel,
        out_shape=[
            jax.ShapeDtypeStruct((rows, depth), jnp.bfloat16),
            jax.ShapeDtypeStruct((16, rank), jnp.bfloat16),
        ],
        in_specs=[VMEM, VMEM],
        out_specs=[VMEM, VMEM],
        compiler_params=grant(16),
        cost_estimate=pl.CostEstimate(flops=NORM_COST * rows * depth, bytes_accessed=NORM_COST * rows * depth, transcendentals=rows),
        name="norm",
    )(arrivals, slots.reshape(1, rows))
    tokens = group_gather(normed, size, blocks[-4:-2])
    early = 0 if w_joined.shape[0] // 2 % 128 else count - 3
    total = []
    if early:
        total = [
            pl.pallas_call(
                functools.partial(early_kernel, count, size),
                out_shape=jax.ShapeDtypeStruct((size * rows, columns), jnp.float32),
                in_specs=[VMEM] * (size + early),
                out_specs=VMEM,
                compiler_params=grant(16),
                cost_estimate=pl.CostEstimate(
                    flops=2 * size * rows * depth * columns, bytes_accessed=4 * depth * columns, transcendentals=0
                ),
                name="project_early",
            )(*tokens, *blocks[:early])
        ]
    *projs, own_expand = pl.pallas_call(
        functools.partial(proj_kernel, count, size, early),
        out_shape=[jax.ShapeDtypeStruct((rows, columns), jnp.bfloat16)] * size
        + [jax.ShapeDtypeStruct((rank, own_columns), jnp.bfloat16)],
        in_specs=[VMEM] * (size + count + 1 + len(total)),
        out_specs=[VMEM] * (size + 1),
        scratch_shapes=[] if early else [pltpu.VMEM((depth, columns), jnp.bfloat16)],
        compiler_params=grant(16),
        cost_estimate=pl.CostEstimate(
            flops=2 * size * rows * depth * columns, bytes_accessed=4 * depth * columns, transcendentals=0
        ),
        name="project",
    )(*tokens, *blocks, *total)

    back = [projs[0]]
    for k in range(1, size):
        back.append(lax.ppermute(projs[k], "group", [(i, i ^ k) for i in range(size)]))
    query, block = pl.pallas_call(
        functools.partial(assemble_kernel, size),
        out_shape=[
            jax.ShapeDtypeStruct((rows, QCOLS), jnp.bfloat16),
            jax.ShapeDtypeStruct((rows + 16, rank), jnp.bfloat16),
        ],
        in_specs=[VMEM] * (size + 1),
        out_specs=[VMEM, VMEM],
        scratch_shapes=[pltpu.VMEM((size, rows, columns), jnp.bfloat16)],
        compiler_params=grant(16),
        name="assemble",
    )(digits, *back)
    lat_blocks = ring_gather(block, count)
    own_expand, _ = lax.optimization_barrier((own_expand, lat_blocks[1:3]))
    expands = group_gather(own_expand, size, lat_blocks[-4:-2])

    total, seen = count * rows, (count - 1) * rows
    needed = grant(8 + total * HEADS * rows * 8 // (1024 * 1024))
    made = pl.pallas_call(
        functools.partial(score_kernel, count, size),
        out_shape=[
            jax.ShapeDtypeStruct((HEADS * rows, rank), jnp.bfloat16),
            jax.ShapeDtypeStruct((rank, QCOLS), jnp.bfloat16),
            jax.ShapeDtypeStruct((seen, rank), jnp.bfloat16),
            jax.ShapeDtypeStruct((HEADS * rows, seen), jnp.bfloat16),
            jax.ShapeDtypeStruct((HEADS * rows, HDIM), jnp.float32),
            jax.ShapeDtypeStruct((HEADS * rows, HDIM), jnp.float32),
        ],
        in_specs=[SMEM] + [VMEM] * (count + size),
        out_specs=[VMEM] * 6,
        scratch_shapes=[
            pltpu.VMEM((rank, 2 * QCOLS), jnp.bfloat16),
            pltpu.VMEM((HEADS * rows, seen), jnp.float32),
        ],
        compiler_params=needed,
        cost_estimate=pl.CostEstimate(
            flops=2 * total * rank * QCOLS, bytes_accessed=8 * QCOLS * rank, transcendentals=0
        ),
        name="score",
    )(lengths, query, *lat_blocks[: count - 1], *expands)
    return pl.pallas_call(
        attend_kernel,
        out_shape=jax.ShapeDtypeStruct((rows, QCOLS), jnp.bfloat16),
        in_specs=[SMEM] + [VMEM] * (3 + len(made)),
        out_specs=VMEM,
        scratch_shapes=[
            pltpu.VMEM((rows, rank), jnp.bfloat16),
            pltpu.VMEM((HEADS * rows, rows), jnp.float32),
        ],
        compiler_params=needed,
        cost_estimate=pl.CostEstimate(
            flops=2 * total * rank * QCOLS, bytes_accessed=8 * QCOLS * rank, transcendentals=HEADS * rows * total
        ),
        name="attend",
    )(lengths, block, *made, *lat_blocks[count - 1 :])


def solution(mesh):
    in_specs = (
        P(("group", "mp"), None),
        P(("group", "mp")),
        P("group", None),
        P("mp", "group"),
        P("mp", "group"),
    )
    out_specs = P(("group", "mp"), None)
    return jax.shard_map(body, mesh=mesh, in_specs=in_specs, out_specs=out_specs, check_vma=False)
```

```python
import functools

import jax
import jax.numpy as jnp
from jax import lax
from jax.experimental import pallas as pl
from jax.experimental.pallas import tpu as pltpu
from jax.sharding import PartitionSpec as P

HEADS = 8
HDIM = 128
QCOLS = HEADS * HDIM

EPS = 1e-06
NEGATIVE = -1e30
LOG2_E = 1.4426950408889634
TILE = 16
NORM_COST = 64
VMEM = pl.BlockSpec(memory_space=pltpu.VMEM)
SMEM = pl.BlockSpec(memory_space=pltpu.SMEM)


def grant(mib):
    return pltpu.CompilerParams(vmem_limit_bytes=mib * 1024 * 1024)


def row_norm(values):
    mean_sq = jnp.mean(values * values, axis=-1, keepdims=True)
    return values * lax.rsqrt(mean_sq + EPS)


def ring_pairs(count, step):
    order = [2 * r if r < count // 2 else 2 * (count - 1 - r) + 1 for r in range(count)]
    return [(order[r], order[(r + step) % count]) for r in range(count)]


def ring_gather(block, count, beside=None):
    up, down = ring_pairs(count, 1), ring_pairs(count, -1)
    below = above = block
    blocks = [block]
    for _ in range((count - 1) // 2):
        below, above = lax.ppermute(below, "mp", up), lax.ppermute(above, "mp", down)
        blocks += [below, above]
    made = None
    if beside is not None:
        made = beside(blocks)
        below, above, made = lax.optimization_barrier((below, above, made))
    cut = -(-block.shape[0] // 32) * 16
    blocks += [lax.ppermute(below[:cut], "mp", up), lax.ppermute(above[cut:], "mp", down)]
    return blocks, made


def ring_owners(count):
    me = lax.axis_index("mp")
    place = jnp.where(me % 2 == 0, me // 2, count - 1 - me // 2)
    owners = [me]
    for step in range(1, count // 2 + 1):
        for shift in (-step, step):
            at = lax.rem(place + shift + count, count)
            owners.append(jnp.where(at < count // 2, 2 * at, 2 * (count - 1 - at) + 1))
    return owners[:count]


def row_ranges(blocks):
    last = len(blocks) - 2
    return [(i, 0) for i in range(last + 1)] + [(last, blocks[last].shape[0])]


def group_gather(block, size, after=None):
    blocks = {0: block}
    bit = size // 2
    while bit:
        pairs = [(i, i ^ bit) for i in range(size)]
        for k in list(blocks):
            sent = blocks[k]
            if k and after is not None:
                sent, _ = lax.optimization_barrier((sent, after))
            blocks[k ^ bit] = lax.ppermute(sent, "group", pairs)
        bit //= 2
    return [blocks[k] for k in range(size)]


def pack_kernel(joined, expand, out):
    columns, high = joined.shape[1], expand.shape[0]
    folds = joined.shape[0] // high
    fold = expand.shape[1] // folds
    out[:, :columns] = joined[...].astype(jnp.bfloat16)
    for i in range(folds):
        out[i * high : (i + 1) * high, columns:] = expand[:, i * fold : (i + 1) * fold].astype(jnp.bfloat16)


def norm_kernel(arrivals, slots, normed, digits):
    normed[...] = row_norm(arrivals[...].astype(jnp.float32)).astype(jnp.bfloat16)
    rows = slots.shape[1]
    bits = jnp.concatenate([slots[...] & 255, slots[...] >> 8], axis=0).astype(jnp.float32)
    bits = jnp.concatenate([bits, jnp.zeros((14, rows), jnp.float32)], axis=0)
    digits[...] = jnp.zeros_like(digits)
    digits[:, :rows] = bits.astype(jnp.bfloat16)


def multiply(tokens, starts, blocks, columns):
    total = None
    for start, block in zip(starts, blocks):
        span = pl.ds(pl.multiple_of(start, 128), block.shape[0])
        left = jnp.concatenate([token[:, span] for token in tokens], axis=0)
        product = jnp.dot(left, block[:, :columns], preferred_element_type=jnp.float32)
        total = product if total is None else total + product
    return total


def early_kernel(count, size, *refs):
    tokens, blocks, total = refs[:size], refs[size:-1], refs[-1]
    depth = blocks[0].shape[0]
    total[...] = multiply(tokens, [owner * depth for owner in ring_owners(count)], blocks, total.shape[1])


def proj_kernel(count, size, early, *refs):
    tokens, refs = refs[:size], refs[size:]
    blocks, refs = refs[: count + 1], refs[count + 1 :]
    depth = blocks[0].shape[0]
    owners = ring_owners(count)
    starts = [owners[i] * depth + offset for i, offset in row_ranges(blocks)]
    if early:
        total, refs = refs[0], refs[1:]
        outs, expand = refs[:size], refs[size]
        rows, columns = outs[0].shape
        proj = total[...] + multiply(tokens, starts[early:], blocks[early:], columns)
    else:
        outs, expand, weight = refs[:size], refs[size], refs[size + 1]
        rows, columns = outs[0].shape
        for start, block in zip(starts, blocks):
            length = block.shape[0]
            weight[pl.ds(pl.multiple_of(start, length), length), :] = block[:, :columns]
        products = [jnp.dot(token[...], weight[...], preferred_element_type=jnp.float32) for token in tokens]
        proj = jnp.concatenate(products, axis=0)
    at = lax.axis_index("group") * columns + lax.broadcasted_iota(jnp.int32, (1, columns), 1)
    proj = proj * jnp.where(at < QCOLS, HDIM**-0.5, 1.0).astype(jnp.float32)
    for i, out in enumerate(outs):
        out[...] = proj[i * rows : (i + 1) * rows].astype(jnp.bfloat16)
    high = expand.shape[0] // count
    for i, owner in enumerate(owners):
        parts = []
        for block in blocks[i:] if i == count - 1 else blocks[i : i + 1]:
            parts += [block[j * high : (j + 1) * high, columns:] for j in range(block.shape[0] // high)]
        expand[pl.ds(pl.multiple_of(owner * high, high), high), :] = jnp.concatenate(parts, axis=1)


def assemble_kernel(size, digits, *refs):
    products, (query, block, proj) = refs[:size], refs[size:]
    group = lax.axis_index("group")
    for i, product in enumerate(products):
        proj[group ^ i] = product[...]
    whole = jnp.concatenate([proj[i] for i in range(size)], axis=1)
    query[...] = whole[:, :QCOLS]
    rows = query.shape[0]
    block[:rows] = row_norm(whole[:, QCOLS:].astype(jnp.float32)).astype(jnp.bfloat16)
    block[rows:] = digits[...]


def position_of(block, rows):
    digits = block[block.shape[0] - 16 :, :rows].astype(jnp.float32)
    return digits[1:2] * 256.0 + digits[:1]


def bias_of(lengths, own, others):
    rows = own.shape[0] - 16
    same = lax.broadcasted_iota(jnp.int32, (rows, rows), 0) == lax.broadcasted_iota(jnp.int32, (rows, rows), 1)
    position = jnp.sum(jnp.where(same, position_of(own, rows), 0.0), axis=1, keepdims=True).astype(jnp.int32)
    start = jnp.zeros_like(position)
    end = 0
    for i in range(lengths.shape[1]):
        end = end + lengths[0, i]
        start = jnp.where(position >= end, end, start)
    others = others.astype(jnp.int32)
    return jnp.where((others <= position) & (others >= start), 0.0, NEGATIVE)


def score(turned, latent, scores):
    half = turned.shape[0] // 2
    for at in (0, half):
        scores[at : at + half] = lax.dot_general(
            turned[at : at + half], latent[...], (((1,), (1,)), ((), ())), preferred_element_type=jnp.float32
        )


def start_kernel(count, size, lengths, query, *refs):
    blocks, refs = refs[: count - 3], refs[count - 3 :]
    expands, refs = refs[:size], refs[size:]
    turned, value, peaks, sums, summed, latent, expand, scores, probs = refs
    rows = query.shape[0]
    for i, block in enumerate(blocks):
        latent[i * rows : (i + 1) * rows, :] = block[:rows]
    bias = bias_of(lengths, blocks[0], jnp.concatenate([position_of(block, rows) for block in blocks], axis=1))
    width = expands[0].shape[1]
    for i, block in enumerate(expands):
        at = (lax.axis_index("group") ^ i) * width
        expand[:, pl.ds(pl.multiple_of(at, width), width)] = block[...]
    for head in range(HEADS):
        value[:, head * HDIM : (head + 1) * HDIM] = expand[:, (2 * head + 1) * HDIM : (2 * head + 2) * HDIM]
        product = lax.dot_general(
            query[:, head * HDIM : (head + 1) * HDIM],
            expand[:, head * 2 * HDIM : (2 * head + 1) * HDIM],
            (((1,), (1,)), ((), ())),
            preferred_element_type=jnp.float32,
        )
        turned[head * rows : (head + 1) * rows] = (product * LOG2_E).astype(jnp.bfloat16)
    score(turned, latent, scores)
    half = HEADS * rows // 2
    for begin in (0, half):
        for at in range(begin, begin + half, TILE):
            here = at % rows
            part = scores[at : at + TILE] + bias[here : here + TILE]
            peak = jnp.max(part, axis=-1, keepdims=True)
            weights = jnp.exp2(part - peak)
            peaks[at : at + TILE] = jnp.broadcast_to(peak, (TILE, HDIM))
            sums[at : at + TILE] = jnp.broadcast_to(jnp.sum(weights, axis=-1, keepdims=True), (TILE, HDIM))
            probs[at : at + TILE] = weights.astype(jnp.bfloat16)
        summed[begin : begin + half] = jnp.dot(
            probs[begin : begin + half], latent[...], preferred_element_type=jnp.float32
        )


def absorb(biases, scores, latent, peaks, sums, summed):
    part = scores + biases
    peak = jnp.maximum(peaks, jnp.max(part, axis=-1, keepdims=True))
    weights = jnp.exp2(part - jnp.concatenate([peak] * (part.shape[1] // HDIM), axis=1))
    factor = jnp.exp2(peaks - peak)
    sums = sums * factor + jnp.sum(weights, axis=-1, keepdims=True)
    update = jnp.dot(weights.astype(jnp.bfloat16), latent, preferred_element_type=jnp.float32)
    return peak, sums, summed * jnp.concatenate([factor] * (summed.shape[1] // HDIM), axis=1) + update


def more_kernel(lengths, own, turned, peaks, sums, summed, *refs):
    blocks, (new_peaks, new_sums, new_summed, latent, scores) = refs[:-5], refs[-5:]
    rows, half = own.shape[0] - 16, turned.shape[0] // 2
    for i, block in enumerate(blocks):
        latent[i * rows : (i + 1) * rows, :] = block[:rows]
    bias = bias_of(lengths, own, jnp.concatenate([position_of(block, rows) for block in blocks], axis=1))
    biases = jnp.concatenate([bias] * (HEADS // 2), axis=0)
    score(turned, latent, scores)
    for begin in (0, half):
        here = slice(begin, begin + half)
        new_peaks[here], new_sums[here], new_summed[here] = absorb(
            biases, scores[here], latent[...], peaks[here], sums[here], summed[here]
        )


def attend_kernel(lengths, own, turned, value, peaks, sums, summed, *refs):
    pieces, (out, latent, scores) = refs[:-3], refs[-3:]
    rows, done = out.shape[0], 0
    for piece in pieces:
        length = min(rows - done, piece.shape[0])
        latent[done : done + length] = piece[:length]
        done += length
    bias = bias_of(lengths, own, position_of(pieces[-1], rows))
    score(turned, latent, scores)
    some = HEADS // 2
    biases = jnp.concatenate([bias] * some, axis=0)
    for first in range(0, HEADS, some):
        here = slice(first * rows, (first + some) * rows)
        _, total, update = absorb(biases, scores[here], latent[...], peaks[here], sums[here], summed[here])
        update = update.astype(jnp.bfloat16)
        for i in range(some):
            columns = slice((first + i) * HDIM, (first + i + 1) * HDIM)
            outcome = jnp.dot(update[i * rows : (i + 1) * rows], value[:, columns], preferred_element_type=jnp.float32)
            out[:, columns] = (outcome / total[i * rows : (i + 1) * rows]).astype(jnp.bfloat16)


def body(arrivals, slots, lengths, w_joined, w_expand):
    count, size = lax.axis_size("mp"), lax.axis_size("group")
    rows, depth = arrivals.shape
    columns, rank = w_joined.shape[1], w_expand.shape[0] * count
    own_columns = w_expand.shape[1]

    weights = pl.pallas_call(
        pack_kernel,
        out_shape=jax.ShapeDtypeStruct(
            (w_joined.shape[0], columns + own_columns * w_expand.shape[0] // w_joined.shape[0]), jnp.bfloat16
        ),
        in_specs=[VMEM, VMEM],
        out_specs=VMEM,
        compiler_params=grant(16),
        name="pack",
    )(w_joined, w_expand)
    blocks, _ = ring_gather(weights, count)
    arrivals, _ = lax.optimization_barrier((arrivals, weights))
    normed, digits = pl.pallas_call(
        norm_kernel,
        out_shape=[
            jax.ShapeDtypeStruct((rows, depth), jnp.bfloat16),
            jax.ShapeDtypeStruct((16, rank), jnp.bfloat16),
        ],
        in_specs=[VMEM, VMEM],
        out_specs=[VMEM, VMEM],
        compiler_params=grant(16),
        cost_estimate=pl.CostEstimate(flops=NORM_COST * rows * depth, bytes_accessed=NORM_COST * rows * depth, transcendentals=rows),
        name="norm",
    )(arrivals, slots.reshape(1, rows))
    tokens = group_gather(normed, size, blocks[-4:-2])
    early = 0 if w_joined.shape[0] // 2 % 128 else count - 3
    total = []
    if early:
        total = [
            pl.pallas_call(
                functools.partial(early_kernel, count, size),
                out_shape=jax.ShapeDtypeStruct((size * rows, columns), jnp.float32),
                in_specs=[VMEM] * (size + early),
                out_specs=VMEM,
                compiler_params=grant(16),
                cost_estimate=pl.CostEstimate(
                    flops=2 * size * rows * depth * columns, bytes_accessed=4 * depth * columns, transcendentals=0
                ),
                name="project_early",
            )(*tokens, *blocks[:early])
        ]
    *projs, own_expand = pl.pallas_call(
        functools.partial(proj_kernel, count, size, early),
        out_shape=[jax.ShapeDtypeStruct((rows, columns), jnp.bfloat16)] * size
        + [jax.ShapeDtypeStruct((rank, own_columns), jnp.bfloat16)],
        in_specs=[VMEM] * (size + count + 1 + len(total)),
        out_specs=[VMEM] * (size + 1),
        scratch_shapes=[] if early else [pltpu.VMEM((depth, columns), jnp.bfloat16)],
        compiler_params=grant(16),
        cost_estimate=pl.CostEstimate(
            flops=2 * size * rows * depth * columns, bytes_accessed=4 * depth * columns, transcendentals=0
        ),
        name="project",
    )(*tokens, *blocks, *total)

    back = [projs[0]]
    for k in range(1, size):
        back.append(lax.ppermute(projs[k], "group", [(i, i ^ k) for i in range(size)]))
    own_expand, _ = lax.optimization_barrier((own_expand, back[1:]))
    query, block = pl.pallas_call(
        functools.partial(assemble_kernel, size),
        out_shape=[
            jax.ShapeDtypeStruct((rows, QCOLS), jnp.bfloat16),
            jax.ShapeDtypeStruct((rows + 16, rank), jnp.bfloat16),
        ],
        in_specs=[VMEM] * (size + 1),
        out_specs=[VMEM, VMEM],
        scratch_shapes=[pltpu.VMEM((size, rows, columns), jnp.bfloat16)],
        compiler_params=grant(16),
        name="assemble",
    )(digits, *back)
    total, early = count * rows, count - 3
    needed = grant(8 + total * HEADS * rows * 8 // (1024 * 1024))
    state = [jax.ShapeDtypeStruct((HEADS * rows, width), jnp.float32) for width in (HDIM, HDIM, rank)]

    def cost(blocks):
        return pl.CostEstimate(
            flops=4 * blocks * rows * rank * QCOLS,
            bytes_accessed=8 * QCOLS * rank,
            transcendentals=HEADS * rows * blocks * rows,
        )

    def attend_start(blocks):
        expands = group_gather(own_expand, size, blocks[3:5])
        return pl.pallas_call(
            functools.partial(start_kernel, count, size),
            out_shape=[
                jax.ShapeDtypeStruct((HEADS * rows, rank), jnp.bfloat16),
                jax.ShapeDtypeStruct((rank, QCOLS), jnp.bfloat16),
                *state,
            ],
            in_specs=[SMEM] + [VMEM] * (1 + early + size),
            out_specs=[VMEM] * 5,
            scratch_shapes=[
                pltpu.VMEM((early * rows, rank), jnp.bfloat16),
                pltpu.VMEM((rank, 2 * QCOLS), jnp.bfloat16),
                pltpu.VMEM((HEADS * rows, early * rows), jnp.float32),
                pltpu.VMEM((HEADS * rows, early * rows), jnp.bfloat16),
            ],
            compiler_params=needed,
            cost_estimate=cost(early),
            name="attend_start",
        )(lengths, query, *blocks[:early], *expands)

    lat_blocks, (turned, value, *running) = ring_gather(block, count, attend_start)
    running = pl.pallas_call(
        more_kernel,
        out_shape=state,
        in_specs=[SMEM] + [VMEM] * 7,
        out_specs=[VMEM] * 3,
        scratch_shapes=[
            pltpu.VMEM((2 * rows, rank), jnp.bfloat16),
            pltpu.VMEM((HEADS * rows, 2 * rows), jnp.float32),
        ],
        compiler_params=grant(16),
        cost_estimate=cost(2),
        name="attend_more",
    )(lengths, block, turned, *running, *lat_blocks[early : count - 1])
    last = lat_blocks[count - 1 :]
    return pl.pallas_call(
        attend_kernel,
        out_shape=jax.ShapeDtypeStruct((rows, QCOLS), jnp.bfloat16),
        in_specs=[SMEM] + [VMEM] * (6 + len(last)),
        out_specs=VMEM,
        scratch_shapes=[
            pltpu.VMEM((rows, rank), jnp.bfloat16),
            pltpu.VMEM((HEADS * rows, rows), jnp.float32),
        ],
        compiler_params=grant(16),
        cost_estimate=cost(2),
        name="attend",
    )(lengths, block, turned, value, *running, *last)


def solution(mesh):
    in_specs = (
        P(("group", "mp"), None),
        P(("group", "mp")),
        P("group", None),
        P("mp", "group"),
        P("mp", "group"),
    )
    out_specs = P(("group", "mp"), None)
    return jax.shard_map(body, mesh=mesh, in_specs=in_specs, out_specs=out_specs, check_vma=False)
```

```python
import functools

import jax
import jax.numpy as jnp
from jax import lax
from jax.experimental import pallas as pl
from jax.experimental.pallas import tpu as pltpu
from jax.sharding import PartitionSpec as P

HEADS = 8
HDIM = 128
QCOLS = HEADS * HDIM

EPS = 1e-06
NEGATIVE = -1e30
LOG2_E = 1.4426950408889634
TILE = 16
NORM_COST = 64
VMEM = pl.BlockSpec(memory_space=pltpu.VMEM)
SMEM = pl.BlockSpec(memory_space=pltpu.SMEM)


def grant(mib):
    return pltpu.CompilerParams(vmem_limit_bytes=mib * 1024 * 1024)


def row_norm(values):
    mean_sq = jnp.mean(values * values, axis=-1, keepdims=True)
    return values * lax.rsqrt(mean_sq + EPS)


def ring_pairs(count, step):
    order = [2 * r if r < count // 2 else 2 * (count - 1 - r) + 1 for r in range(count)]
    return [(order[r], order[(r + step) % count]) for r in range(count)]


def ring_gather(block, count, beside=None):
    up, down = ring_pairs(count, 1), ring_pairs(count, -1)
    below = above = block
    blocks = [block]
    for _ in range((count - 1) // 2):
        below, above = lax.ppermute(below, "mp", up), lax.ppermute(above, "mp", down)
        blocks += [below, above]
    made = None
    if beside is not None:
        made = beside(blocks)
        below, above, made = lax.optimization_barrier((below, above, made))
    cut = -(-block.shape[0] // 32) * 16
    blocks += [lax.ppermute(below[:cut], "mp", up), lax.ppermute(above[cut:], "mp", down)]
    return blocks, made


def ring_owners(count):
    me = lax.axis_index("mp")
    place = jnp.where(me % 2 == 0, me // 2, count - 1 - me // 2)
    owners = [me]
    for step in range(1, count // 2 + 1):
        for shift in (-step, step):
            at = lax.rem(place + shift + count, count)
            owners.append(jnp.where(at < count // 2, 2 * at, 2 * (count - 1 - at) + 1))
    return owners[:count]


def row_ranges(blocks):
    last = len(blocks) - 2
    return [(i, 0) for i in range(last + 1)] + [(last, blocks[last].shape[0])]


def group_gather(block, size, after=None):
    blocks = {0: block}
    bit = size // 2
    while bit:
        pairs = [(i, i ^ bit) for i in range(size)]
        for k in list(blocks):
            sent = blocks[k]
            if k and after is not None:
                sent, _ = lax.optimization_barrier((sent, after))
            blocks[k ^ bit] = lax.ppermute(sent, "group", pairs)
        bit //= 2
    return [blocks[k] for k in range(size)]


def pack_kernel(joined, expand, out):
    columns, high = joined.shape[1], expand.shape[0]
    folds = joined.shape[0] // high
    fold = expand.shape[1] // folds
    out[:, :columns] = joined[...].astype(jnp.bfloat16)
    for i in range(folds):
        out[i * high : (i + 1) * high, columns:] = expand[:, i * fold : (i + 1) * fold].astype(jnp.bfloat16)


def norm_kernel(arrivals, slots, normed, digits):
    normed[...] = row_norm(arrivals[...].astype(jnp.float32)).astype(jnp.bfloat16)
    rows = slots.shape[1]
    bits = jnp.concatenate([slots[...] & 255, slots[...] >> 8], axis=0).astype(jnp.float32)
    bits = jnp.concatenate([bits, jnp.zeros((14, rows), jnp.float32)], axis=0)
    digits[...] = jnp.zeros_like(digits)
    digits[:, :rows] = bits.astype(jnp.bfloat16)


def multiply(tokens, starts, blocks, columns):
    total = None
    for start, block in zip(starts, blocks):
        span = pl.ds(pl.multiple_of(start, 128), block.shape[0])
        left = jnp.concatenate([token[:, span] for token in tokens], axis=0)
        product = jnp.dot(left, block[:, :columns], preferred_element_type=jnp.float32)
        total = product if total is None else total + product
    return total


def early_kernel(count, size, *refs):
    tokens, blocks, total = refs[:size], refs[size:-1], refs[-1]
    depth = blocks[0].shape[0]
    total[...] = multiply(tokens, [owner * depth for owner in ring_owners(count)], blocks, total.shape[1])


def proj_kernel(count, size, early, *refs):
    tokens, refs = refs[:size], refs[size:]
    blocks, refs = refs[: count + 1], refs[count + 1 :]
    depth = blocks[0].shape[0]
    owners = ring_owners(count)
    starts = [owners[i] * depth + offset for i, offset in row_ranges(blocks)]
    if early:
        total, refs = refs[0], refs[1:]
        outs, expand = refs[:size], refs[size]
        rows, columns = outs[0].shape
        proj = total[...] + multiply(tokens, starts[early:], blocks[early:], columns)
    else:
        outs, expand, weight = refs[:size], refs[size], refs[size + 1]
        rows, columns = outs[0].shape
        for start, block in zip(starts, blocks):
            length = block.shape[0]
            weight[pl.ds(pl.multiple_of(start, length), length), :] = block[:, :columns]
        products = [jnp.dot(token[...], weight[...], preferred_element_type=jnp.float32) for token in tokens]
        proj = jnp.concatenate(products, axis=0)
    at = lax.axis_index("group") * columns + lax.broadcasted_iota(jnp.int32, (1, columns), 1)
    proj = proj * jnp.where(at < QCOLS, HDIM**-0.5, 1.0).astype(jnp.float32)
    for i, out in enumerate(outs):
        out[...] = proj[i * rows : (i + 1) * rows].astype(jnp.bfloat16)
    high = expand.shape[0] // count
    for i, owner in enumerate(owners):
        parts = []
        for block in blocks[i:] if i == count - 1 else blocks[i : i + 1]:
            parts += [block[j * high : (j + 1) * high, columns:] for j in range(block.shape[0] // high)]
        expand[pl.ds(pl.multiple_of(owner * high, high), high), :] = jnp.concatenate(parts, axis=1)


def assemble_kernel(size, digits, *refs):
    products, (query, block, proj) = refs[:size], refs[size:]
    group = lax.axis_index("group")
    for i, product in enumerate(products):
        proj[group ^ i] = product[...]
    whole = jnp.concatenate([proj[i] for i in range(size)], axis=1)
    query[...] = whole[:, :QCOLS]
    rows = query.shape[0]
    block[:rows] = row_norm(whole[:, QCOLS:].astype(jnp.float32)).astype(jnp.bfloat16)
    block[rows:] = digits[...]


def position_of(block, rows):
    digits = block[block.shape[0] - 16 :, :rows].astype(jnp.float32)
    return digits[1:2] * 256.0 + digits[:1]


def bias_of(lengths, own, others):
    rows = own.shape[0] - 16
    same = lax.broadcasted_iota(jnp.int32, (rows, rows), 0) == lax.broadcasted_iota(jnp.int32, (rows, rows), 1)
    position = jnp.sum(jnp.where(same, position_of(own, rows), 0.0), axis=1, keepdims=True).astype(jnp.int32)
    start = jnp.zeros_like(position)
    end = 0
    for i in range(lengths.shape[1]):
        end = end + lengths[0, i]
        start = jnp.where(position >= end, end, start)
    others = others.astype(jnp.int32)
    return jnp.where((others <= position) & (others >= start), 0.0, NEGATIVE)


def score(turned, latent, scores):
    half = turned.shape[0] // 2
    for at in (0, half):
        scores[at : at + half] = lax.dot_general(
            turned[at : at + half], latent[...], (((1,), (1,)), ((), ())), preferred_element_type=jnp.float32
        )


def start_kernel(count, size, lengths, query, *refs):
    blocks, refs = refs[: count - 3], refs[count - 3 :]
    expands, refs = refs[:size], refs[size:]
    turned, value, peaks, sums, summed, latent, expand, scores, probs = refs
    rows = query.shape[0]
    for i, block in enumerate(blocks):
        latent[i * rows : (i + 1) * rows, :] = block[:rows]
    bias = bias_of(lengths, blocks[0], jnp.concatenate([position_of(block, rows) for block in blocks], axis=1))
    width = expands[0].shape[1]
    for i, block in enumerate(expands):
        at = (lax.axis_index("group") ^ i) * width
        expand[:, pl.ds(pl.multiple_of(at, width), width)] = block[...]
    for head in range(HEADS):
        value[:, head * HDIM : (head + 1) * HDIM] = expand[:, (2 * head + 1) * HDIM : (2 * head + 2) * HDIM]
        product = lax.dot_general(
            query[:, head * HDIM : (head + 1) * HDIM],
            expand[:, head * 2 * HDIM : (2 * head + 1) * HDIM],
            (((1,), (1,)), ((), ())),
            preferred_element_type=jnp.float32,
        )
        turned[head * rows : (head + 1) * rows] = (product * LOG2_E).astype(jnp.bfloat16)
    score(turned, latent, scores)
    half = HEADS * rows // 2
    for begin in (0, half):
        for at in range(begin, begin + half, TILE):
            here = at % rows
            part = scores[at : at + TILE] + bias[here : here + TILE]
            peak = jnp.max(part, axis=-1, keepdims=True)
            weights = jnp.exp2(part - peak)
            peaks[at : at + TILE] = jnp.broadcast_to(peak, (TILE, HDIM))
            sums[at : at + TILE] = jnp.broadcast_to(jnp.sum(weights, axis=-1, keepdims=True), (TILE, HDIM))
            probs[at : at + TILE] = weights.astype(jnp.bfloat16)
        summed[begin : begin + half] = jnp.dot(
            probs[begin : begin + half], latent[...], preferred_element_type=jnp.float32
        )


def absorb(biases, scores, peaks, sums):
    part = scores + biases
    peak = jnp.maximum(peaks, jnp.max(part, axis=-1, keepdims=True))
    weights = jnp.exp2(part - jnp.concatenate([peak] * (part.shape[1] // HDIM), axis=1))
    factor = jnp.exp2(peaks - peak)
    return weights.astype(jnp.bfloat16), factor, peak, sums * factor + jnp.sum(weights, axis=-1, keepdims=True)


def more_kernel(lengths, own, turned, value, peaks, sums, summed, *refs):
    blocks, (new_peaks, new_sums, outcome, latent, scores) = refs[:-5], refs[-5:]
    rows, some = own.shape[0] - 16, HEADS // 2
    for i, block in enumerate(blocks):
        latent[i * rows : (i + 1) * rows, :] = block[:rows]
    bias = bias_of(lengths, own, jnp.concatenate([position_of(block, rows) for block in blocks], axis=1))
    biases = jnp.concatenate([bias] * some, axis=0)
    score(turned, latent, scores)
    for first in range(0, HEADS, some):
        here = slice(first * rows, (first + some) * rows)
        probs, factor, new_peaks[here], new_sums[here] = absorb(biases, scores[here], peaks[here], sums[here])
        update = jnp.dot(probs, latent[...], preferred_element_type=jnp.float32)
        update = update + summed[here] * jnp.concatenate([factor] * (summed.shape[1] // HDIM), axis=1)
        update = update.astype(jnp.bfloat16)
        for i in range(some):
            head = first + i
            outcome[head * rows : (head + 1) * rows] = jnp.dot(
                update[i * rows : (i + 1) * rows],
                value[:, head * HDIM : (head + 1) * HDIM],
                preferred_element_type=jnp.float32,
            )


def attend_kernel(lengths, own, turned, value, peaks, sums, before, *refs):
    pieces, (out, latent, scores) = refs[:-3], refs[-3:]
    rows, done = out.shape[0], 0
    for piece in pieces:
        length = min(rows - done, piece.shape[0])
        latent[done : done + length] = piece[:length]
        done += length
    bias = bias_of(lengths, own, position_of(pieces[-1], rows))
    score(turned, latent, scores)
    values = jnp.dot(latent[...], value[...], preferred_element_type=jnp.float32).astype(jnp.bfloat16)
    some = HEADS // 2
    biases = jnp.concatenate([bias] * some, axis=0)
    for first in range(0, HEADS, some):
        here = slice(first * rows, (first + some) * rows)
        probs, factor, _, total = absorb(biases, scores[here], peaks[here], sums[here])
        kept = before[here] * factor
        for i in range(some):
            columns = slice((first + i) * HDIM, (first + i + 1) * HDIM)
            mine = slice(i * rows, (i + 1) * rows)
            outcome = kept[mine] + jnp.dot(probs[mine], values[:, columns], preferred_element_type=jnp.float32)
            out[:, columns] = (outcome / total[mine]).astype(jnp.bfloat16)


def body(arrivals, slots, lengths, w_joined, w_expand):
    count, size = lax.axis_size("mp"), lax.axis_size("group")
    rows, depth = arrivals.shape
    columns, rank = w_joined.shape[1], w_expand.shape[0] * count
    own_columns = w_expand.shape[1]

    weights = pl.pallas_call(
        pack_kernel,
        out_shape=jax.ShapeDtypeStruct(
            (w_joined.shape[0], columns + own_columns * w_expand.shape[0] // w_joined.shape[0]), jnp.bfloat16
        ),
        in_specs=[VMEM, VMEM],
        out_specs=VMEM,
        compiler_params=grant(16),
        name="pack",
    )(w_joined, w_expand)
    blocks, _ = ring_gather(weights, count)
    arrivals, _ = lax.optimization_barrier((arrivals, weights))
    normed, digits = pl.pallas_call(
        norm_kernel,
        out_shape=[
            jax.ShapeDtypeStruct((rows, depth), jnp.bfloat16),
            jax.ShapeDtypeStruct((16, rank), jnp.bfloat16),
        ],
        in_specs=[VMEM, VMEM],
        out_specs=[VMEM, VMEM],
        compiler_params=grant(16),
        cost_estimate=pl.CostEstimate(flops=NORM_COST * rows * depth, bytes_accessed=NORM_COST * rows * depth, transcendentals=rows),
        name="norm",
    )(arrivals, slots.reshape(1, rows))
    tokens = group_gather(normed, size, blocks[-4:-2])
    early = 0 if w_joined.shape[0] // 2 % 128 else count - 3
    total = []
    if early:
        total = [
            pl.pallas_call(
                functools.partial(early_kernel, count, size),
                out_shape=jax.ShapeDtypeStruct((size * rows, columns), jnp.float32),
                in_specs=[VMEM] * (size + early),
                out_specs=VMEM,
                compiler_params=grant(16),
                cost_estimate=pl.CostEstimate(
                    flops=2 * size * rows * depth * columns, bytes_accessed=4 * depth * columns, transcendentals=0
                ),
                name="project_early",
            )(*tokens, *blocks[:early])
        ]
    *projs, own_expand = pl.pallas_call(
        functools.partial(proj_kernel, count, size, early),
        out_shape=[jax.ShapeDtypeStruct((rows, columns), jnp.bfloat16)] * size
        + [jax.ShapeDtypeStruct((rank, own_columns), jnp.bfloat16)],
        in_specs=[VMEM] * (size + count + 1 + len(total)),
        out_specs=[VMEM] * (size + 1),
        scratch_shapes=[] if early else [pltpu.VMEM((depth, columns), jnp.bfloat16)],
        compiler_params=grant(16),
        cost_estimate=pl.CostEstimate(
            flops=2 * size * rows * depth * columns, bytes_accessed=4 * depth * columns, transcendentals=0
        ),
        name="project",
    )(*tokens, *blocks, *total)

    back = [projs[0]]
    for k in range(1, size):
        back.append(lax.ppermute(projs[k], "group", [(i, i ^ k) for i in range(size)]))
    own_expand, _ = lax.optimization_barrier((own_expand, back[size // 2]))
    query, block = pl.pallas_call(
        functools.partial(assemble_kernel, size),
        out_shape=[
            jax.ShapeDtypeStruct((rows, QCOLS), jnp.bfloat16),
            jax.ShapeDtypeStruct((rows + 16, rank), jnp.bfloat16),
        ],
        in_specs=[VMEM] * (size + 1),
        out_specs=[VMEM, VMEM],
        scratch_shapes=[pltpu.VMEM((size, rows, columns), jnp.bfloat16)],
        compiler_params=grant(16),
        name="assemble",
    )(digits, *back)
    total, early = count * rows, count - 3
    needed = grant(8 + total * HEADS * rows * 8 // (1024 * 1024))
    state = [jax.ShapeDtypeStruct((HEADS * rows, width), jnp.float32) for width in (HDIM, HDIM, rank)]

    def cost(blocks):
        return pl.CostEstimate(
            flops=4 * blocks * rows * rank * QCOLS,
            bytes_accessed=8 * QCOLS * rank,
            transcendentals=HEADS * rows * blocks * rows,
        )

    def attend_start(blocks):
        expands = group_gather(own_expand, size, blocks[3:5])
        return pl.pallas_call(
            functools.partial(start_kernel, count, size),
            out_shape=[
                jax.ShapeDtypeStruct((HEADS * rows, rank), jnp.bfloat16),
                jax.ShapeDtypeStruct((rank, QCOLS), jnp.bfloat16),
                *state,
            ],
            in_specs=[SMEM] + [VMEM] * (1 + early + size),
            out_specs=[VMEM] * 5,
            scratch_shapes=[
                pltpu.VMEM((early * rows, rank), jnp.bfloat16),
                pltpu.VMEM((rank, 2 * QCOLS), jnp.bfloat16),
                pltpu.VMEM((HEADS * rows, early * rows), jnp.float32),
                pltpu.VMEM((HEADS * rows, early * rows), jnp.bfloat16),
            ],
            compiler_params=needed,
            cost_estimate=cost(early),
            name="attend_start",
        )(lengths, query, *blocks[:early], *expands)

    lat_blocks, (turned, value, *running) = ring_gather(block, count, attend_start)
    running = pl.pallas_call(
        more_kernel,
        out_shape=[jax.ShapeDtypeStruct((HEADS * rows, HDIM), jnp.float32)] * 3,
        in_specs=[SMEM] + [VMEM] * 8,
        out_specs=[VMEM] * 3,
        scratch_shapes=[
            pltpu.VMEM((2 * rows, rank), jnp.bfloat16),
            pltpu.VMEM((HEADS * rows, 2 * rows), jnp.float32),
        ],
        compiler_params=grant(16),
        cost_estimate=cost(2),
        name="attend_more",
    )(lengths, block, turned, value, *running, *lat_blocks[early : count - 1])
    last = lat_blocks[count - 1 :]
    return pl.pallas_call(
        attend_kernel,
        out_shape=jax.ShapeDtypeStruct((rows, QCOLS), jnp.bfloat16),
        in_specs=[SMEM] + [VMEM] * (6 + len(last)),
        out_specs=VMEM,
        scratch_shapes=[
            pltpu.VMEM((rows, rank), jnp.bfloat16),
            pltpu.VMEM((HEADS * rows, rows), jnp.float32),
        ],
        compiler_params=grant(16),
        cost_estimate=cost(2),
        name="attend",
    )(lengths, block, turned, value, *running, *last)


def solution(mesh):
    in_specs = (
        P(("group", "mp"), None),
        P(("group", "mp")),
        P("group", None),
        P("mp", "group"),
        P("mp", "group"),
    )
    out_specs = P(("group", "mp"), None)
    return jax.shard_map(body, mesh=mesh, in_specs=in_specs, out_specs=out_specs, check_vma=False)
```

```python
import functools

import jax
import jax.numpy as jnp
from jax import lax
from jax.experimental import pallas as pl
from jax.experimental.pallas import tpu as pltpu
from jax.sharding import PartitionSpec as P

HEADS = 8
HDIM = 128
QCOLS = HEADS * HDIM

EPS = 1e-06
NEGATIVE = -1e30
LOG2_E = 1.4426950408889634
TILE = 16
NORM_COST = 64
VMEM = pl.BlockSpec(memory_space=pltpu.VMEM)
SMEM = pl.BlockSpec(memory_space=pltpu.SMEM)


def grant(mib):
    return pltpu.CompilerParams(vmem_limit_bytes=mib * 1024 * 1024)


def row_norm(values):
    mean_sq = jnp.mean(values * values, axis=-1, keepdims=True)
    return values * lax.rsqrt(mean_sq + EPS)


def ring_pairs(count, step):
    order = [2 * r if r < count // 2 else 2 * (count - 1 - r) + 1 for r in range(count)]
    return [(order[r], order[(r + step) % count]) for r in range(count)]


def ring_gather(block, count):
    up, down = ring_pairs(count, 1), ring_pairs(count, -1)
    below = above = block
    blocks = [block]
    for _ in range((count - 1) // 2):
        below, above = lax.ppermute(below, "mp", up), lax.ppermute(above, "mp", down)
        blocks += [below, above]
    cut = -(-block.shape[0] // 32) * 16
    return blocks + [lax.ppermute(below[:cut], "mp", up), lax.ppermute(above[cut:], "mp", down)]


def split_ring_gather(block, count, size, beside):
    up, down = ring_pairs(count, 1), ring_pairs(count, -1)
    below = above = block
    blocks = [block]
    for _ in range((count - 1) // 2):
        below, above = lax.ppermute(below, "mp", up), lax.ppermute(above, "mp", down)
        blocks += [below, above]
    made = beside(blocks)
    below, above, made = lax.optimization_barrier((below, above, made))
    last = jnp.where(lax.axis_index("group") % 2 == 0, below, above)
    pairs = [
        (group * count + source, group * count + target)
        for group in range(size)
        for source, target in (down if group % 2 else up)
    ]
    return blocks + [lax.ppermute(last, ("group", "mp"), pairs)], made


def ring_owners(count):
    me = lax.axis_index("mp")
    place = jnp.where(me % 2 == 0, me // 2, count - 1 - me // 2)
    owners = [me]
    for step in range(1, count // 2 + 1):
        for shift in (-step, step):
            at = lax.rem(place + shift + count, count)
            owners.append(jnp.where(at < count // 2, 2 * at, 2 * (count - 1 - at) + 1))
    return owners[:count]


def row_ranges(blocks):
    last = len(blocks) - 2
    return [(i, 0) for i in range(last + 1)] + [(last, blocks[last].shape[0])]


def group_gather(block, size, after=None):
    blocks = {0: block}
    bit = size // 2
    while bit:
        pairs = [(i, i ^ bit) for i in range(size)]
        for k in list(blocks):
            sent = blocks[k]
            if k and after is not None:
                sent, _ = lax.optimization_barrier((sent, after))
            blocks[k ^ bit] = lax.ppermute(sent, "group", pairs)
        bit //= 2
    return [blocks[k] for k in range(size)]


def pack_kernel(joined, expand, out):
    columns, high = joined.shape[1], expand.shape[0]
    folds = joined.shape[0] // high
    fold = expand.shape[1] // folds
    out[:, :columns] = joined[...].astype(jnp.bfloat16)
    for i in range(folds):
        out[i * high : (i + 1) * high, columns:] = expand[:, i * fold : (i + 1) * fold].astype(jnp.bfloat16)


def norm_kernel(arrivals, slots, normed, digits):
    normed[...] = row_norm(arrivals[...].astype(jnp.float32)).astype(jnp.bfloat16)
    rows = slots.shape[1]
    bits = jnp.concatenate([slots[...] & 255, slots[...] >> 8], axis=0).astype(jnp.float32)
    bits = jnp.concatenate([bits, jnp.zeros((14, rows), jnp.float32)], axis=0)
    digits[...] = jnp.zeros_like(digits)
    digits[:, :rows] = bits.astype(jnp.bfloat16)


def multiply(tokens, starts, blocks, columns):
    total = None
    for start, block in zip(starts, blocks):
        span = pl.ds(pl.multiple_of(start, 128), block.shape[0])
        left = jnp.concatenate([token[:, span] for token in tokens], axis=0)
        product = jnp.dot(left, block[:, :columns], preferred_element_type=jnp.float32)
        total = product if total is None else total + product
    return total


def early_kernel(count, size, *refs):
    tokens, blocks, total = refs[:size], refs[size:-1], refs[-1]
    depth = blocks[0].shape[0]
    total[...] = multiply(tokens, [owner * depth for owner in ring_owners(count)], blocks, total.shape[1])


def proj_kernel(count, size, early, *refs):
    tokens, refs = refs[:size], refs[size:]
    blocks, refs = refs[: count + 1], refs[count + 1 :]
    depth = blocks[0].shape[0]
    owners = ring_owners(count)
    starts = [owners[i] * depth + offset for i, offset in row_ranges(blocks)]
    if early:
        total, refs = refs[0], refs[1:]
        outs, expand = refs[:size], refs[size]
        rows, columns = outs[0].shape
        proj = total[...] + multiply(tokens, starts[early:], blocks[early:], columns)
    else:
        outs, expand, weight = refs[:size], refs[size], refs[size + 1]
        rows, columns = outs[0].shape
        for start, block in zip(starts, blocks):
            length = block.shape[0]
            weight[pl.ds(pl.multiple_of(start, length), length), :] = block[:, :columns]
        products = [jnp.dot(token[...], weight[...], preferred_element_type=jnp.float32) for token in tokens]
        proj = jnp.concatenate(products, axis=0)
    at = lax.axis_index("group") * columns + lax.broadcasted_iota(jnp.int32, (1, columns), 1)
    proj = proj * jnp.where(at < QCOLS, HDIM**-0.5, 1.0).astype(jnp.float32)
    for i, out in enumerate(outs):
        out[...] = proj[i * rows : (i + 1) * rows].astype(jnp.bfloat16)
    high = expand.shape[0] // count
    for i, owner in enumerate(owners):
        parts = []
        for block in blocks[i:] if i == count - 1 else blocks[i : i + 1]:
            parts += [block[j * high : (j + 1) * high, columns:] for j in range(block.shape[0] // high)]
        expand[pl.ds(pl.multiple_of(owner * high, high), high), :] = jnp.concatenate(parts, axis=1)


def assemble_kernel(size, digits, *refs):
    products, (query, block, proj) = refs[:size], refs[size:]
    group = lax.axis_index("group")
    for i, product in enumerate(products):
        proj[group ^ i] = product[...]
    whole = jnp.concatenate([proj[i] for i in range(size)], axis=1)
    query[...] = whole[:, :QCOLS]
    rows = query.shape[0]
    block[:rows] = row_norm(whole[:, QCOLS:].astype(jnp.float32)).astype(jnp.bfloat16)
    block[rows:] = digits[...]


def position_of(block, rows):
    digits = block[block.shape[0] - 16 :, :rows].astype(jnp.float32)
    return digits[1:2] * 256.0 + digits[:1]


def bias_of(lengths, own, others):
    rows = own.shape[0] - 16
    same = lax.broadcasted_iota(jnp.int32, (rows, rows), 0) == lax.broadcasted_iota(jnp.int32, (rows, rows), 1)
    position = jnp.sum(jnp.where(same, position_of(own, rows), 0.0), axis=1, keepdims=True).astype(jnp.int32)
    start = jnp.zeros_like(position)
    end = 0
    for i in range(lengths.shape[1]):
        end = end + lengths[0, i]
        start = jnp.where(position >= end, end, start)
    others = others.astype(jnp.int32)
    return jnp.where((others <= position) & (others >= start), 0.0, NEGATIVE)


def score(turned, latent, scores):
    half = turned.shape[0] // 2
    for at in (0, half):
        scores[at : at + half] = lax.dot_general(
            turned[at : at + half], latent[...], (((1,), (1,)), ((), ())), preferred_element_type=jnp.float32
        )


def start_kernel(count, size, lengths, query, *refs):
    blocks, refs = refs[: count - 3], refs[count - 3 :]
    expands, refs = refs[:size], refs[size:]
    turned, value, peaks, sums, summed, latent, expand, scores, probs = refs
    rows = query.shape[0]
    for i, block in enumerate(blocks):
        latent[i * rows : (i + 1) * rows, :] = block[:rows]
    bias = bias_of(lengths, blocks[0], jnp.concatenate([position_of(block, rows) for block in blocks], axis=1))
    width = expands[0].shape[1]
    for i, block in enumerate(expands):
        at = (lax.axis_index("group") ^ i) * width
        expand[:, pl.ds(pl.multiple_of(at, width), width)] = block[...]
    for head in range(HEADS):
        value[:, head * HDIM : (head + 1) * HDIM] = expand[:, (2 * head + 1) * HDIM : (2 * head + 2) * HDIM]
        product = lax.dot_general(
            query[:, head * HDIM : (head + 1) * HDIM],
            expand[:, head * 2 * HDIM : (2 * head + 1) * HDIM],
            (((1,), (1,)), ((), ())),
            preferred_element_type=jnp.float32,
        )
        turned[head * rows : (head + 1) * rows] = (product * LOG2_E).astype(jnp.bfloat16)
    score(turned, latent, scores)
    half = HEADS * rows // 2
    for begin in (0, half):
        for at in range(begin, begin + half, TILE):
            here = at % rows
            part = scores[at : at + TILE] + bias[here : here + TILE]
            peak = jnp.max(part, axis=-1, keepdims=True)
            weights = jnp.exp2(part - peak)
            peaks[at : at + TILE] = jnp.broadcast_to(peak, (TILE, HDIM))
            sums[at : at + TILE] = jnp.broadcast_to(jnp.sum(weights, axis=-1, keepdims=True), (TILE, HDIM))
            probs[at : at + TILE] = weights.astype(jnp.bfloat16)
        summed[begin : begin + half] = jnp.dot(
            probs[begin : begin + half], latent[...], preferred_element_type=jnp.float32
        )


def absorb(biases, scores, peaks, sums):
    part = scores + biases
    peak = jnp.maximum(peaks, jnp.max(part, axis=-1, keepdims=True))
    weights = jnp.exp2(part - jnp.concatenate([peak] * (part.shape[1] // HDIM), axis=1))
    factor = jnp.exp2(peaks - peak)
    return weights.astype(jnp.bfloat16), factor, peak, sums * factor + jnp.sum(weights, axis=-1, keepdims=True)


def more_kernel(lengths, own, turned, value, peaks, sums, summed, *refs):
    blocks, (new_peaks, new_sums, outcome, latent, scores) = refs[:-5], refs[-5:]
    rows, some = own.shape[0] - 16, HEADS // 2
    for i, block in enumerate(blocks):
        latent[i * rows : (i + 1) * rows, :] = block[:rows]
    bias = bias_of(lengths, own, jnp.concatenate([position_of(block, rows) for block in blocks], axis=1))
    biases = jnp.concatenate([bias] * some, axis=0)
    score(turned, latent, scores)
    for first in range(0, HEADS, some):
        here = slice(first * rows, (first + some) * rows)
        probs, factor, new_peaks[here], new_sums[here] = absorb(biases, scores[here], peaks[here], sums[here])
        update = jnp.dot(probs, latent[...], preferred_element_type=jnp.float32)
        update = update + summed[here] * jnp.concatenate([factor] * (summed.shape[1] // HDIM), axis=1)
        update = update.astype(jnp.bfloat16)
        for i in range(some):
            head = first + i
            outcome[head * rows : (head + 1) * rows] = jnp.dot(
                update[i * rows : (i + 1) * rows],
                value[:, head * HDIM : (head + 1) * HDIM],
                preferred_element_type=jnp.float32,
            )


def attend_kernel(lengths, own, turned, value, peaks, sums, before, last, out, scores):
    rows = out.shape[0]
    latent = last[:rows]
    bias = bias_of(lengths, own, position_of(last, rows))
    score(turned, latent, scores)
    values = jnp.dot(latent, value[...], preferred_element_type=jnp.float32).astype(jnp.bfloat16)
    some = HEADS // 2
    biases = jnp.concatenate([bias] * some, axis=0)
    for first in range(0, HEADS, some):
        here = slice(first * rows, (first + some) * rows)
        probs, factor, _, total = absorb(biases, scores[here], peaks[here], sums[here])
        kept = before[here] * factor
        for i in range(some):
            columns = slice((first + i) * HDIM, (first + i + 1) * HDIM)
            mine = slice(i * rows, (i + 1) * rows)
            outcome = kept[mine] + jnp.dot(probs[mine], values[:, columns], preferred_element_type=jnp.float32)
            out[:, columns] = (outcome / total[mine]).astype(jnp.bfloat16)


def body(arrivals, slots, lengths, w_joined, w_expand):
    count, size = lax.axis_size("mp"), lax.axis_size("group")
    rows, depth = arrivals.shape
    columns, rank = w_joined.shape[1], w_expand.shape[0] * count
    own_columns = w_expand.shape[1]

    weights = pl.pallas_call(
        pack_kernel,
        out_shape=jax.ShapeDtypeStruct(
            (w_joined.shape[0], columns + own_columns * w_expand.shape[0] // w_joined.shape[0]), jnp.bfloat16
        ),
        in_specs=[VMEM, VMEM],
        out_specs=VMEM,
        compiler_params=grant(16),
        name="pack",
    )(w_joined, w_expand)
    blocks = ring_gather(weights, count)
    arrivals, _ = lax.optimization_barrier((arrivals, weights))
    normed, digits = pl.pallas_call(
        norm_kernel,
        out_shape=[
            jax.ShapeDtypeStruct((rows, depth), jnp.bfloat16),
            jax.ShapeDtypeStruct((16, rank), jnp.bfloat16),
        ],
        in_specs=[VMEM, VMEM],
        out_specs=[VMEM, VMEM],
        compiler_params=grant(16),
        cost_estimate=pl.CostEstimate(flops=NORM_COST * rows * depth, bytes_accessed=NORM_COST * rows * depth, transcendentals=rows),
        name="norm",
    )(arrivals, slots.reshape(1, rows))
    tokens = group_gather(normed, size, blocks[-4:-2])
    early = 0 if w_joined.shape[0] // 2 % 128 else count - 3
    total = []
    if early:
        total = [
            pl.pallas_call(
                functools.partial(early_kernel, count, size),
                out_shape=jax.ShapeDtypeStruct((size * rows, columns), jnp.float32),
                in_specs=[VMEM] * (size + early),
                out_specs=VMEM,
                compiler_params=grant(16),
                cost_estimate=pl.CostEstimate(
                    flops=2 * size * rows * depth * columns, bytes_accessed=4 * depth * columns, transcendentals=0
                ),
                name="project_early",
            )(*tokens, *blocks[:early])
        ]
    *projs, own_expand = pl.pallas_call(
        functools.partial(proj_kernel, count, size, early),
        out_shape=[jax.ShapeDtypeStruct((rows, columns), jnp.bfloat16)] * size
        + [jax.ShapeDtypeStruct((rank, own_columns), jnp.bfloat16)],
        in_specs=[VMEM] * (size + count + 1 + len(total)),
        out_specs=[VMEM] * (size + 1),
        scratch_shapes=[] if early else [pltpu.VMEM((depth, columns), jnp.bfloat16)],
        compiler_params=grant(16),
        cost_estimate=pl.CostEstimate(
            flops=2 * size * rows * depth * columns, bytes_accessed=4 * depth * columns, transcendentals=0
        ),
        name="project",
    )(*tokens, *blocks, *total)

    back = [projs[0]]
    for k in range(1, size):
        back.append(lax.ppermute(projs[k], "group", [(i, i ^ k) for i in range(size)]))
    own_expand, _ = lax.optimization_barrier((own_expand, back[1:]))
    query, block = pl.pallas_call(
        functools.partial(assemble_kernel, size),
        out_shape=[
            jax.ShapeDtypeStruct((rows, QCOLS), jnp.bfloat16),
            jax.ShapeDtypeStruct((rows + 16, rank), jnp.bfloat16),
        ],
        in_specs=[VMEM] * (size + 1),
        out_specs=[VMEM, VMEM],
        scratch_shapes=[pltpu.VMEM((size, rows, columns), jnp.bfloat16)],
        compiler_params=grant(16),
        name="assemble",
    )(digits, *back)
    total, early = count * rows, count - 3
    needed = grant(8 + total * HEADS * rows * 8 // (1024 * 1024))
    state = [jax.ShapeDtypeStruct((HEADS * rows, width), jnp.float32) for width in (HDIM, HDIM, rank)]

    def cost(blocks):
        return pl.CostEstimate(
            flops=4 * blocks * rows * rank * QCOLS,
            bytes_accessed=8 * QCOLS * rank,
            transcendentals=HEADS * rows * blocks * rows,
        )

    def attend_start(blocks):
        expands = group_gather(own_expand, size, blocks[3:5])
        return pl.pallas_call(
            functools.partial(start_kernel, count, size),
            out_shape=[
                jax.ShapeDtypeStruct((HEADS * rows, rank), jnp.bfloat16),
                jax.ShapeDtypeStruct((rank, QCOLS), jnp.bfloat16),
                *state,
            ],
            in_specs=[SMEM] + [VMEM] * (1 + early + size),
            out_specs=[VMEM] * 5,
            scratch_shapes=[
                pltpu.VMEM((early * rows, rank), jnp.bfloat16),
                pltpu.VMEM((rank, 2 * QCOLS), jnp.bfloat16),
                pltpu.VMEM((HEADS * rows, early * rows), jnp.float32),
                pltpu.VMEM((HEADS * rows, early * rows), jnp.bfloat16),
            ],
            compiler_params=needed,
            cost_estimate=cost(early),
            name="attend_start",
        )(lengths, query, *blocks[:early], *expands)

    lat_blocks, (turned, value, *running) = split_ring_gather(block, count, size, attend_start)
    running = pl.pallas_call(
        more_kernel,
        out_shape=[jax.ShapeDtypeStruct((HEADS * rows, HDIM), jnp.float32)] * 3,
        in_specs=[SMEM] + [VMEM] * 8,
        out_specs=[VMEM] * 3,
        scratch_shapes=[
            pltpu.VMEM((2 * rows, rank), jnp.bfloat16),
            pltpu.VMEM((HEADS * rows, 2 * rows), jnp.float32),
        ],
        compiler_params=grant(16),
        cost_estimate=cost(2),
        name="attend_more",
    )(lengths, block, turned, value, *running, *lat_blocks[early : count - 1])
    return pl.pallas_call(
        attend_kernel,
        out_shape=jax.ShapeDtypeStruct((rows, QCOLS), jnp.bfloat16),
        in_specs=[SMEM] + [VMEM] * 7,
        out_specs=VMEM,
        scratch_shapes=[pltpu.VMEM((HEADS * rows, rows), jnp.float32)],
        compiler_params=grant(16),
        cost_estimate=cost(2),
        name="attend",
    )(lengths, block, turned, value, *running, lat_blocks[-1])


def solution(mesh):
    in_specs = (
        P(("group", "mp"), None),
        P(("group", "mp")),
        P("group", None),
        P("mp", "group"),
        P("mp", "group"),
    )
    out_specs = P(("group", "mp"), None)
    return jax.shard_map(body, mesh=mesh, in_specs=in_specs, out_specs=out_specs, check_vma=False)
```

```python
import functools

import jax
import jax.numpy as jnp
from jax import lax
from jax.experimental import pallas as pl
from jax.experimental.pallas import tpu as pltpu
from jax.sharding import PartitionSpec as P

HEADS = 8
HDIM = 128
QCOLS = HEADS * HDIM

EPS = 1e-06
NEGATIVE = -1e30
LOG2_E = 1.4426950408889634
TILE = 16
NORM_COST = 64
VMEM = pl.BlockSpec(memory_space=pltpu.VMEM)
SMEM = pl.BlockSpec(memory_space=pltpu.SMEM)


def grant(mib):
    return pltpu.CompilerParams(vmem_limit_bytes=mib * 1024 * 1024)


def row_norm(values):
    mean_sq = jnp.mean(values * values, axis=-1, keepdims=True)
    return values * lax.rsqrt(mean_sq + EPS)


def ring_pairs(count, step):
    order = [2 * r if r < count // 2 else 2 * (count - 1 - r) + 1 for r in range(count)]
    return [(order[r], order[(r + step) % count]) for r in range(count)]


def ring_gather(block, count, size, beside=lambda blocks: ()):
    up, down = ring_pairs(count, 1), ring_pairs(count, -1)
    below = above = block
    blocks = [block]
    for _ in range((count - 1) // 2):
        below, above = lax.ppermute(below, "mp", up), lax.ppermute(above, "mp", down)
        blocks += [below, above]
    below, above, made = lax.optimization_barrier((below, above, beside(blocks)))
    last = jnp.where(lax.axis_index("group") % 2 == 0, below, above)
    pairs = [
        (group * count + source, group * count + target)
        for group in range(size)
        for source, target in (down if group % 2 else up)
    ]
    return blocks + [lax.ppermute(last, ("group", "mp"), pairs)], made


def ring_owners(count):
    me = lax.axis_index("mp")
    place = jnp.where(me % 2 == 0, me // 2, count - 1 - me // 2)
    owners = [me]
    for step in range(1, count // 2 + 1):
        for shift in (-step, step):
            at = lax.rem(place + shift + count, count)
            owners.append(jnp.where(at < count // 2, 2 * at, 2 * (count - 1 - at) + 1))
    return owners[:count]


def group_gather(block, size, after=None):
    blocks = {0: block}
    bit = size // 2
    while bit:
        pairs = [(i, i ^ bit) for i in range(size)]
        for k in list(blocks):
            sent = blocks[k]
            if k and after is not None:
                sent, _ = lax.optimization_barrier((sent, after))
            blocks[k ^ bit] = lax.ppermute(sent, "group", pairs)
        bit //= 2
    return [blocks[k] for k in range(size)]


def pack_kernel(joined, expand, out):
    columns, high = joined.shape[1], expand.shape[0]
    folds = joined.shape[0] // high
    fold = expand.shape[1] // folds
    out[:, :columns] = joined[...].astype(jnp.bfloat16)
    for i in range(folds):
        out[i * high : (i + 1) * high, columns:] = expand[:, i * fold : (i + 1) * fold].astype(jnp.bfloat16)


def norm_kernel(arrivals, slots, normed, digits):
    normed[...] = row_norm(arrivals[...].astype(jnp.float32)).astype(jnp.bfloat16)
    rows = slots.shape[1]
    bits = jnp.concatenate([slots[...] & 255, slots[...] >> 8], axis=0).astype(jnp.float32)
    bits = jnp.concatenate([bits, jnp.zeros((14, rows), jnp.float32)], axis=0)
    digits[...] = jnp.zeros_like(digits)
    digits[:, :rows] = bits.astype(jnp.bfloat16)


def multiply(tokens, starts, blocks, columns):
    total = None
    for start, block in zip(starts, blocks):
        span = pl.ds(pl.multiple_of(start, 128), block.shape[0])
        left = jnp.concatenate([token[:, span] for token in tokens], axis=0)
        product = jnp.dot(left, block[:, :columns], preferred_element_type=jnp.float32)
        total = product if total is None else total + product
    return total


def early_kernel(count, size, *refs):
    tokens, blocks, total = refs[:size], refs[size:-1], refs[-1]
    depth = blocks[0].shape[0]
    total[...] = multiply(tokens, [owner * depth for owner in ring_owners(count)], blocks, total.shape[1])


def proj_kernel(count, size, early, *refs):
    tokens, refs = refs[:size], refs[size:]
    blocks, refs = refs[:count], refs[count:]
    depth = blocks[0].shape[0]
    owners = ring_owners(count)
    starts = [owner * depth for owner in owners]
    if early:
        total, refs = refs[0], refs[1:]
        outs, expand = refs[:size], refs[size]
        rows, columns = outs[0].shape
        proj = total[...] + multiply(tokens, starts[early:], blocks[early:], columns)
    else:
        outs, expand, weight = refs[:size], refs[size], refs[size + 1]
        rows, columns = outs[0].shape
        for start, block in zip(starts, blocks):
            length = block.shape[0]
            weight[pl.ds(pl.multiple_of(start, length), length), :] = block[:, :columns]
        products = [jnp.dot(token[...], weight[...], preferred_element_type=jnp.float32) for token in tokens]
        proj = jnp.concatenate(products, axis=0)
    at = lax.axis_index("group") * columns + lax.broadcasted_iota(jnp.int32, (1, columns), 1)
    proj = proj * jnp.where(at < QCOLS, HDIM**-0.5, 1.0).astype(jnp.float32)
    for i, out in enumerate(outs):
        out[...] = proj[i * rows : (i + 1) * rows].astype(jnp.bfloat16)
    high = expand.shape[0] // count
    for owner, block in zip(owners, blocks):
        parts = [block[i * high : (i + 1) * high, columns:] for i in range(depth // high)]
        expand[pl.ds(pl.multiple_of(owner * high, high), high), :] = jnp.concatenate(parts, axis=1)


def assemble_kernel(size, digits, *refs):
    products, (query, block, proj) = refs[:size], refs[size:]
    group = lax.axis_index("group")
    for i, product in enumerate(products):
        proj[group ^ i] = product[...]
    whole = jnp.concatenate([proj[i] for i in range(size)], axis=1)
    query[...] = whole[:, :QCOLS]
    rows = query.shape[0]
    block[:rows] = row_norm(whole[:, QCOLS:].astype(jnp.float32)).astype(jnp.bfloat16)
    block[rows:] = digits[...]


def position_of(block, rows):
    digits = block[block.shape[0] - 16 :, :rows].astype(jnp.float32)
    return digits[1:2] * 256.0 + digits[:1]


def bias_of(lengths, own, others):
    rows = own.shape[0] - 16
    same = lax.broadcasted_iota(jnp.int32, (rows, rows), 0) == lax.broadcasted_iota(jnp.int32, (rows, rows), 1)
    position = jnp.sum(jnp.where(same, position_of(own, rows), 0.0), axis=1, keepdims=True).astype(jnp.int32)
    start = jnp.zeros_like(position)
    end = 0
    for i in range(lengths.shape[1]):
        end = end + lengths[0, i]
        start = jnp.where(position >= end, end, start)
    others = others.astype(jnp.int32)
    return jnp.where((others <= position) & (others >= start), 0.0, NEGATIVE)


def score(turned, latent, scores):
    half = turned.shape[0] // 2
    for at in (0, half):
        scores[at : at + half] = lax.dot_general(
            turned[at : at + half], latent[...], (((1,), (1,)), ((), ())), preferred_element_type=jnp.float32
        )


def start_kernel(count, size, lengths, query, *refs):
    blocks, refs = refs[: count - 3], refs[count - 3 :]
    expands, refs = refs[:size], refs[size:]
    turned, value, peaks, sums, summed, latent, expand, scores, probs = refs
    rows = query.shape[0]
    for i, block in enumerate(blocks):
        latent[i * rows : (i + 1) * rows, :] = block[:rows]
    bias = bias_of(lengths, blocks[0], jnp.concatenate([position_of(block, rows) for block in blocks], axis=1))
    width = expands[0].shape[1]
    for i, block in enumerate(expands):
        at = (lax.axis_index("group") ^ i) * width
        expand[:, pl.ds(pl.multiple_of(at, width), width)] = block[...]
    for head in range(HEADS):
        value[:, head * HDIM : (head + 1) * HDIM] = expand[:, (2 * head + 1) * HDIM : (2 * head + 2) * HDIM]
        product = lax.dot_general(
            query[:, head * HDIM : (head + 1) * HDIM],
            expand[:, head * 2 * HDIM : (2 * head + 1) * HDIM],
            (((1,), (1,)), ((), ())),
            preferred_element_type=jnp.float32,
        )
        turned[head * rows : (head + 1) * rows] = (product * LOG2_E).astype(jnp.bfloat16)
    score(turned, latent, scores)
    half = HEADS * rows // 2
    for begin in (0, half):
        for at in range(begin, begin + half, TILE):
            here = at % rows
            part = scores[at : at + TILE] + bias[here : here + TILE]
            peak = jnp.max(part, axis=-1, keepdims=True)
            weights = jnp.exp2(part - peak)
            peaks[at : at + TILE] = jnp.broadcast_to(peak, (TILE, HDIM))
            sums[at : at + TILE] = jnp.broadcast_to(jnp.sum(weights, axis=-1, keepdims=True), (TILE, HDIM))
            probs[at : at + TILE] = weights.astype(jnp.bfloat16)
        summed[begin : begin + half] = jnp.dot(
            probs[begin : begin + half], latent[...], preferred_element_type=jnp.float32
        )


def absorb(biases, scores, peaks, sums):
    part = scores + biases
    peak = jnp.maximum(peaks, jnp.max(part, axis=-1, keepdims=True))
    weights = jnp.exp2(part - jnp.concatenate([peak] * (part.shape[1] // HDIM), axis=1))
    factor = jnp.exp2(peaks - peak)
    return weights.astype(jnp.bfloat16), factor, peak, sums * factor + jnp.sum(weights, axis=-1, keepdims=True)


def more_kernel(lengths, own, turned, value, peaks, sums, summed, *refs):
    blocks, (new_peaks, new_sums, outcome, latent, scores) = refs[:-5], refs[-5:]
    rows, some = own.shape[0] - 16, HEADS // 2
    for i, block in enumerate(blocks):
        latent[i * rows : (i + 1) * rows, :] = block[:rows]
    bias = bias_of(lengths, own, jnp.concatenate([position_of(block, rows) for block in blocks], axis=1))
    biases = jnp.concatenate([bias] * some, axis=0)
    score(turned, latent, scores)
    for first in range(0, HEADS, some):
        here = slice(first * rows, (first + some) * rows)
        probs, factor, new_peaks[here], new_sums[here] = absorb(biases, scores[here], peaks[here], sums[here])
        update = jnp.dot(probs, latent[...], preferred_element_type=jnp.float32)
        update = update + summed[here] * jnp.concatenate([factor] * (summed.shape[1] // HDIM), axis=1)
        update = update.astype(jnp.bfloat16)
        for i in range(some):
            head = first + i
            outcome[head * rows : (head + 1) * rows] = jnp.dot(
                update[i * rows : (i + 1) * rows],
                value[:, head * HDIM : (head + 1) * HDIM],
                preferred_element_type=jnp.float32,
            )


def attend_kernel(lengths, own, turned, value, peaks, sums, before, last, out, scores):
    rows = out.shape[0]
    latent = last[:rows]
    bias = bias_of(lengths, own, position_of(last, rows))
    score(turned, latent, scores)
    values = jnp.dot(latent, value[...], preferred_element_type=jnp.float32).astype(jnp.bfloat16)
    some = HEADS // 2
    biases = jnp.concatenate([bias] * some, axis=0)
    for first in range(0, HEADS, some):
        here = slice(first * rows, (first + some) * rows)
        probs, factor, _, total = absorb(biases, scores[here], peaks[here], sums[here])
        kept = before[here] * factor
        for i in range(some):
            columns = slice((first + i) * HDIM, (first + i + 1) * HDIM)
            mine = slice(i * rows, (i + 1) * rows)
            outcome = kept[mine] + jnp.dot(probs[mine], values[:, columns], preferred_element_type=jnp.float32)
            out[:, columns] = (outcome / total[mine]).astype(jnp.bfloat16)


def body(arrivals, slots, lengths, w_joined, w_expand):
    count, size = lax.axis_size("mp"), lax.axis_size("group")
    rows, depth = arrivals.shape
    columns, rank = w_joined.shape[1], w_expand.shape[0] * count
    own_columns = w_expand.shape[1]

    weights = pl.pallas_call(
        pack_kernel,
        out_shape=jax.ShapeDtypeStruct(
            (w_joined.shape[0], columns + own_columns * w_expand.shape[0] // w_joined.shape[0]), jnp.bfloat16
        ),
        in_specs=[VMEM, VMEM],
        out_specs=VMEM,
        compiler_params=grant(16),
        name="pack",
    )(w_joined, w_expand)
    blocks, _ = ring_gather(weights, count, size)
    arrivals, _ = lax.optimization_barrier((arrivals, weights))
    normed, digits = pl.pallas_call(
        norm_kernel,
        out_shape=[
            jax.ShapeDtypeStruct((rows, depth), jnp.bfloat16),
            jax.ShapeDtypeStruct((16, rank), jnp.bfloat16),
        ],
        in_specs=[VMEM, VMEM],
        out_specs=[VMEM, VMEM],
        compiler_params=grant(16),
        cost_estimate=pl.CostEstimate(flops=NORM_COST * rows * depth, bytes_accessed=NORM_COST * rows * depth, transcendentals=rows),
        name="norm",
    )(arrivals, slots.reshape(1, rows))
    tokens = group_gather(normed, size, blocks[-3:-1])
    early = 0 if w_joined.shape[0] % 128 else count - 1
    total = []
    if early:
        total = [
            pl.pallas_call(
                functools.partial(early_kernel, count, size),
                out_shape=jax.ShapeDtypeStruct((size * rows, columns), jnp.float32),
                in_specs=[VMEM] * (size + early),
                out_specs=VMEM,
                compiler_params=grant(16),
                cost_estimate=pl.CostEstimate(
                    flops=2 * size * rows * depth * columns, bytes_accessed=4 * depth * columns, transcendentals=0
                ),
                name="project_early",
            )(*tokens, *blocks[:early])
        ]
    *projs, own_expand = pl.pallas_call(
        functools.partial(proj_kernel, count, size, early),
        out_shape=[jax.ShapeDtypeStruct((rows, columns), jnp.bfloat16)] * size
        + [jax.ShapeDtypeStruct((rank, own_columns), jnp.bfloat16)],
        in_specs=[VMEM] * (size + count + len(total)),
        out_specs=[VMEM] * (size + 1),
        scratch_shapes=[] if early else [pltpu.VMEM((depth, columns), jnp.bfloat16)],
        compiler_params=grant(16),
        cost_estimate=pl.CostEstimate(
            flops=2 * size * rows * depth * columns, bytes_accessed=4 * depth * columns, transcendentals=0
        ),
        name="project",
    )(*tokens, *blocks, *total)

    back = [projs[0]]
    for k in range(1, size):
        back.append(lax.ppermute(projs[k], "group", [(i, i ^ k) for i in range(size)]))
    own_expand, _ = lax.optimization_barrier((own_expand, back[1:]))
    query, block = pl.pallas_call(
        functools.partial(assemble_kernel, size),
        out_shape=[
            jax.ShapeDtypeStruct((rows, QCOLS), jnp.bfloat16),
            jax.ShapeDtypeStruct((rows + 16, rank), jnp.bfloat16),
        ],
        in_specs=[VMEM] * (size + 1),
        out_specs=[VMEM, VMEM],
        scratch_shapes=[pltpu.VMEM((size, rows, columns), jnp.bfloat16)],
        compiler_params=grant(16),
        name="assemble",
    )(digits, *back)
    total, early = count * rows, count - 3
    needed = grant(8 + total * HEADS * rows * 8 // (1024 * 1024))
    state = [jax.ShapeDtypeStruct((HEADS * rows, width), jnp.float32) for width in (HDIM, HDIM, rank)]

    def cost(blocks):
        return pl.CostEstimate(
            flops=4 * blocks * rows * rank * QCOLS,
            bytes_accessed=8 * QCOLS * rank,
            transcendentals=HEADS * rows * blocks * rows,
        )

    def attend_start(blocks):
        expands = group_gather(own_expand, size, blocks[3:5])
        return pl.pallas_call(
            functools.partial(start_kernel, count, size),
            out_shape=[
                jax.ShapeDtypeStruct((HEADS * rows, rank), jnp.bfloat16),
                jax.ShapeDtypeStruct((rank, QCOLS), jnp.bfloat16),
                *state,
            ],
            in_specs=[SMEM] + [VMEM] * (1 + early + size),
            out_specs=[VMEM] * 5,
            scratch_shapes=[
                pltpu.VMEM((early * rows, rank), jnp.bfloat16),
                pltpu.VMEM((rank, 2 * QCOLS), jnp.bfloat16),
                pltpu.VMEM((HEADS * rows, early * rows), jnp.float32),
                pltpu.VMEM((HEADS * rows, early * rows), jnp.bfloat16),
            ],
            compiler_params=needed,
            cost_estimate=cost(early),
            name="attend_start",
        )(lengths, query, *blocks[:early], *expands)

    lat_blocks, (turned, value, *running) = ring_gather(block, count, size, attend_start)
    running = pl.pallas_call(
        more_kernel,
        out_shape=[jax.ShapeDtypeStruct((HEADS * rows, HDIM), jnp.float32)] * 3,
        in_specs=[SMEM] + [VMEM] * 8,
        out_specs=[VMEM] * 3,
        scratch_shapes=[
            pltpu.VMEM((2 * rows, rank), jnp.bfloat16),
            pltpu.VMEM((HEADS * rows, 2 * rows), jnp.float32),
        ],
        compiler_params=grant(16),
        cost_estimate=cost(2),
        name="attend_more",
    )(lengths, block, turned, value, *running, *lat_blocks[early : count - 1])
    return pl.pallas_call(
        attend_kernel,
        out_shape=jax.ShapeDtypeStruct((rows, QCOLS), jnp.bfloat16),
        in_specs=[SMEM] + [VMEM] * 7,
        out_specs=VMEM,
        scratch_shapes=[pltpu.VMEM((HEADS * rows, rows), jnp.float32)],
        compiler_params=grant(16),
        cost_estimate=cost(2),
        name="attend",
    )(lengths, block, turned, value, *running, lat_blocks[-1])


def solution(mesh):
    in_specs = (
        P(("group", "mp"), None),
        P(("group", "mp")),
        P("group", None),
        P("mp", "group"),
        P("mp", "group"),
    )
    out_specs = P(("group", "mp"), None)
    return jax.shard_map(body, mesh=mesh, in_specs=in_specs, out_specs=out_specs, check_vma=False)
```

```python
import functools

import jax
import jax.numpy as jnp
from jax import lax
from jax.experimental import pallas as pl
from jax.experimental.pallas import tpu as pltpu
from jax.sharding import PartitionSpec as P

HEADS = 8
HDIM = 128
QCOLS = HEADS * HDIM

EPS = 1e-06
NEGATIVE = -1e30
LOG2_E = 1.4426950408889634
TILE = 16
NORM_COST = 64
VMEM = pl.BlockSpec(memory_space=pltpu.VMEM)
SMEM = pl.BlockSpec(memory_space=pltpu.SMEM)


def grant(mib):
    return pltpu.CompilerParams(vmem_limit_bytes=mib * 1024 * 1024)


def row_norm(values):
    mean_sq = jnp.mean(values * values, axis=-1, keepdims=True)
    return values * lax.rsqrt(mean_sq + EPS)


def ring_pairs(count, step):
    order = [2 * r if r < count // 2 else 2 * (count - 1 - r) + 1 for r in range(count)]
    return [(order[r], order[(r + step) % count]) for r in range(count)]


def ring_gather(block, count):
    up, down = ring_pairs(count, 1), ring_pairs(count, -1)
    below = above = block
    blocks = [block]
    for _ in range((count - 1) // 2):
        below, above = lax.ppermute(below, "mp", up), lax.ppermute(above, "mp", down)
        blocks += [below, above]
    cut = -(-block.shape[0] // 32) * 16
    return blocks + [lax.ppermute(below[:cut], "mp", up), lax.ppermute(above[cut:], "mp", down)]


def split_ring_gather(block, count, size, beside):
    up, down = ring_pairs(count, 1), ring_pairs(count, -1)
    below = above = block
    blocks = [block]
    for _ in range((count - 1) // 2):
        below, above = lax.ppermute(below, "mp", up), lax.ppermute(above, "mp", down)
        blocks += [below, above]
    made = beside(blocks)
    below, above, made = lax.optimization_barrier((below, above, made))
    last = jnp.where(lax.axis_index("group") % 2 == 0, below, above)
    pairs = [
        (group * count + source, group * count + target)
        for group in range(size)
        for source, target in (down if group % 2 else up)
    ]
    return blocks + [lax.ppermute(last, ("group", "mp"), pairs)], made


def ring_owners(count):
    me = lax.axis_index("mp")
    place = jnp.where(me % 2 == 0, me // 2, count - 1 - me // 2)
    owners = [me]
    for step in range(1, count // 2 + 1):
        for shift in (-step, step):
            at = lax.rem(place + shift + count, count)
            owners.append(jnp.where(at < count // 2, 2 * at, 2 * (count - 1 - at) + 1))
    return owners[:count]


def row_ranges(blocks):
    last = len(blocks) - 2
    return [(i, 0) for i in range(last + 1)] + [(last, blocks[last].shape[0])]


def group_gather(block, size, after=None):
    blocks = {0: block}
    bit = size // 2
    while bit:
        pairs = [(i, i ^ bit) for i in range(size)]
        for k in list(blocks):
            sent = blocks[k]
            if k and after is not None:
                sent, _ = lax.optimization_barrier((sent, after))
            blocks[k ^ bit] = lax.ppermute(sent, "group", pairs)
        bit //= 2
    return [blocks[k] for k in range(size)]


def norm_kernel(arrivals, slots, normed, digits):
    normed[...] = row_norm(arrivals[...].astype(jnp.float32)).astype(jnp.bfloat16)
    rows = slots.shape[1]
    bits = jnp.concatenate([slots[...] & 255, slots[...] >> 8], axis=0).astype(jnp.float32)
    bits = jnp.concatenate([bits, jnp.zeros((14, rows), jnp.float32)], axis=0)
    digits[...] = jnp.zeros_like(digits)
    digits[:, :rows] = bits.astype(jnp.bfloat16)


def multiply(tokens, starts, blocks, columns):
    total = None
    for start, block in zip(starts, blocks):
        span = pl.ds(pl.multiple_of(start, 128), block.shape[0])
        left = jnp.concatenate([token[:, span] for token in tokens], axis=0)
        product = jnp.dot(left, block[:, :columns], preferred_element_type=jnp.float32)
        total = product if total is None else total + product
    return total


def early_kernel(count, size, *refs):
    tokens, blocks, total = refs[:size], refs[size:-1], refs[-1]
    depth = blocks[0].shape[0]
    total[...] = multiply(tokens, [owner * depth for owner in ring_owners(count)], blocks, total.shape[1])


def proj_kernel(count, size, early, *refs):
    tokens, refs = refs[:size], refs[size:]
    blocks, refs = refs[: count + 1], refs[count + 1 :]
    depth = blocks[0].shape[0]
    owners = ring_owners(count)
    starts = [owners[i] * depth + offset for i, offset in row_ranges(blocks)]
    if early:
        total, refs = refs[0], refs[1:]
        outs = refs[:size]
        rows, columns = outs[0].shape
        proj = total[...] + multiply(tokens, starts[early:], blocks[early:], columns)
    else:
        outs, weight = refs[:size], refs[size]
        rows, columns = outs[0].shape
        for start, block in zip(starts, blocks):
            length = block.shape[0]
            weight[pl.ds(pl.multiple_of(start, length), length), :] = block[:, :columns]
        products = [jnp.dot(token[...], weight[...], preferred_element_type=jnp.float32) for token in tokens]
        proj = jnp.concatenate(products, axis=0)
    at = lax.axis_index("group") * columns + lax.broadcasted_iota(jnp.int32, (1, columns), 1)
    proj = proj * jnp.where(at < QCOLS, HDIM**-0.5, 1.0).astype(jnp.float32)
    for i, out in enumerate(outs):
        out[...] = proj[i * rows : (i + 1) * rows].astype(jnp.bfloat16)


def assemble_kernel(size, digits, *refs):
    products, (query, block, proj) = refs[:size], refs[size:]
    group = lax.axis_index("group")
    for i, product in enumerate(products):
        proj[group ^ i] = product[...]
    whole = jnp.concatenate([proj[i] for i in range(size)], axis=1)
    query[...] = whole[:, :QCOLS]
    rows = query.shape[0]
    block[:rows] = row_norm(whole[:, QCOLS:].astype(jnp.float32)).astype(jnp.bfloat16)
    block[rows:] = digits[...]


def position_of(block, rows):
    digits = block[block.shape[0] - 16 :, :rows].astype(jnp.float32)
    return digits[1:2] * 256.0 + digits[:1]


def bias_of(lengths, own, others):
    rows = own.shape[0] - 16
    same = lax.broadcasted_iota(jnp.int32, (rows, rows), 0) == lax.broadcasted_iota(jnp.int32, (rows, rows), 1)
    position = jnp.sum(jnp.where(same, position_of(own, rows), 0.0), axis=1, keepdims=True).astype(jnp.int32)
    start = jnp.zeros_like(position)
    end = 0
    for i in range(lengths.shape[1]):
        end = end + lengths[0, i]
        start = jnp.where(position >= end, end, start)
    others = others.astype(jnp.int32)
    return jnp.where((others <= position) & (others >= start), 0.0, NEGATIVE)


def score(turned, latent, scores):
    half = turned.shape[0] // 2
    for at in (0, half):
        scores[at : at + half] = lax.dot_general(
            turned[at : at + half], latent[...], (((1,), (1,)), ((), ())), preferred_element_type=jnp.float32
        )


def start_kernel(count, size, lengths, query, *refs):
    blocks, refs = refs[: count - 3], refs[count - 3 :]
    expands, refs = refs[:size], refs[size:]
    turned, value, peaks, sums, summed, latent, expand, scores, probs = refs
    rows = query.shape[0]
    for i, block in enumerate(blocks):
        latent[i * rows : (i + 1) * rows, :] = block[:rows]
    bias = bias_of(lengths, blocks[0], jnp.concatenate([position_of(block, rows) for block in blocks], axis=1))
    width = expands[0].shape[1]
    for i, block in enumerate(expands):
        at = (lax.axis_index("group") ^ i) * width
        expand[:, pl.ds(pl.multiple_of(at, width), width)] = block[...]
    for head in range(HEADS):
        value[:, head * HDIM : (head + 1) * HDIM] = expand[:, (2 * head + 1) * HDIM : (2 * head + 2) * HDIM]
        product = lax.dot_general(
            query[:, head * HDIM : (head + 1) * HDIM],
            expand[:, head * 2 * HDIM : (2 * head + 1) * HDIM],
            (((1,), (1,)), ((), ())),
            preferred_element_type=jnp.float32,
        )
        turned[head * rows : (head + 1) * rows] = (product * LOG2_E).astype(jnp.bfloat16)
    score(turned, latent, scores)
    half = HEADS * rows // 2
    for begin in (0, half):
        for at in range(begin, begin + half, TILE):
            here = at % rows
            part = scores[at : at + TILE] + bias[here : here + TILE]
            peak = jnp.max(part, axis=-1, keepdims=True)
            weights = jnp.exp2(part - peak)
            peaks[at : at + TILE] = jnp.broadcast_to(peak, (TILE, HDIM))
            sums[at : at + TILE] = jnp.broadcast_to(jnp.sum(weights, axis=-1, keepdims=True), (TILE, HDIM))
            probs[at : at + TILE] = weights.astype(jnp.bfloat16)
        summed[begin : begin + half] = jnp.dot(
            probs[begin : begin + half], latent[...], preferred_element_type=jnp.float32
        )


def absorb(biases, scores, peaks, sums):
    part = scores + biases
    peak = jnp.maximum(peaks, jnp.max(part, axis=-1, keepdims=True))
    weights = jnp.exp2(part - jnp.concatenate([peak] * (part.shape[1] // HDIM), axis=1))
    factor = jnp.exp2(peaks - peak)
    return weights.astype(jnp.bfloat16), factor, peak, sums * factor + jnp.sum(weights, axis=-1, keepdims=True)


def more_kernel(lengths, own, turned, value, peaks, sums, summed, *refs):
    blocks, (new_peaks, new_sums, outcome, latent, scores) = refs[:-5], refs[-5:]
    rows, some = own.shape[0] - 16, HEADS // 2
    for i, block in enumerate(blocks):
        latent[i * rows : (i + 1) * rows, :] = block[:rows]
    bias = bias_of(lengths, own, jnp.concatenate([position_of(block, rows) for block in blocks], axis=1))
    biases = jnp.concatenate([bias] * some, axis=0)
    score(turned, latent, scores)
    for first in range(0, HEADS, some):
        here = slice(first * rows, (first + some) * rows)
        probs, factor, new_peaks[here], new_sums[here] = absorb(biases, scores[here], peaks[here], sums[here])
        update = jnp.dot(probs, latent[...], preferred_element_type=jnp.float32)
        update = update + summed[here] * jnp.concatenate([factor] * (summed.shape[1] // HDIM), axis=1)
        update = update.astype(jnp.bfloat16)
        for i in range(some):
            head = first + i
            outcome[head * rows : (head + 1) * rows] = jnp.dot(
                update[i * rows : (i + 1) * rows],
                value[:, head * HDIM : (head + 1) * HDIM],
                preferred_element_type=jnp.float32,
            )


def attend_kernel(lengths, own, turned, value, peaks, sums, before, last, out, scores):
    rows = out.shape[0]
    latent = last[:rows]
    bias = bias_of(lengths, own, position_of(last, rows))
    score(turned, latent, scores)
    values = jnp.dot(latent, value[...], preferred_element_type=jnp.float32).astype(jnp.bfloat16)
    some = HEADS // 2
    biases = jnp.concatenate([bias] * some, axis=0)
    for first in range(0, HEADS, some):
        here = slice(first * rows, (first + some) * rows)
        probs, factor, _, total = absorb(biases, scores[here], peaks[here], sums[here])
        kept = before[here] * factor
        for i in range(some):
            columns = slice((first + i) * HDIM, (first + i + 1) * HDIM)
            mine = slice(i * rows, (i + 1) * rows)
            outcome = kept[mine] + jnp.dot(probs[mine], values[:, columns], preferred_element_type=jnp.float32)
            out[:, columns] = (outcome / total[mine]).astype(jnp.bfloat16)


def body(arrivals, slots, lengths, w_joined, w_expand):
    count, size = lax.axis_size("mp"), lax.axis_size("group")
    rows, depth = arrivals.shape
    columns, rank = w_joined.shape[1], w_expand.shape[0] * count

    weights = w_joined.astype(jnp.bfloat16)
    blocks = ring_gather(weights, count)
    w_expand, _ = lax.optimization_barrier((w_expand, weights))
    own_expand = lax.all_gather(w_expand.astype(jnp.bfloat16), "mp", axis=0, tiled=True)
    arrivals, _ = lax.optimization_barrier((arrivals, weights))
    normed, digits = pl.pallas_call(
        norm_kernel,
        out_shape=[
            jax.ShapeDtypeStruct((rows, depth), jnp.bfloat16),
            jax.ShapeDtypeStruct((16, rank), jnp.bfloat16),
        ],
        in_specs=[VMEM, VMEM],
        out_specs=[VMEM, VMEM],
        compiler_params=grant(16),
        cost_estimate=pl.CostEstimate(flops=NORM_COST * rows * depth, bytes_accessed=NORM_COST * rows * depth, transcendentals=rows),
        name="norm",
    )(arrivals, slots.reshape(1, rows))
    tokens = group_gather(normed, size, blocks[-4:-2])
    early = 0 if w_joined.shape[0] // 2 % 128 else count - 3
    total = []
    if early:
        total = [
            pl.pallas_call(
                functools.partial(early_kernel, count, size),
                out_shape=jax.ShapeDtypeStruct((size * rows, columns), jnp.float32),
                in_specs=[VMEM] * (size + early),
                out_specs=VMEM,
                compiler_params=grant(16),
                cost_estimate=pl.CostEstimate(
                    flops=2 * size * rows * depth * columns, bytes_accessed=4 * depth * columns, transcendentals=0
                ),
                name="project_early",
            )(*tokens, *blocks[:early])
        ]
    projs = pl.pallas_call(
        functools.partial(proj_kernel, count, size, early),
        out_shape=[jax.ShapeDtypeStruct((rows, columns), jnp.bfloat16)] * size,
        in_specs=[VMEM] * (size + count + 1 + len(total)),
        out_specs=[VMEM] * size,
        scratch_shapes=[] if early else [pltpu.VMEM((depth, columns), jnp.bfloat16)],
        compiler_params=grant(16),
        cost_estimate=pl.CostEstimate(
            flops=2 * size * rows * depth * columns, bytes_accessed=4 * depth * columns, transcendentals=0
        ),
        name="project",
    )(*tokens, *blocks, *total)

    back = [projs[0]]
    for k in range(1, size):
        back.append(lax.ppermute(projs[k], "group", [(i, i ^ k) for i in range(size)]))
    own_expand, _ = lax.optimization_barrier((own_expand, back[1:]))
    query, block = pl.pallas_call(
        functools.partial(assemble_kernel, size),
        out_shape=[
            jax.ShapeDtypeStruct((rows, QCOLS), jnp.bfloat16),
            jax.ShapeDtypeStruct((rows + 16, rank), jnp.bfloat16),
        ],
        in_specs=[VMEM] * (size + 1),
        out_specs=[VMEM, VMEM],
        scratch_shapes=[pltpu.VMEM((size, rows, columns), jnp.bfloat16)],
        compiler_params=grant(16),
        name="assemble",
    )(digits, *back)
    total, early = count * rows, count - 3
    needed = grant(8 + total * HEADS * rows * 8 // (1024 * 1024))
    state = [jax.ShapeDtypeStruct((HEADS * rows, width), jnp.float32) for width in (HDIM, HDIM, rank)]

    def cost(blocks):
        return pl.CostEstimate(
            flops=4 * blocks * rows * rank * QCOLS,
            bytes_accessed=8 * QCOLS * rank,
            transcendentals=HEADS * rows * blocks * rows,
        )

    def attend_start(blocks):
        expands = group_gather(own_expand, size, blocks[3:5])
        return pl.pallas_call(
            functools.partial(start_kernel, count, size),
            out_shape=[
                jax.ShapeDtypeStruct((HEADS * rows, rank), jnp.bfloat16),
                jax.ShapeDtypeStruct((rank, QCOLS), jnp.bfloat16),
                *state,
            ],
            in_specs=[SMEM] + [VMEM] * (1 + early + size),
            out_specs=[VMEM] * 5,
            scratch_shapes=[
                pltpu.VMEM((early * rows, rank), jnp.bfloat16),
                pltpu.VMEM((rank, 2 * QCOLS), jnp.bfloat16),
                pltpu.VMEM((HEADS * rows, early * rows), jnp.float32),
                pltpu.VMEM((HEADS * rows, early * rows), jnp.bfloat16),
            ],
            compiler_params=needed,
            cost_estimate=cost(early),
            name="attend_start",
        )(lengths, query, *blocks[:early], *expands)

    lat_blocks, (turned, value, *running) = split_ring_gather(block, count, size, attend_start)
    running = pl.pallas_call(
        more_kernel,
        out_shape=[jax.ShapeDtypeStruct((HEADS * rows, HDIM), jnp.float32)] * 3,
        in_specs=[SMEM] + [VMEM] * 8,
        out_specs=[VMEM] * 3,
        scratch_shapes=[
            pltpu.VMEM((2 * rows, rank), jnp.bfloat16),
            pltpu.VMEM((HEADS * rows, 2 * rows), jnp.float32),
        ],
        compiler_params=grant(16),
        cost_estimate=cost(2),
        name="attend_more",
    )(lengths, block, turned, value, *running, *lat_blocks[early : count - 1])
    return pl.pallas_call(
        attend_kernel,
        out_shape=jax.ShapeDtypeStruct((rows, QCOLS), jnp.bfloat16),
        in_specs=[SMEM] + [VMEM] * 7,
        out_specs=VMEM,
        scratch_shapes=[pltpu.VMEM((HEADS * rows, rows), jnp.float32)],
        compiler_params=grant(16),
        cost_estimate=cost(2),
        name="attend",
    )(lengths, block, turned, value, *running, lat_blocks[-1])


def solution(mesh):
    in_specs = (
        P(("group", "mp"), None),
        P(("group", "mp")),
        P("group", None),
        P("mp", "group"),
        P("mp", "group"),
    )
    out_specs = P(("group", "mp"), None)
    return jax.shard_map(body, mesh=mesh, in_specs=in_specs, out_specs=out_specs, check_vma=False)
```

```python
import functools

import jax
import jax.numpy as jnp
from jax import lax
from jax.experimental import pallas as pl
from jax.experimental.pallas import tpu as pltpu
from jax.sharding import PartitionSpec as P

HEADS = 8
HDIM = 128
QCOLS = HEADS * HDIM

EPS = 1e-06
NEGATIVE = -1e30
LOG2_E = 1.4426950408889634
TILE = 16
NORM_COST = 64
VMEM = pl.BlockSpec(memory_space=pltpu.VMEM)
SMEM = pl.BlockSpec(memory_space=pltpu.SMEM)


def grant(mib):
    return pltpu.CompilerParams(vmem_limit_bytes=mib * 1024 * 1024)


def row_norm(values):
    mean_sq = jnp.mean(values * values, axis=-1, keepdims=True)
    return values * lax.rsqrt(mean_sq + EPS)


def ring_pairs(count, step):
    order = [2 * r if r < count // 2 else 2 * (count - 1 - r) + 1 for r in range(count)]
    return [(order[r], order[(r + step) % count]) for r in range(count)]


def ring_gather(block, count):
    up, down = ring_pairs(count, 1), ring_pairs(count, -1)
    below = above = block
    blocks = [block]
    for _ in range((count - 1) // 2):
        below, above = lax.ppermute(below, "mp", up), lax.ppermute(above, "mp", down)
        blocks += [below, above]
    cut = -(-block.shape[0] // 32) * 16
    return blocks + [lax.ppermute(below[:cut], "mp", up), lax.ppermute(above[cut:], "mp", down)]


def split_ring_gather(block, count, size, beside):
    up, down = ring_pairs(count, 1), ring_pairs(count, -1)
    below = above = block
    blocks = [block]
    for _ in range((count - 1) // 2):
        below, above = lax.ppermute(below, "mp", up), lax.ppermute(above, "mp", down)
        blocks += [below, above]
    made = beside(blocks)
    below, above, made = lax.optimization_barrier((below, above, made))
    last = jnp.where(lax.axis_index("group") % 2 == 0, below, above)
    pairs = [
        (group * count + source, group * count + target)
        for group in range(size)
        for source, target in (down if group % 2 else up)
    ]
    return blocks + [lax.ppermute(last, ("group", "mp"), pairs)], made


def ring_owners(count):
    me = lax.axis_index("mp")
    place = jnp.where(me % 2 == 0, me // 2, count - 1 - me // 2)
    owners = [me]
    for step in range(1, count // 2 + 1):
        for shift in (-step, step):
            at = lax.rem(place + shift + count, count)
            owners.append(jnp.where(at < count // 2, 2 * at, 2 * (count - 1 - at) + 1))
    return owners[:count]


def row_ranges(blocks):
    last = len(blocks) - 2
    return [(i, 0) for i in range(last + 1)] + [(last, blocks[last].shape[0])]


def group_gather(block, size, after=None):
    blocks = {0: block}
    bit = size // 2
    while bit:
        pairs = [(i, i ^ bit) for i in range(size)]
        for k in list(blocks):
            sent = blocks[k]
            if k and after is not None:
                sent, _ = lax.optimization_barrier((sent, after))
            blocks[k ^ bit] = lax.ppermute(sent, "group", pairs)
        bit //= 2
    return [blocks[k] for k in range(size)]


def pack_kernel(joined, expand, out):
    columns, high = joined.shape[1], expand.shape[0]
    folds = joined.shape[0] // high
    fold = expand.shape[1] // folds
    out[:, :columns] = joined[...].astype(jnp.bfloat16)
    for i in range(folds):
        out[i * high : (i + 1) * high, columns:] = expand[:, i * fold : (i + 1) * fold].astype(jnp.bfloat16)


def norm_kernel(arrivals, slots, normed, digits):
    normed[...] = row_norm(arrivals[...].astype(jnp.float32)).astype(jnp.bfloat16)
    rows = slots.shape[1]
    bits = jnp.concatenate([slots[...] & 255, slots[...] >> 8], axis=0).astype(jnp.float32)
    bits = jnp.concatenate([bits, jnp.zeros((14, rows), jnp.float32)], axis=0)
    digits[...] = jnp.zeros_like(digits)
    digits[:, :rows] = bits.astype(jnp.bfloat16)


def multiply(tokens, starts, blocks, columns):
    total = None
    for start, block in zip(starts, blocks):
        span = pl.ds(pl.multiple_of(start, 128), block.shape[0])
        left = jnp.concatenate([token[:, span] for token in tokens], axis=0)
        product = jnp.dot(left, block[:, :columns], preferred_element_type=jnp.float32)
        total = product if total is None else total + product
    return total


def early_kernel(count, size, *refs):
    tokens, blocks, total = refs[:size], refs[size:-1], refs[-1]
    depth = blocks[0].shape[0]
    total[...] = multiply(tokens, [owner * depth for owner in ring_owners(count)], blocks, total.shape[1])


def proj_kernel(count, size, early, *refs):
    tokens, refs = refs[:size], refs[size:]
    blocks, refs = refs[: count + 1], refs[count + 1 :]
    depth = blocks[0].shape[0]
    owners = ring_owners(count)
    starts = [owners[i] * depth + offset for i, offset in row_ranges(blocks)]
    if early:
        total, refs = refs[0], refs[1:]
        outs, expand = refs[:size], refs[size]
        rows, columns = outs[0].shape
        proj = total[...] + multiply(tokens, starts[early:], blocks[early:], columns)
    else:
        outs, expand, weight = refs[:size], refs[size], refs[size + 1]
        rows, columns = outs[0].shape
        for start, block in zip(starts, blocks):
            length = block.shape[0]
            weight[pl.ds(pl.multiple_of(start, length), length), :] = block[:, :columns]
        products = [jnp.dot(token[...], weight[...], preferred_element_type=jnp.float32) for token in tokens]
        proj = jnp.concatenate(products, axis=0)
    at = lax.axis_index("group") * columns + lax.broadcasted_iota(jnp.int32, (1, columns), 1)
    proj = proj * jnp.where(at < QCOLS, HDIM**-0.5, 1.0).astype(jnp.float32)
    for i, out in enumerate(outs):
        out[...] = proj[i * rows : (i + 1) * rows].astype(jnp.bfloat16)
    high = expand.shape[0] // count
    for i, owner in enumerate(owners):
        parts = []
        for block in blocks[i:] if i == count - 1 else blocks[i : i + 1]:
            parts += [block[j * high : (j + 1) * high, columns:] for j in range(block.shape[0] // high)]
        expand[pl.ds(pl.multiple_of(owner * high, high), high), :] = jnp.concatenate(parts, axis=1)


def assemble_kernel(size, digits, *refs):
    products, (query, block, proj) = refs[:size], refs[size:]
    group = lax.axis_index("group")
    for i, product in enumerate(products):
        proj[group ^ i] = product[...]
    whole = jnp.concatenate([proj[i] for i in range(size)], axis=1)
    query[...] = whole[:, :QCOLS]
    rows = query.shape[0]
    block[:rows] = row_norm(whole[:, QCOLS:].astype(jnp.float32)).astype(jnp.bfloat16)
    block[rows:] = digits[...]


def position_of(block, rows):
    digits = block[block.shape[0] - 16 :, :rows].astype(jnp.float32)
    return digits[1:2] * 256.0 + digits[:1]


def bias_of(lengths, own, others):
    rows = own.shape[0] - 16
    same = lax.broadcasted_iota(jnp.int32, (rows, rows), 0) == lax.broadcasted_iota(jnp.int32, (rows, rows), 1)
    position = jnp.sum(jnp.where(same, position_of(own, rows), 0.0), axis=1, keepdims=True).astype(jnp.int32)
    start = jnp.zeros_like(position)
    end = 0
    for i in range(lengths.shape[1]):
        end = end + lengths[0, i]
        start = jnp.where(position >= end, end, start)
    others = others.astype(jnp.int32)
    return jnp.where((others <= position) & (others >= start), 0.0, NEGATIVE)


def score(turned, latent, scores):
    half = turned.shape[0] // 2
    for at in (0, half):
        scores[at : at + half] = lax.dot_general(
            turned[at : at + half], latent[...], (((1,), (1,)), ((), ())), preferred_element_type=jnp.float32
        )


def start_kernel(count, size, lengths, query, *refs):
    blocks, refs = refs[: count - 5], refs[count - 5 :]
    expands, refs = refs[:size], refs[size:]
    turned, value, peaks, sums, summed, latent, expand, scores, probs = refs
    rows = query.shape[0]
    for i, block in enumerate(blocks):
        latent[i * rows : (i + 1) * rows, :] = block[:rows]
    bias = bias_of(lengths, blocks[0], jnp.concatenate([position_of(block, rows) for block in blocks], axis=1))
    width = expands[0].shape[1]
    for i, block in enumerate(expands):
        at = (lax.axis_index("group") ^ i) * width
        expand[:, pl.ds(pl.multiple_of(at, width), width)] = block[...]
    for head in range(HEADS):
        value[:, head * HDIM : (head + 1) * HDIM] = expand[:, (2 * head + 1) * HDIM : (2 * head + 2) * HDIM]
        product = lax.dot_general(
            query[:, head * HDIM : (head + 1) * HDIM],
            expand[:, head * 2 * HDIM : (2 * head + 1) * HDIM],
            (((1,), (1,)), ((), ())),
            preferred_element_type=jnp.float32,
        )
        turned[head * rows : (head + 1) * rows] = (product * LOG2_E).astype(jnp.bfloat16)
    score(turned, latent, scores)
    half = HEADS * rows // 2
    for begin in (0, half):
        for at in range(begin, begin + half, TILE):
            here = at % rows
            part = scores[at : at + TILE] + bias[here : here + TILE]
            peak = jnp.max(part, axis=-1, keepdims=True)
            weights = jnp.exp2(part - peak)
            peaks[at : at + TILE] = jnp.broadcast_to(peak, (TILE, HDIM))
            sums[at : at + TILE] = jnp.broadcast_to(jnp.sum(weights, axis=-1, keepdims=True), (TILE, HDIM))
            probs[at : at + TILE] = weights.astype(jnp.bfloat16)
        summed[begin : begin + half] = jnp.dot(
            probs[begin : begin + half], latent[...], preferred_element_type=jnp.float32
        )


def absorb(biases, scores, peaks, sums):
    part = scores + biases
    peak = jnp.maximum(peaks, jnp.max(part, axis=-1, keepdims=True))
    weights = jnp.exp2(part - jnp.concatenate([peak] * (part.shape[1] // HDIM), axis=1))
    factor = jnp.exp2(peaks - peak)
    return weights.astype(jnp.bfloat16), factor, peak, sums * factor + jnp.sum(weights, axis=-1, keepdims=True)


def more_kernel(lengths, own, turned, value, peaks, sums, summed, *refs):
    blocks, (new_peaks, new_sums, outcome, latent, scores) = refs[:-5], refs[-5:]
    rows, some = own.shape[0] - 16, HEADS // 2
    for i, block in enumerate(blocks):
        latent[i * rows : (i + 1) * rows, :] = block[:rows]
    bias = bias_of(lengths, own, jnp.concatenate([position_of(block, rows) for block in blocks], axis=1))
    biases = jnp.concatenate([bias] * some, axis=0)
    score(turned, latent, scores)
    for first in range(0, HEADS, some):
        here = slice(first * rows, (first + some) * rows)
        probs, factor, new_peaks[here], new_sums[here] = absorb(biases, scores[here], peaks[here], sums[here])
        update = jnp.dot(probs, latent[...], preferred_element_type=jnp.float32)
        update = update + summed[here] * jnp.concatenate([factor] * (summed.shape[1] // HDIM), axis=1)
        update = update.astype(jnp.bfloat16)
        for i in range(some):
            head = first + i
            outcome[head * rows : (head + 1) * rows] = jnp.dot(
                update[i * rows : (i + 1) * rows],
                value[:, head * HDIM : (head + 1) * HDIM],
                preferred_element_type=jnp.float32,
            )


def attend_kernel(lengths, own, turned, value, peaks, sums, before, last, out, scores):
    rows = out.shape[0]
    latent = last[:rows]
    bias = bias_of(lengths, own, position_of(last, rows))
    score(turned, latent, scores)
    values = jnp.dot(latent, value[...], preferred_element_type=jnp.float32).astype(jnp.bfloat16)
    some = HEADS // 2
    biases = jnp.concatenate([bias] * some, axis=0)
    for first in range(0, HEADS, some):
        here = slice(first * rows, (first + some) * rows)
        probs, factor, _, total = absorb(biases, scores[here], peaks[here], sums[here])
        kept = before[here] * factor
        for i in range(some):
            columns = slice((first + i) * HDIM, (first + i + 1) * HDIM)
            mine = slice(i * rows, (i + 1) * rows)
            outcome = kept[mine] + jnp.dot(probs[mine], values[:, columns], preferred_element_type=jnp.float32)
            out[:, columns] = (outcome / total[mine]).astype(jnp.bfloat16)


def body(arrivals, slots, lengths, w_joined, w_expand):
    count, size = lax.axis_size("mp"), lax.axis_size("group")
    rows, depth = arrivals.shape
    columns, rank = w_joined.shape[1], w_expand.shape[0] * count
    own_columns = w_expand.shape[1]

    weights = pl.pallas_call(
        pack_kernel,
        out_shape=jax.ShapeDtypeStruct(
            (w_joined.shape[0], columns + own_columns * w_expand.shape[0] // w_joined.shape[0]), jnp.bfloat16
        ),
        in_specs=[VMEM, VMEM],
        out_specs=VMEM,
        compiler_params=grant(16),
        name="pack",
    )(w_joined, w_expand)
    blocks = ring_gather(weights, count)
    arrivals, _ = lax.optimization_barrier((arrivals, weights))
    normed, digits = pl.pallas_call(
        norm_kernel,
        out_shape=[
            jax.ShapeDtypeStruct((rows, depth), jnp.bfloat16),
            jax.ShapeDtypeStruct((16, rank), jnp.bfloat16),
        ],
        in_specs=[VMEM, VMEM],
        out_specs=[VMEM, VMEM],
        compiler_params=grant(16),
        cost_estimate=pl.CostEstimate(flops=NORM_COST * rows * depth, bytes_accessed=NORM_COST * rows * depth, transcendentals=rows),
        name="norm",
    )(arrivals, slots.reshape(1, rows))
    tokens = group_gather(normed, size, blocks[-4:-2])
    early = 0 if w_joined.shape[0] // 2 % 128 else count - 3
    total = []
    if early:
        total = [
            pl.pallas_call(
                functools.partial(early_kernel, count, size),
                out_shape=jax.ShapeDtypeStruct((size * rows, columns), jnp.float32),
                in_specs=[VMEM] * (size + early),
                out_specs=VMEM,
                compiler_params=grant(16),
                cost_estimate=pl.CostEstimate(
                    flops=2 * size * rows * depth * columns, bytes_accessed=4 * depth * columns, transcendentals=0
                ),
                name="project_early",
            )(*tokens, *blocks[:early])
        ]
    *projs, own_expand = pl.pallas_call(
        functools.partial(proj_kernel, count, size, early),
        out_shape=[jax.ShapeDtypeStruct((rows, columns), jnp.bfloat16)] * size
        + [jax.ShapeDtypeStruct((rank, own_columns), jnp.bfloat16)],
        in_specs=[VMEM] * (size + count + 1 + len(total)),
        out_specs=[VMEM] * (size + 1),
        scratch_shapes=[] if early else [pltpu.VMEM((depth, columns), jnp.bfloat16)],
        compiler_params=grant(16),
        cost_estimate=pl.CostEstimate(
            flops=2 * size * rows * depth * columns, bytes_accessed=4 * depth * columns, transcendentals=0
        ),
        name="project",
    )(*tokens, *blocks, *total)

    back = [projs[0]]
    for k in range(1, size):
        back.append(lax.ppermute(projs[k], "group", [(i, i ^ k) for i in range(size)]))
    own_expand, _ = lax.optimization_barrier((own_expand, back[1:]))
    query, block = pl.pallas_call(
        functools.partial(assemble_kernel, size),
        out_shape=[
            jax.ShapeDtypeStruct((rows, QCOLS), jnp.bfloat16),
            jax.ShapeDtypeStruct((rows + 16, rank), jnp.bfloat16),
        ],
        in_specs=[VMEM] * (size + 1),
        out_specs=[VMEM, VMEM],
        scratch_shapes=[pltpu.VMEM((size, rows, columns), jnp.bfloat16)],
        compiler_params=grant(16),
        name="assemble",
    )(digits, *back)
    total, early = count * rows, count - 5
    needed = grant(8 + total * HEADS * rows * 8 // (1024 * 1024))
    state = [jax.ShapeDtypeStruct((HEADS * rows, width), jnp.float32) for width in (HDIM, HDIM, rank)]

    def cost(blocks):
        return pl.CostEstimate(
            flops=4 * blocks * rows * rank * QCOLS,
            bytes_accessed=8 * QCOLS * rank,
            transcendentals=HEADS * rows * blocks * rows,
        )

    def attend_start(blocks):
        expands = group_gather(own_expand, size, blocks[3:5])
        return pl.pallas_call(
            functools.partial(start_kernel, count, size),
            out_shape=[
                jax.ShapeDtypeStruct((HEADS * rows, rank), jnp.bfloat16),
                jax.ShapeDtypeStruct((rank, QCOLS), jnp.bfloat16),
                *state,
            ],
            in_specs=[SMEM] + [VMEM] * (1 + early + size),
            out_specs=[VMEM] * 5,
            scratch_shapes=[
                pltpu.VMEM((early * rows, rank), jnp.bfloat16),
                pltpu.VMEM((rank, 2 * QCOLS), jnp.bfloat16),
                pltpu.VMEM((HEADS * rows, early * rows), jnp.float32),
                pltpu.VMEM((HEADS * rows, early * rows), jnp.bfloat16),
            ],
            compiler_params=needed,
            cost_estimate=cost(early),
            name="attend_start",
        )(lengths, query, *blocks[:early], *expands)

    lat_blocks, (turned, value, *running) = split_ring_gather(block, count, size, attend_start)
    running = pl.pallas_call(
        more_kernel,
        out_shape=[jax.ShapeDtypeStruct((HEADS * rows, HDIM), jnp.float32)] * 3,
        in_specs=[SMEM] + [VMEM] * 10,
        out_specs=[VMEM] * 3,
        scratch_shapes=[
            pltpu.VMEM((4 * rows, rank), jnp.bfloat16),
            pltpu.VMEM((HEADS * rows, 4 * rows), jnp.float32),
        ],
        compiler_params=grant(16),
        cost_estimate=cost(4),
        name="attend_more",
    )(lengths, block, turned, value, *running, *lat_blocks[early : count - 1])
    return pl.pallas_call(
        attend_kernel,
        out_shape=jax.ShapeDtypeStruct((rows, QCOLS), jnp.bfloat16),
        in_specs=[SMEM] + [VMEM] * 7,
        out_specs=VMEM,
        scratch_shapes=[pltpu.VMEM((HEADS * rows, rows), jnp.float32)],
        compiler_params=grant(16),
        cost_estimate=cost(2),
        name="attend",
    )(lengths, block, turned, value, *running, lat_blocks[-1])


def solution(mesh):
    in_specs = (
        P(("group", "mp"), None),
        P(("group", "mp")),
        P("group", None),
        P("mp", "group"),
        P("mp", "group"),
    )
    out_specs = P(("group", "mp"), None)
    return jax.shard_map(body, mesh=mesh, in_specs=in_specs, out_specs=out_specs, check_vma=False)
```

```python
import functools

import jax
import jax.numpy as jnp
from jax import lax
from jax.experimental import pallas as pl
from jax.experimental.pallas import tpu as pltpu
from jax.sharding import PartitionSpec as P

HEADS = 8
HDIM = 128
QCOLS = HEADS * HDIM

EPS = 1e-06
NEGATIVE = -1e30
LOG2_E = 1.4426950408889634
TILE = 16
NORM_COST = 64
VMEM = pl.BlockSpec(memory_space=pltpu.VMEM)
SMEM = pl.BlockSpec(memory_space=pltpu.SMEM)


def grant(mib):
    return pltpu.CompilerParams(vmem_limit_bytes=mib * 1024 * 1024)


def row_norm(values):
    mean_sq = jnp.mean(values * values, axis=-1, keepdims=True)
    return values * lax.rsqrt(mean_sq + EPS)


def ring_pairs(count, step):
    order = [2 * r if r < count // 2 else 2 * (count - 1 - r) + 1 for r in range(count)]
    return [(order[r], order[(r + step) % count]) for r in range(count)]


def ring_gather(block, count):
    up, down = ring_pairs(count, 1), ring_pairs(count, -1)
    below = above = block
    blocks = [block]
    for _ in range((count - 1) // 2):
        below, above = lax.ppermute(below, "mp", up), lax.ppermute(above, "mp", down)
        blocks += [below, above]
    cut = -(-block.shape[0] // 32) * 16
    return blocks + [lax.ppermute(below[:cut], "mp", up), lax.ppermute(above[cut:], "mp", down)]


def split_ring_gather(block, count, size, beside):
    up, down = ring_pairs(count, 1), ring_pairs(count, -1)
    below = above = block
    blocks = [block]
    for _ in range((count - 1) // 2):
        below, above = lax.ppermute(below, "mp", up), lax.ppermute(above, "mp", down)
        blocks += [below, above]
    made = beside(blocks)
    below, above, made = lax.optimization_barrier((below, above, made))
    last = jnp.where(lax.axis_index("group") % 2 == 0, below, above)
    pairs = [
        (group * count + source, group * count + target)
        for group in range(size)
        for source, target in (down if group % 2 else up)
    ]
    return blocks + [lax.ppermute(last, ("group", "mp"), pairs)], made


def ring_owners(count):
    me = lax.axis_index("mp")
    place = jnp.where(me % 2 == 0, me // 2, count - 1 - me // 2)
    owners = [me]
    for step in range(1, count // 2 + 1):
        for shift in (-step, step):
            at = lax.rem(place + shift + count, count)
            owners.append(jnp.where(at < count // 2, 2 * at, 2 * (count - 1 - at) + 1))
    return owners[:count]


def row_ranges(blocks):
    last = len(blocks) - 2
    return [(i, 0) for i in range(last + 1)] + [(last, blocks[last].shape[0])]


def group_gather(block, size, after=None):
    blocks = {0: block}
    bit = size // 2
    while bit:
        pairs = [(i, i ^ bit) for i in range(size)]
        for k in list(blocks):
            sent = blocks[k]
            if k and after is not None:
                sent, _ = lax.optimization_barrier((sent, after))
            blocks[k ^ bit] = lax.ppermute(sent, "group", pairs)
        bit //= 2
    return [blocks[k] for k in range(size)]


def pack_kernel(joined, expand, out):
    columns, high = joined.shape[1], expand.shape[0]
    folds = joined.shape[0] // high
    fold = expand.shape[1] // folds
    out[:, :columns] = joined[...].astype(jnp.bfloat16)
    for i in range(folds):
        out[i * high : (i + 1) * high, columns:] = expand[:, i * fold : (i + 1) * fold].astype(jnp.bfloat16)


def norm_kernel(arrivals, slots, normed, digits):
    normed[...] = row_norm(arrivals[...].astype(jnp.float32)).astype(jnp.bfloat16)
    rows = slots.shape[1]
    bits = jnp.concatenate([slots[...] & 255, slots[...] >> 8], axis=0).astype(jnp.float32)
    bits = jnp.concatenate([bits, jnp.zeros((14, rows), jnp.float32)], axis=0)
    digits[...] = jnp.zeros_like(digits)
    digits[:, :rows] = bits.astype(jnp.bfloat16)


def multiply(tokens, starts, blocks, columns):
    total = None
    for start, block in zip(starts, blocks):
        span = pl.ds(pl.multiple_of(start, 128), block.shape[0])
        left = jnp.concatenate([token[:, span] for token in tokens], axis=0)
        product = jnp.dot(left, block[:, :columns], preferred_element_type=jnp.float32)
        total = product if total is None else total + product
    return total


def early_kernel(count, size, *refs):
    tokens, blocks, total = refs[:size], refs[size:-1], refs[-1]
    depth = blocks[0].shape[0]
    total[...] = multiply(tokens, [owner * depth for owner in ring_owners(count)], blocks, total.shape[1])


def proj_kernel(count, size, early, *refs):
    tokens, refs = refs[:size], refs[size:]
    blocks, refs = refs[: count + 1], refs[count + 1 :]
    depth = blocks[0].shape[0]
    owners = ring_owners(count)
    starts = [owners[i] * depth + offset for i, offset in row_ranges(blocks)]
    if early:
        total, refs = refs[0], refs[1:]
        outs, expand = refs[:size], refs[size]
        rows, columns = outs[0].shape
        proj = total[...] + multiply(tokens, starts[early:], blocks[early:], columns)
    else:
        outs, expand, weight = refs[:size], refs[size], refs[size + 1]
        rows, columns = outs[0].shape
        for start, block in zip(starts, blocks):
            length = block.shape[0]
            weight[pl.ds(pl.multiple_of(start, length), length), :] = block[:, :columns]
        products = [jnp.dot(token[...], weight[...], preferred_element_type=jnp.float32) for token in tokens]
        proj = jnp.concatenate(products, axis=0)
    at = lax.axis_index("group") * columns + lax.broadcasted_iota(jnp.int32, (1, columns), 1)
    proj = proj * jnp.where(at < QCOLS, HDIM**-0.5, 1.0).astype(jnp.float32)
    for i, out in enumerate(outs):
        out[...] = proj[i * rows : (i + 1) * rows].astype(jnp.bfloat16)
    high = expand.shape[0] // count
    for i, owner in enumerate(owners):
        parts = []
        for block in blocks[i:] if i == count - 1 else blocks[i : i + 1]:
            parts += [block[j * high : (j + 1) * high, columns:] for j in range(block.shape[0] // high)]
        expand[pl.ds(pl.multiple_of(owner * high, high), high), :] = jnp.concatenate(parts, axis=1)


def assemble_kernel(size, digits, *refs):
    products, (query, block, proj) = refs[:size], refs[size:]
    group = lax.axis_index("group")
    for i, product in enumerate(products):
        proj[group ^ i] = product[...]
    whole = jnp.concatenate([proj[i] for i in range(size)], axis=1)
    query[...] = whole[:, :QCOLS]
    rows = query.shape[0]
    block[:rows] = row_norm(whole[:, QCOLS:].astype(jnp.float32)).astype(jnp.bfloat16)
    block[rows:] = digits[...]


def position_of(block, rows):
    digits = block[block.shape[0] - 16 :, :rows].astype(jnp.float32)
    return digits[1:2] * 256.0 + digits[:1]


def bias_of(lengths, own, others):
    rows = own.shape[0] - 16
    same = lax.broadcasted_iota(jnp.int32, (rows, rows), 0) == lax.broadcasted_iota(jnp.int32, (rows, rows), 1)
    position = jnp.sum(jnp.where(same, position_of(own, rows), 0.0), axis=1, keepdims=True).astype(jnp.int32)
    start = jnp.zeros_like(position)
    end = 0
    for i in range(lengths.shape[1]):
        end = end + lengths[0, i]
        start = jnp.where(position >= end, end, start)
    others = others.astype(jnp.int32)
    return jnp.where((others <= position) & (others >= start), 0.0, NEGATIVE)


def score(turned, latent, scores):
    half = turned.shape[0] // 2
    for at in (0, half):
        scores[at : at + half] = lax.dot_general(
            turned[at : at + half], latent[...], (((1,), (1,)), ((), ())), preferred_element_type=jnp.float32
        )


def start_kernel(count, size, lengths, query, *refs):
    blocks, refs = refs[: count - 3], refs[count - 3 :]
    expands, refs = refs[:size], refs[size:]
    turned, value, peaks, sums, summed, latent, expand, scores, probs = refs
    rows = query.shape[0]
    for i, block in enumerate(blocks):
        latent[i * rows : (i + 1) * rows, :] = block[:rows]
    bias = bias_of(lengths, blocks[0], jnp.concatenate([position_of(block, rows) for block in blocks], axis=1))
    width = expands[0].shape[1]
    for i, block in enumerate(expands):
        at = (lax.axis_index("group") ^ i) * width
        expand[:, pl.ds(pl.multiple_of(at, width), width)] = block[...]
    for head in range(HEADS):
        value[:, head * HDIM : (head + 1) * HDIM] = expand[:, (2 * head + 1) * HDIM : (2 * head + 2) * HDIM]
        product = lax.dot_general(
            query[:, head * HDIM : (head + 1) * HDIM],
            expand[:, head * 2 * HDIM : (2 * head + 1) * HDIM],
            (((1,), (1,)), ((), ())),
            preferred_element_type=jnp.float32,
        )
        turned[head * rows : (head + 1) * rows] = (product * LOG2_E).astype(jnp.bfloat16)
    score(turned, latent, scores)
    half = HEADS * rows // 2
    for begin in (0, half):
        for at in range(begin, begin + half, TILE):
            here = at % rows
            part = scores[at : at + TILE] + bias[here : here + TILE]
            peak = jnp.max(part, axis=-1, keepdims=True)
            weights = jnp.exp2(part - peak)
            peaks[at : at + TILE] = jnp.broadcast_to(peak, (TILE, HDIM))
            sums[at : at + TILE] = jnp.broadcast_to(jnp.sum(weights, axis=-1, keepdims=True), (TILE, HDIM))
            probs[at : at + TILE] = weights.astype(jnp.bfloat16)
        summed[begin : begin + half] = jnp.dot(
            probs[begin : begin + half], latent[...], preferred_element_type=jnp.float32
        )


def absorb(biases, scores, peaks, sums):
    part = scores + biases
    peak = jnp.maximum(peaks, jnp.max(part, axis=-1, keepdims=True))
    weights = jnp.exp2(part - jnp.concatenate([peak] * (part.shape[1] // HDIM), axis=1))
    factor = jnp.exp2(peaks - peak)
    return weights.astype(jnp.bfloat16), factor, peak, sums * factor + jnp.sum(weights, axis=-1, keepdims=True)


def more_kernel(lengths, own, turned, value, peaks, sums, summed, *refs):
    blocks, (new_peaks, new_sums, outcome, latent, scores) = refs[:-5], refs[-5:]
    rows, some = own.shape[0] - 16, HEADS // 2
    for i, block in enumerate(blocks):
        latent[i * rows : (i + 1) * rows, :] = block[:rows]
    bias = bias_of(lengths, own, jnp.concatenate([position_of(block, rows) for block in blocks], axis=1))
    biases = jnp.concatenate([bias] * some, axis=0)
    score(turned, latent, scores)
    for first in range(0, HEADS, some):
        here = slice(first * rows, (first + some) * rows)
        probs, factor, new_peaks[here], new_sums[here] = absorb(biases, scores[here], peaks[here], sums[here])
        update = jnp.dot(probs, latent[...], preferred_element_type=jnp.float32)
        update = update + summed[here] * jnp.concatenate([factor] * (summed.shape[1] // HDIM), axis=1)
        update = update.astype(jnp.bfloat16)
        for i in range(some):
            head = first + i
            outcome[head * rows : (head + 1) * rows] = jnp.dot(
                update[i * rows : (i + 1) * rows],
                value[:, head * HDIM : (head + 1) * HDIM],
                preferred_element_type=jnp.float32,
            )


def attend_kernel(lengths, own, turned, value, peaks, sums, before, last, out, scores):
    rows = out.shape[0]
    latent = last[:rows]
    bias = bias_of(lengths, own, position_of(last, rows))
    score(turned, latent, scores)
    values = jnp.dot(latent, value[...], preferred_element_type=jnp.float32).astype(jnp.bfloat16)
    some = HEADS // 2
    biases = jnp.concatenate([bias] * some, axis=0)
    for first in range(0, HEADS, some):
        here = slice(first * rows, (first + some) * rows)
        probs, factor, _, total = absorb(biases, scores[here], peaks[here], sums[here])
        kept = before[here] * factor
        for i in range(some):
            columns = slice((first + i) * HDIM, (first + i + 1) * HDIM)
            mine = slice(i * rows, (i + 1) * rows)
            outcome = kept[mine] + jnp.dot(probs[mine], values[:, columns], preferred_element_type=jnp.float32)
            out[:, columns] = (outcome / total[mine]).astype(jnp.bfloat16)


def body(arrivals, slots, lengths, w_joined, w_expand):
    count, size = lax.axis_size("mp"), lax.axis_size("group")
    rows, depth = arrivals.shape
    columns, rank = w_joined.shape[1], w_expand.shape[0] * count
    own_columns = w_expand.shape[1]

    weights = pl.pallas_call(
        pack_kernel,
        out_shape=jax.ShapeDtypeStruct(
            (w_joined.shape[0], columns + own_columns * w_expand.shape[0] // w_joined.shape[0]), jnp.bfloat16
        ),
        in_specs=[VMEM, VMEM],
        out_specs=VMEM,
        compiler_params=grant(16),
        name="pack",
    )(w_joined, w_expand)
    blocks = ring_gather(weights, count)
    arrivals, _ = lax.optimization_barrier((arrivals, weights))
    normed, digits = pl.pallas_call(
        norm_kernel,
        out_shape=[
            jax.ShapeDtypeStruct((rows, depth), jnp.bfloat16),
            jax.ShapeDtypeStruct((16, rank), jnp.bfloat16),
        ],
        in_specs=[VMEM, VMEM],
        out_specs=[VMEM, VMEM],
        compiler_params=grant(16),
        cost_estimate=pl.CostEstimate(flops=NORM_COST * rows * depth, bytes_accessed=NORM_COST * rows * depth, transcendentals=rows),
        name="norm",
    )(arrivals, slots.reshape(1, rows))
    tokens = group_gather(normed, size, blocks[-4:-2])
    early = 0 if w_joined.shape[0] // 2 % 128 else count - 1
    total = []
    if early:
        total = [
            pl.pallas_call(
                functools.partial(early_kernel, count, size),
                out_shape=jax.ShapeDtypeStruct((size * rows, columns), jnp.float32),
                in_specs=[VMEM] * (size + early),
                out_specs=VMEM,
                compiler_params=grant(16),
                cost_estimate=pl.CostEstimate(
                    flops=2 * size * rows * depth * columns, bytes_accessed=4 * depth * columns, transcendentals=0
                ),
                name="project_early",
            )(*tokens, *blocks[:early])
        ]
    *projs, own_expand = pl.pallas_call(
        functools.partial(proj_kernel, count, size, early),
        out_shape=[jax.ShapeDtypeStruct((rows, columns), jnp.bfloat16)] * size
        + [jax.ShapeDtypeStruct((rank, own_columns), jnp.bfloat16)],
        in_specs=[VMEM] * (size + count + 1 + len(total)),
        out_specs=[VMEM] * (size + 1),
        scratch_shapes=[] if early else [pltpu.VMEM((depth, columns), jnp.bfloat16)],
        compiler_params=grant(16),
        cost_estimate=pl.CostEstimate(
            flops=2 * size * rows * depth * columns, bytes_accessed=4 * depth * columns, transcendentals=0
        ),
        name="project",
    )(*tokens, *blocks, *total)

    back = [projs[0]]
    for k in range(1, size):
        back.append(lax.ppermute(projs[k], "group", [(i, i ^ k) for i in range(size)]))
    own_expand, _ = lax.optimization_barrier((own_expand, back[1:]))
    query, block = pl.pallas_call(
        functools.partial(assemble_kernel, size),
        out_shape=[
            jax.ShapeDtypeStruct((rows, QCOLS), jnp.bfloat16),
            jax.ShapeDtypeStruct((rows + 16, rank), jnp.bfloat16),
        ],
        in_specs=[VMEM] * (size + 1),
        out_specs=[VMEM, VMEM],
        scratch_shapes=[pltpu.VMEM((size, rows, columns), jnp.bfloat16)],
        compiler_params=grant(16),
        name="assemble",
    )(digits, *back)
    total, early = count * rows, count - 3
    needed = grant(8 + total * HEADS * rows * 8 // (1024 * 1024))
    state = [jax.ShapeDtypeStruct((HEADS * rows, width), jnp.float32) for width in (HDIM, HDIM, rank)]

    def cost(blocks):
        return pl.CostEstimate(
            flops=4 * blocks * rows * rank * QCOLS,
            bytes_accessed=8 * QCOLS * rank,
            transcendentals=HEADS * rows * blocks * rows,
        )

    def attend_start(blocks):
        expands = group_gather(own_expand, size, blocks[3:5])
        return pl.pallas_call(
            functools.partial(start_kernel, count, size),
            out_shape=[
                jax.ShapeDtypeStruct((HEADS * rows, rank), jnp.bfloat16),
                jax.ShapeDtypeStruct((rank, QCOLS), jnp.bfloat16),
                *state,
            ],
            in_specs=[SMEM] + [VMEM] * (1 + early + size),
            out_specs=[VMEM] * 5,
            scratch_shapes=[
                pltpu.VMEM((early * rows, rank), jnp.bfloat16),
                pltpu.VMEM((rank, 2 * QCOLS), jnp.bfloat16),
                pltpu.VMEM((HEADS * rows, early * rows), jnp.float32),
                pltpu.VMEM((HEADS * rows, early * rows), jnp.bfloat16),
            ],
            compiler_params=needed,
            cost_estimate=cost(early),
            name="attend_start",
        )(lengths, query, *blocks[:early], *expands)

    lat_blocks, (turned, value, *running) = split_ring_gather(block, count, size, attend_start)
    running = pl.pallas_call(
        more_kernel,
        out_shape=[jax.ShapeDtypeStruct((HEADS * rows, HDIM), jnp.float32)] * 3,
        in_specs=[SMEM] + [VMEM] * 8,
        out_specs=[VMEM] * 3,
        scratch_shapes=[
            pltpu.VMEM((2 * rows, rank), jnp.bfloat16),
            pltpu.VMEM((HEADS * rows, 2 * rows), jnp.float32),
        ],
        compiler_params=grant(16),
        cost_estimate=cost(2),
        name="attend_more",
    )(lengths, block, turned, value, *running, *lat_blocks[early : count - 1])
    return pl.pallas_call(
        attend_kernel,
        out_shape=jax.ShapeDtypeStruct((rows, QCOLS), jnp.bfloat16),
        in_specs=[SMEM] + [VMEM] * 7,
        out_specs=VMEM,
        scratch_shapes=[pltpu.VMEM((HEADS * rows, rows), jnp.float32)],
        compiler_params=grant(16),
        cost_estimate=cost(2),
        name="attend",
    )(lengths, block, turned, value, *running, lat_blocks[-1])


def solution(mesh):
    in_specs = (
        P(("group", "mp"), None),
        P(("group", "mp")),
        P("group", None),
        P("mp", "group"),
        P("mp", "group"),
    )
    out_specs = P(("group", "mp"), None)
    return jax.shard_map(body, mesh=mesh, in_specs=in_specs, out_specs=out_specs, check_vma=False)
```
